128 devices in a mesh: old: 8 (over z, core), new: 16 (over y, x).
Axes of the slice: x: 4, y: 4, z: 4, core: 2. Of those that a mesh axis runs over, the one named last changes fastest.
Arguments:
- old_values: float32 [32, 1048576], P(None, ('old', 'new')), may hold values from -6 to 6
- pair_rows: int32 [128, 128, 128], P(('old', 'new')), may hold values from 0 to 8191
- pair_targets: int32 [128, 128, 128], P(('old', 'new')), may hold values from 0 to 65535
- pair_weights: float32 [128, 128, 128], P(('old', 'new')), may hold values from 0.1 to 1
- pair_counts: int32 [128, 128], P(('old', 'new')), may hold values from 0 to 128, as said below
- cell_area: float32 [2, 512, 8192], P(None, 'new', 'old'), may hold values from 0.5 to 2
- thickness: float32 [2, 512, 8192], P(None, 'new', 'old'), may hold values from 0.5 to 2
- displacement: float32 [3, 512, 8192], P(None, 'new', 'old'), may hold values from -0.05 to 0.05
- velocity: float32 [3, 512, 8192], P(None, 'new', 'old'), may hold values from -3 to 3
Outputs:
- projected: float32 [32, 512, 8192], P(None, 'new', 'old')
- velocity_next: float32 [3, 512, 8192], P(None, 'new', 'old')
The draws below stay inside these ranges and needn't reach their ends.
Inputs may be any that keep to these rules, and one draw needn't show every extreme that they name: `pair_counts`: at most 128 live slots for every pair; some owner receives 128 from every source, and every source sends 128 to some owner. `pair_targets`: triangle id local to the owner; ids of cells outside the sheet may occur and take nothing.
All inputs are finite; a program needn't handle non-finite values.
Results may differ from the reference program's by a relative error of at most 0.000023.
Values sent between devices are 32-bit elements; how exact they have to be, the bound alone decides.
A program may use at most 128 MiB of HBM per device.

```python
import math
import jax
import jax.numpy as jnp
from jax import lax

RD = 32
CD = 1024
QD = 8192
CAP = 128
POINTS = 4
COMP = 8
ITERS = 3
CH = 32
RANKS = 128
NR = 512
NC = 8192
ELEMS = 65536
QUADS = 1048576
N_OLD = 8
N_NEW = 16


def draw_pair_counts(key, part):
    key = jax.random.fold_in(key, 7)
    key_factor, key_count, key_owner, key_each = jax.random.split(key, 4)
    factor = 2 ** jax.random.randint(key_factor, (RANKS,), 0, 3)
    upper_bound = jnp.minimum(CAP + 1, CAP // 3 * factor + 1)
    counts = jax.random.randint(key_count, (RANKS, RANKS), 0, upper_bound[None, :])
    busiest = jax.random.randint(key_owner, (), 0, RANKS)
    each_full = jax.random.randint(key_each, (RANKS,), 0, RANKS)
    columns = jnp.arange(RANKS, dtype=jnp.int32)[None, :]
    full_slot = (columns == busiest) | (columns == each_full[:, None])
    return jnp.where(full_slot, CAP, counts).astype(jnp.int32)


def plant(result, own_key, least, top_value):
    shape = result.shape
    place = [jax.random.randint(jax.random.fold_in(own_key, axis), (), 0, shape[axis]) for axis in range(len(shape))]
    result = result.at[tuple(place)].set(least)
    longest = shape.index(max(shape))
    place[longest] = (place[longest] + 1) % shape[longest]
    return result.at[tuple(place)].set(top_value)


def block_scale(key, dims, pieces, low, largest):
    factor_of, own = 1.0, jax.random.fold_in(key, 6)
    for axis_at, parts in pieces:
        draws = jnp.exp(jax.random.uniform(jax.random.fold_in(own, axis_at), (parts,), jnp.float32, low / len(pieces), largest / len(pieces)))
        factor_of = factor_of * jnp.repeat(draws, dims[axis_at] // parts).reshape([-1 if axis == axis_at else 1 for axis in range(len(dims))])
    return factor_of


def bell_draw(stream_key, dims, scale, most, pieces=(), kind=jnp.bfloat16):
    result = jax.random.normal(stream_key, dims, jnp.float32) * scale
    if len(pieces) > 0:
        result = block_scale(stream_key, dims, pieces, -0.22, 0.18) * result
    return jnp.clip(result, min=-most, max=most).astype(kind)


def setup_inputs(seed: int = 0) -> dict:
    key_of = jax.random.split(jax.random.key(seed), 10)
    return {
        "old_values": bell_draw(key_of[0], (CH, QUADS), 1.0, 6.0, ((1, 128),), jnp.float32),
        "pair_rows": plant(jax.random.randint(key_of[1], (RANKS, RANKS, CAP), 0, QD), jax.random.fold_in(key_of[1], 1), 0, QD - 1).astype(jnp.int32),
        "pair_targets": plant(jax.random.randint(key_of[2], (RANKS, RANKS, CAP), 0, ELEMS), jax.random.fold_in(key_of[2], 1), 0, ELEMS - 1).astype(jnp.int32),
        "pair_weights": jnp.clip(0.1 + 0.9 * jax.random.uniform(key_of[3], (RANKS, RANKS, CAP), jnp.float32) ** block_scale(key_of[3], (RANKS, RANKS, CAP), ((0, 128),), -0.2, 0.2), 0.1, 1.0),
        "pair_counts": draw_pair_counts(jax.random.fold_in(key_of[9], 71), 0),
        "cell_area": jnp.clip(jnp.exp(math.log(2.0) - 1.3862944 * jax.random.uniform(key_of[5], (2, NR, NC), jnp.float32) ** block_scale(key_of[5], (2, NR, NC), ((1, 16), (2, 8)), -0.2, 0.2)), 0.5, 2.0),
        "thickness": jnp.clip(jnp.exp(math.log(2.0) - 1.3862944 * jax.random.uniform(key_of[6], (2, NR, NC), jnp.float32) ** block_scale(key_of[6], (2, NR, NC), ((1, 16), (2, 8)), -0.2, 0.2)), 0.5, 2.0),
        "displacement": jnp.clip(jax.random.uniform(key_of[7], (3, NR, NC), jnp.float32, -0.05, 0.05) * block_scale(key_of[7], (3, NR, NC), ((1, 16), (2, 8)), -0.4, 0.0), -0.05, 0.05),
        "velocity": bell_draw(key_of[8], (3, NR, NC), 0.5, 3.0, ((1, 16), (2, 8)), jnp.float32),
    }


MU_BASE = 10.0
LAMBDA_BULK = 20.0
PRESTRESS = 4.0
TIME_STEP = 1.0
GRAVITY = -1.0
EIG_LOW = 0.5
EIG_HIGH = 2.0


def corners(padded):
    return padded[..., :-1, :-1], padded[..., :-1, 1:], padded[..., 1:, :-1], padded[..., 1:, 1:]


def node_sum(lower_part, upper_part):
    summed = lower_part + upper_part
    return summed[..., 1:, 1:] + lower_part[..., 1:, :-1] + upper_part[..., :-1, 1:] + summed[..., :-1, :-1]


def mass_terms(padded, area_cells):
    anchor, beside, upward, across = corners(padded)
    lower_tri = area_cells[0] / 12.0 * (anchor + beside + across)
    upper_tri = area_cells[1] / 12.0 * (anchor + across + upward)
    return node_sum(lower_tri, upper_tri)


def chebyshev(rhs, weight_diag, apply_mass):
    centre = 0.5 * (EIG_HIGH + EIG_LOW)
    half_width = 0.5 * (EIG_HIGH - EIG_LOW)
    ratio_eig = centre / half_width
    rho_now = 1.0 / ratio_eig
    inv_diag = 1.0 / (2.0 * weight_diag)
    residual = rhs
    direction = inv_diag * residual / centre
    solution = direction
    for sweep in range(ITERS):
        residual = residual - apply_mass(direction)
        rho_next = 1.0 / (2.0 * ratio_eig - rho_now)
        direction = (rho_next * rho_now) * direction + (2.0 * rho_next / half_width) * (inv_diag * residual)
        solution = solution + direction
        rho_now = rho_next
    return solution


def membrane_fields(projected):
    through = jnp.mean(projected.reshape(POINTS, COMP, projected.shape[1], projected.shape[2]), axis=0)
    return jnp.stack([through[0], through[1], through[5], through[7]], 0)


def first_piola(stretch_x, stretch_y, fields):
    gram_xx = jnp.sum(stretch_x * stretch_x, axis=0)
    gram_xy = jnp.sum(stretch_x * stretch_y, axis=0)
    gram_yy = jnp.sum(stretch_y * stretch_y, axis=0)
    determinant = gram_xx * gram_yy - gram_xy * gram_xy
    inv_xx = gram_yy / determinant
    inv_xy = -gram_xy / determinant
    inv_yy = gram_xx / determinant
    push_x = stretch_x * inv_xx + stretch_y * inv_xy
    push_y = stretch_x * inv_xy + stretch_y * inv_yy
    shear_mod = MU_BASE * (1.5 + jnp.tanh(fields[3]))
    log_jacobian = 0.5 * jnp.log(determinant)
    piola_x = shear_mod * (stretch_x - push_x) + LAMBDA_BULK * log_jacobian * push_x + PRESTRESS * (stretch_x * fields[0] + stretch_y * fields[2])
    piola_y = shear_mod * (stretch_y - push_y) + LAMBDA_BULK * log_jacobian * push_y + PRESTRESS * (stretch_x * fields[2] + stretch_y * fields[1])
    return piola_x, piola_y


def triangle_forces(padded, volume):
    anchor, beside, upward, across = corners(padded)
    unit_x = jnp.array([1.0, 0.0, 0.0], jnp.float32)[:, None, None]
    unit_y = jnp.array([0.0, 1.0, 0.0], jnp.float32)[:, None, None]
    lower_x = unit_x + beside[:3] - anchor[:3]
    lower_y = unit_y + across[:3] - beside[:3]
    lower_fields = (anchor[3:] + beside[3:] + across[3:]) / 3.0
    upper_x = unit_x + across[:3] - upward[:3]
    upper_y = unit_y + upward[:3] - anchor[:3]
    upper_fields = (anchor[3:] + across[3:] + upward[3:]) / 3.0
    piola_lx, piola_ly = first_piola(lower_x, lower_y, lower_fields)
    piola_ux, piola_uy = first_piola(upper_x, upper_y, upper_fields)
    force_beside = -volume[0] * (piola_lx - piola_ly)
    force_across_low = -volume[0] * piola_ly
    force_across_up = -volume[1] * piola_ux
    force_upward = -volume[1] * (piola_uy - piola_ux)
    force_anchor = -(force_beside + force_across_low) - (force_across_up + force_upward)
    return force_anchor, force_beside, force_upward, force_across_low + force_across_up


def force_sum(force_anchor, force_beside, force_upward, force_across):
    return force_anchor[..., 1:, 1:] + force_beside[..., 1:, :-1] + force_upward[..., :-1, 1:] + force_across[..., :-1, :-1]


def reference(old_values, pair_rows, pair_targets, pair_weights, pair_counts, cell_area, thickness, displacement, velocity):
    slot_index = jnp.arange(CAP, dtype=jnp.int32)
    is_live = slot_index[None, None, :] < pair_counts[:, :, None]
    slot_weight = jnp.where(is_live, pair_weights, 0.0)
    slot_target = jnp.where(is_live, pair_targets, 0)
    offsets = (jnp.arange(RANKS, dtype=jnp.int32) * QD)[:, None]

    def one_owner(owner):
        rows_global = pair_rows[:, owner, :] + offsets
        picked = old_values[:, rows_global] * slot_weight[:, owner, :][None]
        empty = jnp.zeros((CH, ELEMS), jnp.float32)
        return empty.at[:, slot_target[:, owner, :].reshape(-1)].add(picked.reshape(CH, -1))

    per_owner = lax.map(one_owner, jnp.arange(RANKS, dtype=jnp.int32))
    element_sums = per_owner.reshape(N_OLD, N_NEW, CH, 2, RD, CD).transpose(2, 3, 1, 4, 0, 5).reshape(CH, 2, NR, NC)
    row_ok = jnp.arange(NR, dtype=jnp.int32) < NR - 1
    col_ok = jnp.arange(NC, dtype=jnp.int32) < NC - 1
    valid = (row_ok[:, None] & col_ok[None, :]).astype(jnp.float32)
    element_sums = element_sums * valid
    area_valid = cell_area * valid
    volume = thickness * area_valid
    sums_cells = jnp.pad(element_sums, ((0, 0), (0, 0), (1, 0), (1, 0)))
    area_cells = jnp.pad(area_valid, ((0, 0), (1, 0), (1, 0)))
    volume_cells = jnp.pad(volume, ((0, 0), (1, 0), (1, 0)))
    rhs = node_sum(sums_cells[:, 0], sums_cells[:, 1]) / 3.0
    weight_diag = node_sum(area_cells[0] / 12.0, area_cells[1] / 12.0)
    node_mass = node_sum(volume_cells[0] / 3.0, volume_cells[1] / 3.0)

    def apply_mass(field):
        return weight_diag * field + mass_terms(jnp.pad(field, ((0, 0), (1, 1), (1, 1))), area_cells)

    projected = chebyshev(rhs, weight_diag, apply_mass)
    nodal = jnp.concatenate([displacement, membrane_fields(projected)], 0)
    force_anchor, force_beside, force_upward, force_across = triangle_forces(jnp.pad(nodal, ((0, 0), (1, 1), (1, 1))), volume_cells)
    forces = force_sum(force_anchor, force_beside, force_upward, force_across)
    gravity_vec = jnp.array([0.0, 0.0, GRAVITY], jnp.float32)[:, None, None]
    velocity_next = velocity + TIME_STEP * (forces / node_mass + gravity_vec)
    return projected, velocity_next
```

```python
import functools

import jax
import jax.numpy as jnp
from jax import lax
from jax.experimental import pallas as pl
from jax.experimental.pallas import tpu as pltpu
from jax.sharding import PartitionSpec as P

POINTS = 4
COMP = 8
ITERS = 3
MU_BASE = 10.0
LAMBDA_BULK = 20.0
PRESTRESS = 4.0
TIME_STEP = 1.0
GRAVITY = -1.0
EIG_LOW = 0.5
EIG_HIGH = 2.0

LANE = 128
FRONT = 8
BATCH = 4
HALO = 4
MESH = pl.DeviceIdType.MESH
MIB = 1024 * 1024

VMEM = pl.BlockSpec(memory_space=pltpu.VMEM)
SMEM = pl.BlockSpec(memory_space=pltpu.SMEM)
ANY = pl.BlockSpec(memory_space=pl.ANY)


def lane_ids(shape):
    return lax.broadcasted_iota(jnp.int32, shape, len(shape) - 1)


def gather_kernel(counts, rows, weights, values, out, table):
    ranks = out.shape[0]
    per = out.shape[1] * 4
    channels, total = values.shape

    def flip(step, _):
        start = pl.multiple_of(step * LANE, LANE)
        part = values[:, pl.ds(start, LANE)]
        table[pl.ds(start, LANE), :] = jnp.concatenate([part] * 4, axis=0).T
        return 0

    lax.fori_loop(0, total // LANE, flip, 0)
    lane = lane_ids((1, LANE))
    first, second, third = lane < 32, lane < 64, lane < 96

    def one_owner(owner, _):
        blocks = (counts[owner] + 31) // 32
        for block in range(per // 32):

            @pl.when(block < blocks)
            def _():
                for row in range(8):
                    base = owner * per + block * 32 + row * 4
                    part = [
                        table[pl.ds(rows[base + g], 1), :] * weights[base + g] for g in range(4)
                    ]
                    merged = jnp.where(
                        first,
                        part[0],
                        jnp.where(second, part[1], jnp.where(third, part[2], part[3])),
                    )
                    out[owner, pl.ds(block * 8 + row, 1), :] = merged

            @pl.when(block >= blocks)
            def _():
                out[owner, pl.ds(block * 8, 8), :] = jnp.zeros((8, LANE), jnp.float32)

        return 0

    lax.fori_loop(0, ranks, one_owner, 0)


def gather(counts, rows, weights, values):
    ranks, per = rows.shape
    return pl.pallas_call(
        gather_kernel,
        out_shape=jax.ShapeDtypeStruct((ranks, per // 4, LANE), jnp.float32),
        in_specs=[SMEM, SMEM, SMEM, VMEM],
        out_specs=VMEM,
        scratch_shapes=[pltpu.VMEM((values.shape[1], LANE), jnp.float32)],
        compiler_params=pltpu.CompilerParams(vmem_limit_bytes=24 * MIB),
        name="gather",
    )(counts, rows.reshape(-1), weights.reshape(-1), values)


def scatter_kernel(rows_dev, cols_dev, ids, clash, data, part, right_tile, acc):
    width = cols_dev + LANE
    ranks, payload, _ = data.shape
    per = payload * 4
    size = acc.shape[0]
    chunk = width // 8
    zeros = jnp.zeros((chunk, LANE), jnp.float32)
    acc[pl.ds(0, FRONT), :] = jnp.zeros((FRONT, LANE), jnp.float32)

    def clear(step, _):
        acc[pl.ds(pl.multiple_of(FRONT + step * chunk, 8), chunk), :] = zeros
        return 0

    lax.fori_loop(0, (size - FRONT) // chunk, clear, 0)

    lane = lane_ids((1, LANE))
    masks = [(lane >= 32 * g) & (lane < 32 * g + 32) for g in range(4)]

    def add_rows(source, first, count):
        slots = [(r, g) for r in range(count) for g in range(4)]
        where_to = [ids[source * per + (first + r) * 4 + g] for r, g in slots]
        new = [data[source, pl.ds(first + r, 1), :] for r in range(count)]
        old = [acc[pl.ds(row, 1), :] for row in where_to]
        for (r, g), row, have in zip(slots, where_to, old):
            pltpu.store(acc.at[pl.ds(row, 1), :], have + new[r], mask=masks[g])

    def one_source(source, _):
        @pl.when(clash[source] == 0)
        def _():
            for first in range(0, payload, BATCH):
                add_rows(source, first, BATCH)

        @pl.when(clash[source] != 0)
        def _():
            def slow(row, _):
                add_rows(source, row, 1)
                return 0

            lax.fori_loop(0, payload, slow, 0)

        return 0

    lax.fori_loop(0, ranks, one_source, 0)

    def fold(total):
        flipped = total.T
        return flipped[0:32] + flipped[32:64] + flipped[64:96] + flipped[96:128]

    upper_base = rows_dev * width
    for tile in range(width // LANE):

        def one_row(i, carry, tile=tile):
            base = i * width + tile * LANE + FRONT
            lower = acc[pl.ds(base, LANE), :]
            upper = acc[pl.ds(base + upper_base, LANE), :]
            lower_left = acc[pl.ds(base - 1, LANE), :]
            upper_left = acc[pl.ds(base + upper_base - 1, LANE), :]
            shared = upper + lower_left
            part[i, :, tile * LANE : (tile + 1) * LANE] = fold(lower + shared + carry)
            return shared + upper_left

        last = lax.fori_loop(0, rows_dev, one_row, jnp.zeros((LANE, LANE), jnp.float32))
        part[rows_dev, :, tile * LANE : (tile + 1) * LANE] = fold(last)

    edge = lane_ids((part.shape[1], LANE))

    def pack(i, _):
        own = part[i, :, cols_dev - LANE : cols_dev]
        ghost = part[i, :, cols_dev:width]
        right_tile[i] = jnp.where(edge >= 64, own, jnp.where(edge == 0, ghost, 0.0))
        return 0

    lax.fori_loop(0, rows_dev + 1, pack, 0)


def scatter(ids, clash, data, rows_dev, cols_dev):
    channels = LANE // 4
    width = cols_dev + LANE
    return pl.pallas_call(
        functools.partial(scatter_kernel, rows_dev, cols_dev),
        out_shape=(
            jax.ShapeDtypeStruct((rows_dev + 1, channels, width), jnp.float32),
            jax.ShapeDtypeStruct((rows_dev + 1, channels, LANE), jnp.float32),
        ),
        in_specs=[SMEM, SMEM, VMEM],
        out_specs=(VMEM, VMEM),
        scratch_shapes=[pltpu.VMEM((FRONT + 2 * rows_dev * width, LANE), jnp.float32)],
        compiler_params=pltpu.CompilerParams(vmem_limit_bytes=56 * MIB),
        name="scatter",
    )(ids.reshape(-1), clash, data)


def exchange_kernel(pick, body, edge, *refs):
    outs, send_sem, recv_sem = refs[:-2], refs[-2], refs[-1]
    n_old, n_new = lax.axis_size("old"), lax.axis_size("new")
    old, new = lax.axis_index("old"), lax.axis_index("new")
    left, right = lax.rem(old + n_old - 1, n_old), lax.rem(old + 1, n_old)
    below, above = lax.rem(new + n_new - 1, n_new), lax.rem(new + 1, n_new)
    around = [
        (old, above),
        (old, below),
        (right, new),
        (left, new),
        (right, above),
        (left, above),
        (right, below),
        (left, below),
    ]
    barrier = pltpu.get_barrier_semaphore()
    for device in around:
        pl.semaphore_signal(barrier, inc=1, device_id=device, device_id_type=MESH)
    pl.semaphore_wait(barrier, len(around))
    copies = [
        pltpu.make_async_remote_copy(
            src_ref=source,
            dst_ref=target,
            send_sem=send_sem.at[at],
            recv_sem=recv_sem.at[at],
            device_id=device,
            device_id_type=MESH,
        )
        for at, (source, target, device) in enumerate(zip(pick(body, edge), outs, around))
    ]
    for copy in copies:
        copy.start()
    for copy in copies:
        copy.wait()


def pick_partial(body, edge):
    top, low = pl.ds(body.shape[0] - HALO - 1, HALO + 1), pl.ds(0, HALO)
    near = pl.ds(0, LANE)
    return [
        body.at[top],
        body.at[low],
        edge,
        body.at[:, :, near],
        edge.at[top],
        body.at[top, :, near],
        edge.at[low],
        body.at[low, :, near],
    ]


def pick_fields(body, edge):
    rows, cols = body.shape[1:]
    top, low = pl.ds(rows - 8, 8), pl.ds(0, 8)
    near, far = pl.ds(0, LANE), pl.ds(cols - LANE, LANE)
    return [
        body.at[:, top, :],
        body.at[:, low, :],
        body.at[:, :, far],
        body.at[:, :, near],
        body.at[:, top, far],
        body.at[:, top, near],
        body.at[:, low, far],
        body.at[:, low, near],
    ]


def exchange(pick, shapes, body, edge, ident):
    return pl.pallas_call(
        functools.partial(exchange_kernel, pick),
        out_shape=tuple(jax.ShapeDtypeStruct(shape, jnp.float32) for shape in shapes),
        in_specs=[ANY, ANY],
        out_specs=(ANY,) * len(shapes),
        scratch_shapes=[pltpu.SemaphoreType.DMA((8,)), pltpu.SemaphoreType.DMA((8,))],
        compiler_params=pltpu.CompilerParams(collective_id=ident, has_side_effects=True),
        name="exchange",
    )(body, edge)


def first_piola(stretch_x, stretch_y, fields):
    gram_xx = sum(x * x for x in stretch_x)
    gram_xy = sum(x * y for x, y in zip(stretch_x, stretch_y))
    gram_yy = sum(y * y for y in stretch_y)
    determinant = gram_xx * gram_yy - gram_xy * gram_xy
    inverse = 1.0 / determinant
    inv_xx = gram_yy * inverse
    inv_xy = -gram_xy * inverse
    inv_yy = gram_xx * inverse
    shear_mod = MU_BASE * (1.5 + jnp.tanh(fields[3]))
    bulk = LAMBDA_BULK * 0.5 * jnp.log(determinant)
    piola_x, piola_y = [], []
    for along_x, along_y in zip(stretch_x, stretch_y):
        push_x = along_x * inv_xx + along_y * inv_xy
        push_y = along_x * inv_xy + along_y * inv_yy
        piola_x.append(
            shear_mod * (along_x - push_x)
            + bulk * push_x
            + PRESTRESS * (along_x * fields[0] + along_y * fields[2])
        )
        piola_y.append(
            shear_mod * (along_y - push_y)
            + bulk * push_y
            + PRESTRESS * (along_x * fields[2] + along_y * fields[1])
        )
    return piola_x, piola_y


def sheet_kernel(n_rows, n_cols, *refs):
    (part, p_dn, p_up, p_l, p_r, p_dl, p_dr, p_ul, p_ur) = refs[:9]
    (body, s_dn, s_up, s_l, s_r, s_dl, s_dr, s_ul, s_ur) = refs[9:18]
    velocity, out, vel_out = refs[18:21]
    resid, dir_a, dir_b, total, field, mem, mass, coef = refs[21:]
    rows_dev, cols_dev = body.shape[1:]
    channels, width = part.shape[1:]
    tall = rows_dev + 16

    edge8, edge_mid = lane_ids((8, LANE)), lane_ids((rows_dev, LANE))
    for f in range(body.shape[0]):
        field[f, 0:8, 0:cols_dev] = s_dn[f]
        field[f, 8 : 8 + rows_dev, 0:cols_dev] = body[f]
        field[f, 8 + rows_dev : tall, 0:cols_dev] = s_up[f]
        field[f, 0:8, cols_dev:width] = jnp.where(edge8 < 64, s_dr[f], s_dl[f])
        field[f, 8 : 8 + rows_dev, cols_dev:width] = jnp.where(edge_mid < 64, s_r[f], s_l[f])
        field[f, 8 + rows_dev : tall, cols_dev:width] = jnp.where(edge8 < 64, s_ur[f], s_ul[f])

    shape = (tall, width)
    row = lax.broadcasted_iota(jnp.int32, shape, 0) - 8 + lax.axis_index("new") * rows_dev
    lane = lax.broadcasted_iota(jnp.int32, shape, 1)
    col = jnp.where(lane < cols_dev + 64, lane, lane - width) + lax.axis_index("old") * cols_dev
    valid = (row >= 0) & (row < n_rows - 1) & (col >= 0) & (col < n_cols - 1)

    def from_left(x):
        return pltpu.roll(x, 1, 1)

    def from_right(x):
        return pltpu.roll(x, width - 1, 1)

    def from_below(x):
        return pltpu.roll(x, 1, 0)

    def from_above(x):
        return pltpu.roll(x, tall - 1, 0)

    area_low = jnp.where(valid, field[0], 0.0)
    area_up = jnp.where(valid, field[1], 0.0)
    field[2] = field[2] * area_low
    field[3] = field[3] * area_up
    low, high = area_low / 12.0, area_up / 12.0
    both = low + high
    low_left, high_below = from_left(low), from_below(high)
    weight = both + low_left + high_below + from_below(from_left(both))
    inv = jnp.where(weight > 0.0, 1.0 / (2.0 * weight), 0.0)
    inv_right = from_right(inv)
    east, north = low + high_below, high + low_left
    coef[0] = inv * (1.0 / 3.0)
    coef[1] = inv * north
    coef[2] = inv * from_below(north)
    coef[3] = from_left(inv * east)
    coef[4] = from_left(inv * both)
    coef[5] = inv_right * east
    coef[6] = inv_right * from_below(both)
    vol_low, vol_up = field[2], field[3]
    mass[...] = (
        vol_low
        + vol_up
        + from_left(vol_low)
        + from_below(vol_up)
        + from_below(from_left(vol_low + vol_up))
    ) * (1.0 / 3.0)

    centre = 0.5 * (EIG_HIGH + EIG_LOW)
    half_width = 0.5 * (EIG_HIGH - EIG_LOW)
    ratio_eig = centre / half_width
    rho = 1.0 / ratio_eig
    edge = lane_ids((channels, LANE))

    def widen(middle, left, right):
        first = middle[:, 0:LANE] + jnp.where(edge == 0, left, 0.0)
        last = middle[:, cols_dev:width] + jnp.where(edge >= 64, left, right)
        return jnp.concatenate([first, middle[:, LANE:cols_dev], last], axis=1)

    def begin(e, rhs):
        scaled = rhs * coef[0, pl.ds(e + 4, 1), :]
        start = scaled * (1.0 / centre)
        resid[e] = scaled
        dir_a[e] = start
        total[e] = start

    def own(i):
        return widen(part[i], p_l[i], p_r[i])

    def lower(i):
        return widen(p_dn[i], p_dl[i], p_dr[i])

    def upper(i):
        return widen(p_up[i], p_ul[i], p_ur[i])

    for e in range(HALO):
        begin(e, lower(e))
    begin(HALO, own(0) + lower(HALO))

    def inner(i, _):
        begin(i + HALO, own(i))
        return 0

    lax.fori_loop(1, rows_dev, inner, 0)
    begin(rows_dev + HALO, own(rows_dev) + upper(0))
    for e in range(1, HALO):
        begin(rows_dev + HALO + e, upper(e))

    mem[...] = jnp.zeros_like(mem)
    source, target = dir_a, dir_b
    for sweep in range(ITERS):
        rho_next = 1.0 / (2.0 * ratio_eig - rho)
        keep, gain = rho_next * rho, 2.0 * rho_next / half_width
        rho = rho_next
        final = sweep == ITERS - 1

        def step(e, _, source=source, target=target, keep=keep, gain=gain, final=final):
            k = [coef[c, pl.ds(e + 4, 1), :] for c in range(1, 7)]
            through = None
            for group in range(0, channels, 8):
                at = slice(group, group + 8)
                here, over, under = source[e, at, :], source[e + 1, at, :], source[e - 1, at, :]
                to_left = k[2] * here + k[3] * over
                to_right = k[4] * here + k[5] * under
                left = resid[e, at, :] - (
                    here
                    + k[0] * over
                    + k[1] * under
                    + pltpu.roll(to_left, width - 1, 1)
                    + pltpu.roll(to_right, 1, 1)
                )
                new = keep * here + gain * left
                summed = total[e, at, :] + new
                total[e, at, :] = summed
                if final:
                    through = summed if through is None else through + summed
                else:
                    resid[e, at, :] = left
                    target[e, at, :] = new
            if final:
                through = through * (1.0 / POINTS)
                for at, value in enumerate((0, 1, 5, 7)):
                    mem[at, pl.ds(e + 4, 1), :] = through[value : value + 1, :]
            return 0

        lax.fori_loop(1 + sweep, rows_dev + 2 * HALO - 1 - sweep, step, 0)
        source, target = target, source

    for channel in range(channels):
        for block in range(0, rows_dev, 8):
            out[channel, block : block + 8, :] = total[
                HALO + block : HALO + block + 8, channel, 0:cols_dev
            ]

    anchor = [field[4 + c] for c in range(3)]
    beside = [from_right(x) for x in anchor]
    upward = [from_above(x) for x in anchor]
    across = [from_above(x) for x in beside]
    m_anchor = [mem[c] for c in range(4)]
    m_beside = [from_right(x) for x in m_anchor]
    m_upward = [from_above(x) for x in m_anchor]
    m_across = [from_above(x) for x in m_beside]
    third = 1.0 / 3.0
    m_low = [(a + b + x) * third for a, b, x in zip(m_anchor, m_beside, m_across)]
    m_up = [(a + x + u) * third for a, x, u in zip(m_anchor, m_across, m_upward)]
    low_x = [b - a for a, b in zip(anchor, beside)]
    low_y = [x - b for b, x in zip(beside, across)]
    up_x = [x - u for u, x in zip(upward, across)]
    up_y = [u - a for a, u in zip(anchor, upward)]
    low_x[0], up_x[0] = 1.0 + low_x[0], 1.0 + up_x[0]
    low_y[1], up_y[1] = 1.0 + low_y[1], 1.0 + up_y[1]
    piola_lx, piola_ly = first_piola(low_x, low_y, m_low)
    piola_ux, piola_uy = first_piola(up_x, up_y, m_up)
    vol_low, vol_up = field[2], field[3]
    node_mass = mass[8 : 8 + rows_dev, 0:cols_dev]
    for c in range(3):
        f_beside = -vol_low * (piola_lx[c] - piola_ly[c])
        f_across_low = -vol_low * piola_ly[c]
        f_across_up = -vol_up * piola_ux[c]
        f_upward = -vol_up * (piola_uy[c] - piola_ux[c])
        f_anchor = -(f_beside + f_across_low) - (f_across_up + f_upward)
        force = (
            f_anchor
            + from_left(f_beside)
            + from_below(f_upward)
            + from_below(from_left(f_across_low + f_across_up))
        )
        speed_up = force[8 : 8 + rows_dev, 0:cols_dev] / node_mass
        if c == 2:
            speed_up = speed_up + GRAVITY
        vel_out[c] = velocity[c] + TIME_STEP * speed_up


def sheet(part, part_halo, body, body_halo, velocity, n_rows, n_cols):
    channels, width = part.shape[1:]
    rows_dev, cols_dev = body.shape[1:]
    tall, long = rows_dev + 16, rows_dev + 2 * HALO
    block = pltpu.VMEM((long, channels, width), jnp.float32)

    def plane(count):
        return pltpu.VMEM((count, tall, width), jnp.float32)

    return pl.pallas_call(
        functools.partial(sheet_kernel, n_rows, n_cols),
        out_shape=(
            jax.ShapeDtypeStruct((channels, rows_dev, cols_dev), jnp.float32),
            jax.ShapeDtypeStruct(velocity.shape, jnp.float32),
        ),
        in_specs=[VMEM] * 19,
        out_specs=(VMEM, VMEM),
        scratch_shapes=[
            block,
            block,
            block,
            block,
            plane(body.shape[0]),
            plane(4),
            pltpu.VMEM((tall, width), jnp.float32),
            plane(7),
        ],
        compiler_params=pltpu.CompilerParams(vmem_limit_bytes=56 * MIB),
        name="sheet",
    )(part, *part_halo, body, *body_halo, velocity)


def local(
    old_values,
    pair_rows,
    pair_targets,
    pair_weights,
    pair_counts,
    cell_area,
    thickness,
    displacement,
    velocity,
):
    channels = old_values.shape[0]
    ranks, slots = pair_rows.shape[1:]
    rows_dev, cols_dev = cell_area.shape[1:]
    n_old, n_new = lax.axis_size("old"), lax.axis_size("new")
    width = cols_dev + LANE

    slot = jnp.arange(slots, dtype=jnp.int32)[None, :]
    owner = jnp.arange(ranks, dtype=jnp.int32)[:, None]
    cell = pair_targets[0] // cols_dev
    col = pair_targets[0] % cols_dev
    outside = ((owner % n_new == n_new - 1) & (cell % rows_dev == rows_dev - 1)) | (
        (owner // n_new == n_old - 1) & (col == cols_dev - 1)
    )
    used = (slot < pair_counts[0][:, None]) & ~outside
    slot_weight = jnp.where(used, pair_weights[0], 0.0)
    slot_row = jnp.where(used, FRONT + cell * width + col, FRONT + cols_dev + slot)

    picked = gather(pair_counts[0], pair_rows[0], slot_weight, old_values)
    ids = lax.all_to_all(slot_row, ("old", "new"), split_axis=0, concat_axis=0, tiled=True)
    arrived = lax.all_to_all(picked, ("old", "new"), split_axis=0, concat_axis=0, tiled=True)

    batches = ids.reshape(ranks, slots // (4 * BATCH), BATCH, 4)
    clash = jnp.zeros((ranks,), jnp.bool_)
    for a in range(BATCH):
        for b in range(a):
            clash = clash | jnp.any(batches[:, :, a] == batches[:, :, b], axis=(1, 2))

    body = jnp.concatenate([cell_area, thickness, displacement], axis=0)
    fields = body.shape[0]
    body_halo = exchange(
        pick_fields,
        [(fields, 8, cols_dev)] * 2 + [(fields, rows_dev, LANE)] * 2 + [(fields, 8, LANE)] * 4,
        body,
        body,
        1,
    )
    part, edge = scatter(ids, clash.astype(jnp.int32), arrived, rows_dev, cols_dev)
    part_halo = exchange(
        pick_partial,
        [(HALO + 1, channels, width), (HALO, channels, width)]
        + [(rows_dev + 1, channels, LANE)] * 2
        + [(HALO + 1, channels, LANE)] * 2
        + [(HALO, channels, LANE)] * 2,
        part,
        edge,
        2,
    )
    return sheet(
        part, part_halo, body, body_halo, velocity, n_new * rows_dev, n_old * cols_dev
    )


def solution(mesh):
    return jax.shard_map(
        local,
        mesh=mesh,
        in_specs=(
            P(None, ("old", "new")),
            P(("old", "new"), None, None),
            P(("old", "new"), None, None),
            P(("old", "new"), None, None),
            P(("old", "new"), None),
            P(None, "new", "old"),
            P(None, "new", "old"),
            P(None, "new", "old"),
            P(None, "new", "old"),
        ),
        out_specs=(P(None, "new", "old"), P(None, "new", "old")),
        check_vma=False,
    )
```

```python
import functools

import jax
import jax.numpy as jnp
from jax import lax
from jax.experimental import pallas as pl
from jax.experimental.pallas import tpu as pltpu
from jax.sharding import PartitionSpec as P

POINTS = 4
COMP = 8
ITERS = 3
MU_BASE = 10.0
LAMBDA_BULK = 20.0
PRESTRESS = 4.0
TIME_STEP = 1.0
GRAVITY = -1.0
EIG_LOW = 0.5
EIG_HIGH = 2.0

LANE = 128
FRONT = 8
BATCH = 4
HALO = 4
STRIDE = 37
MESH = pl.DeviceIdType.MESH
MIB = 1024 * 1024

VMEM = pl.BlockSpec(memory_space=pltpu.VMEM)
SMEM = pl.BlockSpec(memory_space=pltpu.SMEM)
ANY = pl.BlockSpec(memory_space=pl.ANY)


def lane_ids(shape):
    return lax.broadcasted_iota(jnp.int32, shape, len(shape) - 1)


def send_kernel(
    rows_dev,
    cols_dev,
    counts,
    rows_in,
    targets,
    weights_in,
    values,
    body,
    arrived,
    arrived_ids,
    s_dn,
    s_up,
    s_l,
    s_r,
    s_dl,
    s_dr,
    s_ul,
    s_ur,
    table,
    picked,
    ids,
    notes,
    weights_flat,
    rows,
    weights,
    local_sem,
    pair_sem,
    near_send,
    near_recv,
):
    n_old, n_new = lax.axis_size("old"), lax.axis_size("new")
    old, new = lax.axis_index("old"), lax.axis_index("new")
    ranks, payload, _ = picked.shape
    slots = payload * 4
    width = cols_dev + LANE
    total = values.shape[1]
    me = old * n_new + new

    load_rows = pltpu.make_async_copy(rows_in, rows, local_sem.at[0])
    load_rows.start()

    barrier = pltpu.get_barrier_semaphore()

    def greet(step, _):
        other = lax.rem(me + step, ranks)
        pl.semaphore_signal(
            barrier, inc=1, device_id=(other // n_new, other % n_new), device_id_type=MESH
        )
        return 0

    lax.fori_loop(1, ranks, greet, 0)

    slot = lane_ids((ranks, slots))
    owner = lax.broadcasted_iota(jnp.int32, (ranks, slots), 0)
    count = jnp.broadcast_to(counts[...].astype(jnp.float32), (ranks, ranks)).T.astype(jnp.int32)
    target = targets[0]
    cell, col = target // cols_dev, target % cols_dev
    outside = ((owner % n_new == n_new - 1) & (cell % rows_dev == rows_dev - 1)) | (
        (owner // n_new == n_old - 1) & (col == cols_dev - 1)
    )
    used = (slot < count) & jnp.logical_not(outside)
    weights_flat[...] = jnp.where(used, weights_in[0], 0.0)
    load_weights = pltpu.make_async_copy(weights_flat, weights, local_sem.at[1])
    load_weights.start()
    where_to = jnp.where(used, FRONT + cell * width + col, FRONT + cols_dev + slot)
    clash = jnp.zeros((ranks, slots), jnp.int32)
    for gap in range(1, BATCH):
        same = (where_to == pltpu.roll(where_to, 4 * gap, 1)) & (slot % (4 * BATCH) >= 4 * gap)
        clash = clash | same.astype(jnp.int32)
    notes[:, 0:slots] = where_to
    notes[:, slots : slots + LANE] = jnp.broadcast_to(
        jnp.max(clash, axis=1, keepdims=True), (ranks, LANE)
    )

    unroll = 8

    def flip(step, _):
        for at in range(unroll):
            start = pl.multiple_of((step * unroll + at) * LANE, LANE)
            part = values[:, pl.ds(start, LANE)]
            table[pl.ds(start, LANE), :] = jnp.concatenate([part] * 4, axis=0).T
        return 0

    lax.fori_loop(0, total // (LANE * unroll), flip, 0)
    load_rows.wait()
    load_weights.wait()
    pl.semaphore_wait(barrier, ranks - 1)

    left, right = lax.rem(old + n_old - 1, n_old), lax.rem(old + 1, n_old)
    below, above = lax.rem(new + n_new - 1, n_new), lax.rem(new + 1, n_new)
    top, low = pl.ds(rows_dev - 8, 8), pl.ds(0, 8)
    near, far = pl.ds(0, LANE), pl.ds(cols_dev - LANE, LANE)
    halo = [
        (body.at[:, top, :], s_dn, (old, above)),
        (body.at[:, low, :], s_up, (old, below)),
        (body.at[:, :, far], s_l, (right, new)),
        (body.at[:, :, near], s_r, (left, new)),
        (body.at[:, top, far], s_dl, (right, above)),
        (body.at[:, top, near], s_dr, (left, above)),
        (body.at[:, low, far], s_ul, (right, below)),
        (body.at[:, low, near], s_ur, (left, below)),
    ]
    halo = [
        pltpu.make_async_remote_copy(
            src_ref=source,
            dst_ref=target,
            send_sem=near_send.at[at],
            recv_sem=near_recv.at[at],
            device_id=device,
            device_id_type=MESH,
        )
        for at, (source, target, device) in enumerate(halo)
    ]
    for copy in halo:
        copy.start()

    lane = lane_ids((1, LANE))
    first, second, third = lane < 32, lane < 64, lane < 96

    def fill(owner):
        for row in range(payload):
            part = [
                table[pl.ds(rows[0, owner, row * 4 + g], 1), :] * weights[owner, row * 4 + g]
                for g in range(4)
            ]
            merged = jnp.where(
                first, part[0], jnp.where(second, part[1], jnp.where(third, part[2], part[3]))
            )
            picked[owner, pl.ds(row, 1), :] = merged
        ids[owner] = notes[pl.ds(owner, 1), :]

    def one_owner(step, _):
        shift = lax.rem(step * STRIDE, ranks)
        to_old = lax.rem(old + shift // n_new, n_old)
        to_new = lax.rem(new + shift % n_new, n_new)
        owner = to_old * n_new + to_new
        fill(owner)
        for at, (source, target) in enumerate(((picked, arrived), (ids, arrived_ids))):
            pltpu.make_async_remote_copy(
                src_ref=source.at[owner],
                dst_ref=target.at[me],
                send_sem=pair_sem.at[2 * at],
                recv_sem=pair_sem.at[2 * at + 1],
                device_id=(to_old, to_new),
                device_id_type=MESH,
            ).start()
        return 0

    lax.fori_loop(1, ranks, one_owner, 0)
    fill(me)
    for at, (source, target) in enumerate(((picked, arrived), (ids, arrived_ids))):
        pltpu.make_async_copy(source.at[me], target.at[me], pair_sem.at[2 * at + 1]).start()
    for copy in halo:
        copy.wait()
    for at, (source, target) in enumerate(((picked, arrived), (ids, arrived_ids))):
        rest = pl.ds(0, ranks - 1)
        pltpu.make_async_copy(source.at[rest], source.at[rest], pair_sem.at[2 * at]).wait()
        pltpu.make_async_copy(source, target, pair_sem.at[2 * at + 1]).wait()


def send(counts, rows, targets, weights, values, body):
    ranks, slots = rows.shape[1:]
    payload = slots // 4
    fields, rows_dev, cols_dev = body.shape
    shapes = (
        [(ranks, payload, LANE)]
        + [(fields, 8, cols_dev)] * 2
        + [(fields, rows_dev, LANE)] * 2
        + [(fields, 8, LANE)] * 4
    )
    shapes = [jax.ShapeDtypeStruct(shape, jnp.float32) for shape in shapes]
    shapes.insert(1, jax.ShapeDtypeStruct((ranks, 1, slots + LANE), jnp.int32))
    result = pl.pallas_call(
        functools.partial(send_kernel, rows_dev, cols_dev),
        out_shape=tuple(shapes),
        in_specs=[VMEM, ANY, VMEM, VMEM, VMEM, ANY],
        out_specs=(ANY,) * len(shapes),
        scratch_shapes=[
            pltpu.VMEM((values.shape[1], LANE), jnp.float32),
            pltpu.VMEM((ranks, payload, LANE), jnp.float32),
            pltpu.VMEM((ranks, 1, slots + LANE), jnp.int32),
            pltpu.VMEM((ranks, slots + LANE), jnp.int32),
            pltpu.VMEM((ranks, slots), jnp.float32),
            pltpu.SMEM((1, ranks, slots), jnp.int32),
            pltpu.SMEM((ranks, slots), jnp.float32),
            pltpu.SemaphoreType.DMA((2,)),
            pltpu.SemaphoreType.DMA((4,)),
            pltpu.SemaphoreType.DMA((8,)),
            pltpu.SemaphoreType.DMA((8,)),
        ],
        compiler_params=pltpu.CompilerParams(
            vmem_limit_bytes=24 * MIB, collective_id=1, has_side_effects=True
        ),
        name="send",
    )(counts, rows, targets, weights, values, body)
    return result[0], result[1], result[2:]


def scatter_kernel(rows_dev, cols_dev, ids_in, data_in, part, right_tile, acc, carry, data, ids, sem):
    width = cols_dev + LANE
    ranks, payload, _ = data.shape
    size = acc.shape[0]
    chunk = width // 8
    load_ids = pltpu.make_async_copy(ids_in, ids, sem.at[0])
    load_data = pltpu.make_async_copy(data_in, data, sem.at[1])
    load_ids.start()
    load_data.start()
    zeros = jnp.zeros((chunk, LANE), jnp.float32)
    acc[pl.ds(0, FRONT), :] = jnp.zeros((FRONT, LANE), jnp.float32)
    carry[...] = jnp.zeros_like(carry)

    def clear(step, _):
        acc[pl.ds(pl.multiple_of(FRONT + step * chunk, 8), chunk), :] = zeros
        return 0

    lax.fori_loop(0, (size - FRONT) // chunk, clear, 0)
    load_ids.wait()
    load_data.wait()

    lane = lane_ids((1, LANE))
    masks = [(lane >= 32 * g) & (lane < 32 * g + 32) for g in range(4)]

    def add_rows(source, first, count):
        slots = [(r, g) for r in range(count) for g in range(4)]
        where_to = [ids[source, 0, (first + r) * 4 + g] for r, g in slots]
        new = [data[source, pl.ds(first + r, 1), :] for r in range(count)]
        old = [acc[pl.ds(row, 1), :] for row in where_to]
        for (r, g), row, have in zip(slots, where_to, old):
            pltpu.store(acc.at[pl.ds(row, 1), :], have + new[r], mask=masks[g])

    def one_source(source, _):
        clash = ids[source, 0, payload * 4]

        @pl.when(clash == 0)
        def _():
            for first in range(0, payload, BATCH):
                add_rows(source, first, BATCH)

        @pl.when(clash != 0)
        def _():
            def slow(row, _):
                add_rows(source, row, 1)
                return 0

            lax.fori_loop(0, payload, slow, 0)

        return 0

    lax.fori_loop(0, ranks, one_source, 0)

    def fold(total):
        flipped = total.T
        return (flipped[0:32] + flipped[32:64]) + (flipped[64:96] + flipped[96:128])

    upper_base = rows_dev * width
    edge = lane_ids((part.shape[1], LANE))

    def pack(i, own, ghost):
        right_tile[i] = jnp.where(edge >= 64, own, jnp.where(edge == 0, ghost, 0.0))

    tiles = width // LANE

    def one_row(i, _):
        done = []
        for tile in range(tiles):
            span = slice(tile * LANE, (tile + 1) * LANE)
            base = pl.multiple_of(i * width + tile * LANE + FRONT, 8)
            lower = acc[pl.ds(base, LANE), :]
            upper = acc[pl.ds(pl.multiple_of(base + upper_base, 8), LANE), :]
            shared = upper + acc[pl.ds(base - 1, LANE), :]
            summed = lower + shared + carry[span, :]
            carry[span, :] = shared + acc[pl.ds(base + upper_base - 1, LANE), :]
            folded = fold(summed)
            part[i, :, span] = folded
            done.append(folded)
        pack(i, done[-2], done[-1])
        return 0

    lax.fori_loop(0, rows_dev, one_row, 0)
    done = [fold(carry[tile * LANE : (tile + 1) * LANE, :]) for tile in range(tiles)]
    for tile in range(tiles):
        part[rows_dev, :, tile * LANE : (tile + 1) * LANE] = done[tile]
    pack(rows_dev, done[-2], done[-1])


def scatter(ids, data, rows_dev, cols_dev):
    channels = LANE // 4
    width = cols_dev + LANE
    return pl.pallas_call(
        functools.partial(scatter_kernel, rows_dev, cols_dev),
        out_shape=(
            jax.ShapeDtypeStruct((rows_dev + 1, channels, width), jnp.float32),
            jax.ShapeDtypeStruct((rows_dev + 1, channels, LANE), jnp.float32),
        ),
        in_specs=[ANY, ANY],
        out_specs=(VMEM, VMEM),
        scratch_shapes=[
            pltpu.VMEM((FRONT + 2 * rows_dev * width, LANE), jnp.float32),
            pltpu.VMEM((width, LANE), jnp.float32),
            pltpu.VMEM(data.shape, jnp.float32),
            pltpu.SMEM(ids.shape, jnp.int32),
            pltpu.SemaphoreType.DMA((2,)),
        ],
        compiler_params=pltpu.CompilerParams(vmem_limit_bytes=56 * MIB),
        name="scatter",
    )(ids, data)


def exchange_kernel(pick, body, edge, *refs):
    outs, send_sem, recv_sem = refs[:-2], refs[-2], refs[-1]
    n_old, n_new = lax.axis_size("old"), lax.axis_size("new")
    old, new = lax.axis_index("old"), lax.axis_index("new")
    left, right = lax.rem(old + n_old - 1, n_old), lax.rem(old + 1, n_old)
    below, above = lax.rem(new + n_new - 1, n_new), lax.rem(new + 1, n_new)
    around = [
        (old, above),
        (old, below),
        (right, new),
        (left, new),
        (right, above),
        (left, above),
        (right, below),
        (left, below),
    ]
    barrier = pltpu.get_barrier_semaphore()
    for device in around:
        pl.semaphore_signal(barrier, inc=1, device_id=device, device_id_type=MESH)
    pl.semaphore_wait(barrier, len(around))
    copies = [
        pltpu.make_async_remote_copy(
            src_ref=source,
            dst_ref=target,
            send_sem=send_sem.at[at],
            recv_sem=recv_sem.at[at],
            device_id=device,
            device_id_type=MESH,
        )
        for at, (source, target, device) in enumerate(zip(pick(body, edge), outs, around))
    ]
    for copy in copies:
        copy.start()
    for copy in copies:
        copy.wait()


def pick_partial(body, edge):
    top, low = pl.ds(body.shape[0] - HALO - 1, HALO + 1), pl.ds(0, HALO)
    near = pl.ds(0, LANE)
    return [
        body.at[top],
        body.at[low],
        edge,
        body.at[:, :, near],
        edge.at[top],
        body.at[top, :, near],
        edge.at[low],
        body.at[low, :, near],
    ]


def exchange(pick, shapes, body, edge, ident):
    return pl.pallas_call(
        functools.partial(exchange_kernel, pick),
        out_shape=tuple(jax.ShapeDtypeStruct(shape, jnp.float32) for shape in shapes),
        in_specs=[ANY, ANY],
        out_specs=(ANY,) * len(shapes),
        scratch_shapes=[pltpu.SemaphoreType.DMA((8,)), pltpu.SemaphoreType.DMA((8,))],
        compiler_params=pltpu.CompilerParams(collective_id=ident, has_side_effects=True),
        name="exchange",
    )(body, edge)


def first_piola(stretch_x, stretch_y, fields):
    gram_xx = sum(x * x for x in stretch_x)
    gram_xy = sum(x * y for x, y in zip(stretch_x, stretch_y))
    gram_yy = sum(y * y for y in stretch_y)
    determinant = gram_xx * gram_yy - gram_xy * gram_xy
    inverse = 1.0 / determinant
    inv_xx = gram_yy * inverse
    inv_xy = -gram_xy * inverse
    inv_yy = gram_xx * inverse
    shear_mod = MU_BASE * (1.5 + jnp.tanh(fields[3]))
    bulk = LAMBDA_BULK * 0.5 * jnp.log(determinant)
    piola_x, piola_y = [], []
    for along_x, along_y in zip(stretch_x, stretch_y):
        push_x = along_x * inv_xx + along_y * inv_xy
        push_y = along_x * inv_xy + along_y * inv_yy
        piola_x.append(
            shear_mod * (along_x - push_x)
            + bulk * push_x
            + PRESTRESS * (along_x * fields[0] + along_y * fields[2])
        )
        piola_y.append(
            shear_mod * (along_y - push_y)
            + bulk * push_y
            + PRESTRESS * (along_x * fields[2] + along_y * fields[1])
        )
    return piola_x, piola_y


def sheet_kernel(n_rows, n_cols, *refs):
    (part, p_dn, p_up, p_l, p_r, p_dl, p_dr, p_ul, p_ur) = refs[:9]
    (body, s_dn, s_up, s_l, s_r, s_dl, s_dr, s_ul, s_ur) = refs[9:18]
    velocity, out, vel_out = refs[18:21]
    resid, dir_a, dir_b, total, field, mem, mass, coef = refs[21:]
    rows_dev, cols_dev = body.shape[1:]
    channels, width = part.shape[1:]
    tall = rows_dev + 16

    edge8, edge_mid = lane_ids((8, LANE)), lane_ids((rows_dev, LANE))
    for f in range(body.shape[0]):
        field[f, 0:8, 0:cols_dev] = s_dn[f]
        field[f, 8 : 8 + rows_dev, 0:cols_dev] = body[f]
        field[f, 8 + rows_dev : tall, 0:cols_dev] = s_up[f]
        field[f, 0:8, cols_dev:width] = jnp.where(edge8 < 64, s_dr[f], s_dl[f])
        field[f, 8 : 8 + rows_dev, cols_dev:width] = jnp.where(edge_mid < 64, s_r[f], s_l[f])
        field[f, 8 + rows_dev : tall, cols_dev:width] = jnp.where(edge8 < 64, s_ur[f], s_ul[f])

    shape = (tall, width)
    row = lax.broadcasted_iota(jnp.int32, shape, 0) - 8 + lax.axis_index("new") * rows_dev
    lane = lax.broadcasted_iota(jnp.int32, shape, 1)
    col = jnp.where(lane < cols_dev + 64, lane, lane - width) + lax.axis_index("old") * cols_dev
    valid = (row >= 0) & (row < n_rows - 1) & (col >= 0) & (col < n_cols - 1)

    def from_left(x):
        return pltpu.roll(x, 1, 1)

    def from_right(x):
        return pltpu.roll(x, width - 1, 1)

    def from_below(x):
        return pltpu.roll(x, 1, 0)

    def from_above(x):
        return pltpu.roll(x, tall - 1, 0)

    area_low = jnp.where(valid, field[0], 0.0)
    area_up = jnp.where(valid, field[1], 0.0)
    field[2] = field[2] * area_low
    field[3] = field[3] * area_up
    low, high = area_low / 12.0, area_up / 12.0
    both = low + high
    low_left, high_below = from_left(low), from_below(high)
    weight = both + low_left + high_below + from_below(from_left(both))
    inv = jnp.where(weight > 0.0, 1.0 / (2.0 * weight), 0.0)
    inv_right = from_right(inv)
    east, north = low + high_below, high + low_left
    coef[0] = inv * (1.0 / 3.0)
    coef[1] = inv * north
    coef[2] = inv * from_below(north)
    coef[3] = from_left(inv * east)
    coef[4] = from_left(inv * both)
    coef[5] = inv_right * east
    coef[6] = inv_right * from_below(both)
    vol_low, vol_up = field[2], field[3]
    mass[...] = (
        vol_low
        + vol_up
        + from_left(vol_low)
        + from_below(vol_up)
        + from_below(from_left(vol_low + vol_up))
    ) * (1.0 / 3.0)

    centre = 0.5 * (EIG_HIGH + EIG_LOW)
    half_width = 0.5 * (EIG_HIGH - EIG_LOW)
    ratio_eig = centre / half_width
    rho = 1.0 / ratio_eig
    edge = lane_ids((channels, LANE))

    def widen(middle, left, right):
        first = middle[:, 0:LANE] + jnp.where(edge == 0, left, 0.0)
        last = middle[:, cols_dev:width] + jnp.where(edge >= 64, left, right)
        return jnp.concatenate([first, middle[:, LANE:cols_dev], last], axis=1)

    def begin(e, rhs):
        scaled = rhs * coef[0, pl.ds(e + 4, 1), :]
        start = scaled * (1.0 / centre)
        resid[e] = scaled
        dir_a[e] = start
        total[e] = start

    def own(i):
        return widen(part[i], p_l[i], p_r[i])

    def lower(i):
        return widen(p_dn[i], p_dl[i], p_dr[i])

    def upper(i):
        return widen(p_up[i], p_ul[i], p_ur[i])

    for e in range(HALO):
        begin(e, lower(e))
    begin(HALO, own(0) + lower(HALO))

    def inner(i, _):
        begin(i + HALO, own(i))
        return 0

    lax.fori_loop(1, rows_dev, inner, 0)
    begin(rows_dev + HALO, own(rows_dev) + upper(0))
    for e in range(1, HALO):
        begin(rows_dev + HALO + e, upper(e))

    mem[...] = jnp.zeros_like(mem)
    source, target = dir_a, dir_b
    for sweep in range(ITERS):
        rho_next = 1.0 / (2.0 * ratio_eig - rho)
        keep, gain = rho_next * rho, 2.0 * rho_next / half_width
        rho = rho_next
        final = sweep == ITERS - 1

        def step(e, _, source=source, target=target, keep=keep, gain=gain, final=final):
            k = [coef[c, pl.ds(e + 4, 1), :] for c in range(1, 7)]
            through = None
            for group in range(0, channels, 8):
                at = slice(group, group + 8)
                here, over, under = source[e, at, :], source[e + 1, at, :], source[e - 1, at, :]
                to_left = k[2] * here + k[3] * over
                to_right = k[4] * here + k[5] * under
                left = resid[e, at, :] - (
                    here
                    + k[0] * over
                    + k[1] * under
                    + pltpu.roll(to_left, width - 1, 1)
                    + pltpu.roll(to_right, 1, 1)
                )
                new = keep * here + gain * left
                summed = total[e, at, :] + new
                total[e, at, :] = summed
                if final:
                    through = summed if through is None else through + summed
                else:
                    resid[e, at, :] = left
                    target[e, at, :] = new
            if final:
                through = through * (1.0 / POINTS)
                for at, value in enumerate((0, 1, 5, 7)):
                    mem[at, pl.ds(e + 4, 1), :] = through[value : value + 1, :]
            return 0

        lax.fori_loop(1 + sweep, rows_dev + 2 * HALO - 1 - sweep, step, 0)
        source, target = target, source

    for channel in range(channels):
        for block in range(0, rows_dev, 8):
            out[channel, block : block + 8, :] = total[
                HALO + block : HALO + block + 8, channel, 0:cols_dev
            ]

    anchor = [field[4 + c] for c in range(3)]
    beside = [from_right(x) for x in anchor]
    upward = [from_above(x) for x in anchor]
    across = [from_above(x) for x in beside]
    m_anchor = [mem[c] for c in range(4)]
    m_beside = [from_right(x) for x in m_anchor]
    m_upward = [from_above(x) for x in m_anchor]
    m_across = [from_above(x) for x in m_beside]
    third = 1.0 / 3.0
    m_low = [(a + b + x) * third for a, b, x in zip(m_anchor, m_beside, m_across)]
    m_up = [(a + x + u) * third for a, x, u in zip(m_anchor, m_across, m_upward)]
    low_x = [b - a for a, b in zip(anchor, beside)]
    low_y = [x - b for b, x in zip(beside, across)]
    up_x = [x - u for u, x in zip(upward, across)]
    up_y = [u - a for a, u in zip(anchor, upward)]
    low_x[0], up_x[0] = 1.0 + low_x[0], 1.0 + up_x[0]
    low_y[1], up_y[1] = 1.0 + low_y[1], 1.0 + up_y[1]
    piola_lx, piola_ly = first_piola(low_x, low_y, m_low)
    piola_ux, piola_uy = first_piola(up_x, up_y, m_up)
    vol_low, vol_up = field[2], field[3]
    node_mass = mass[8 : 8 + rows_dev, 0:cols_dev]
    for c in range(3):
        f_beside = -vol_low * (piola_lx[c] - piola_ly[c])
        f_across_low = -vol_low * piola_ly[c]
        f_across_up = -vol_up * piola_ux[c]
        f_upward = -vol_up * (piola_uy[c] - piola_ux[c])
        f_anchor = -(f_beside + f_across_low) - (f_across_up + f_upward)
        force = (
            f_anchor
            + from_left(f_beside)
            + from_below(f_upward)
            + from_below(from_left(f_across_low + f_across_up))
        )
        speed_up = force[8 : 8 + rows_dev, 0:cols_dev] / node_mass
        if c == 2:
            speed_up = speed_up + GRAVITY
        vel_out[c] = velocity[c] + TIME_STEP * speed_up


def sheet(part, part_halo, body, body_halo, velocity, n_rows, n_cols):
    channels, width = part.shape[1:]
    rows_dev, cols_dev = body.shape[1:]
    tall, long = rows_dev + 16, rows_dev + 2 * HALO
    block = pltpu.VMEM((long, channels, width), jnp.float32)

    def plane(count):
        return pltpu.VMEM((count, tall, width), jnp.float32)

    return pl.pallas_call(
        functools.partial(sheet_kernel, n_rows, n_cols),
        out_shape=(
            jax.ShapeDtypeStruct((channels, rows_dev, cols_dev), jnp.float32),
            jax.ShapeDtypeStruct(velocity.shape, jnp.float32),
        ),
        in_specs=[VMEM] * 19,
        out_specs=(VMEM, VMEM),
        scratch_shapes=[
            block,
            block,
            block,
            block,
            plane(body.shape[0]),
            plane(4),
            pltpu.VMEM((tall, width), jnp.float32),
            plane(7),
        ],
        compiler_params=pltpu.CompilerParams(vmem_limit_bytes=56 * MIB),
        name="sheet",
    )(part, *part_halo, body, *body_halo, velocity)


def local(
    old_values,
    pair_rows,
    pair_targets,
    pair_weights,
    pair_counts,
    cell_area,
    thickness,
    displacement,
    velocity,
):
    channels = old_values.shape[0]
    rows_dev, cols_dev = cell_area.shape[1:]
    n_old, n_new = lax.axis_size("old"), lax.axis_size("new")
    width = cols_dev + LANE
    body = jnp.concatenate([cell_area, thickness, displacement], axis=0)
    arrived, ids, body_halo = send(
        pair_counts, pair_rows, pair_targets, pair_weights, old_values, body
    )
    part, edge = scatter(ids, arrived, rows_dev, cols_dev)
    part_halo = exchange(
        pick_partial,
        [(HALO + 1, channels, width), (HALO, channels, width)]
        + [(rows_dev + 1, channels, LANE)] * 2
        + [(HALO + 1, channels, LANE)] * 2
        + [(HALO, channels, LANE)] * 2,
        part,
        edge,
        2,
    )
    return sheet(
        part, part_halo, body, body_halo, velocity, n_new * rows_dev, n_old * cols_dev
    )


def solution(mesh):
    return jax.shard_map(
        local,
        mesh=mesh,
        in_specs=(
            P(None, ("old", "new")),
            P(("old", "new"), None, None),
            P(("old", "new"), None, None),
            P(("old", "new"), None, None),
            P(("old", "new"), None),
            P(None, "new", "old"),
            P(None, "new", "old"),
            P(None, "new", "old"),
            P(None, "new", "old"),
        ),
        out_specs=(P(None, "new", "old"), P(None, "new", "old")),
        check_vma=False,
    )
```

```python
import functools

import jax
import jax.numpy as jnp
from jax import lax
from jax.experimental import pallas as pl
from jax.experimental.pallas import tpu as pltpu
from jax.sharding import PartitionSpec as P

POINTS = 4
COMP = 8
ITERS = 3
MU_BASE = 10.0
LAMBDA_BULK = 20.0
PRESTRESS = 4.0
TIME_STEP = 1.0
GRAVITY = -1.0
EIG_LOW = 0.5
EIG_HIGH = 2.0

LANE = 128
FRONT = 8
BATCH = 4
HALO = 4
STRIDE = 37
MESH = pl.DeviceIdType.MESH
MIB = 1024 * 1024

VMEM = pl.BlockSpec(memory_space=pltpu.VMEM)
SMEM = pl.BlockSpec(memory_space=pltpu.SMEM)
HBM = pl.BlockSpec(memory_space=pltpu.HBM)


def lane_ids(shape):
    return lax.broadcasted_iota(jnp.int32, shape, len(shape) - 1)


def neighbours():
    n_old, n_new = lax.axis_size("old"), lax.axis_size("new")
    old, new = lax.axis_index("old"), lax.axis_index("new")
    left, right = lax.rem(old + n_old - 1, n_old), lax.rem(old + 1, n_old)
    below, above = lax.rem(new + n_new - 1, n_new), lax.rem(new + 1, n_new)
    return [
        (old, above),
        (old, below),
        (right, new),
        (left, new),
        (right, above),
        (left, above),
        (right, below),
        (left, below),
    ]


def to_neighbours(sources, targets, send_sem, recv_sem):
    return [
        pltpu.make_async_remote_copy(
            src_ref=source,
            dst_ref=target,
            send_sem=send_sem.at[at],
            recv_sem=recv_sem.at[at],
            device_id=device,
            device_id_type=MESH,
        )
        for at, (source, target, device) in enumerate(zip(sources, targets, neighbours()))
    ]


def send_kernel(
    rows_dev,
    cols_dev,
    counts,
    rows_in,
    targets_in,
    weights_in,
    values_in,
    area,
    thick,
    shift_in,
    arrived,
    arrived_ids,
    s_dn,
    s_up,
    s_l,
    s_r,
    s_dl,
    s_dr,
    s_ul,
    s_ur,
    table,
    picked,
    ids,
    notes,
    weights_flat,
    targets,
    weights_raw,
    values,
    rim_low,
    rim_high,
    rim_left,
    rim_right,
    pack_up,
    pack_down,
    pack_right,
    pack_left,
    rows,
    weights,
    local_sem,
    pair_sem,
    near_send,
    near_recv,
):
    n_old, n_new = lax.axis_size("old"), lax.axis_size("new")
    old, new = lax.axis_index("old"), lax.axis_index("new")
    ranks, payload, _ = picked.shape
    slots = payload * 4
    width = cols_dev + LANE
    total = values.shape[1]
    me = old * n_new + new
    top, low = pl.ds(rows_dev - 8, 8), pl.ds(0, 8)
    near, far = pl.ds(0, LANE), pl.ds(cols_dev - LANE, LANE)

    loads = [
        (targets_in, targets),
        (weights_in, weights_raw),
        (values_in, values),
        (rows_in, rows),
    ]
    for source, at, count in ((area, 0, 2), (thick, 2, 2), (shift_in, 4, 3)):
        into = pl.ds(at, count)
        loads.append((source.at[:, top, :], rim_high.at[into]))
        loads.append((source.at[:, low, :], rim_low.at[into]))
        loads.append((source.at[:, :, far], rim_right.at[into]))
        loads.append((source.at[:, :, near], rim_left.at[into]))
    loads = [
        pltpu.make_async_copy(source, target, local_sem.at[at])
        for at, (source, target) in enumerate(loads)
    ]
    for load in loads:
        load.start()

    barrier = pltpu.get_barrier_semaphore()

    def greet(step, _):
        other = lax.rem(me + step, ranks)
        pl.semaphore_signal(
            barrier, inc=1, device_id=(other // n_new, other % n_new), device_id_type=MESH
        )
        return 0

    lax.fori_loop(1, ranks, greet, 0)

    slot = lane_ids((ranks, slots))
    owner = lax.broadcasted_iota(jnp.int32, (ranks, slots), 0)
    count = jnp.broadcast_to(counts[...].astype(jnp.float32), (ranks, ranks)).T.astype(jnp.int32)
    loads[0].wait()
    loads[1].wait()
    target = targets[0]
    cell, col = target // cols_dev, target % cols_dev
    outside = ((owner % n_new == n_new - 1) & (cell % rows_dev == rows_dev - 1)) | (
        (owner // n_new == n_old - 1) & (col == cols_dev - 1)
    )
    used = (slot < count) & jnp.logical_not(outside)
    weights_flat[...] = jnp.where(used, weights_raw[0], 0.0)
    load_weights = pltpu.make_async_copy(weights_flat, weights, local_sem.at[len(loads)])
    load_weights.start()
    where_to = jnp.where(used, FRONT + cell * width + col, FRONT + cols_dev + slot)
    clash = jnp.zeros((ranks, slots), jnp.int32)
    for gap in range(1, BATCH):
        same = (where_to == pltpu.roll(where_to, 4 * gap, 1)) & (slot % (4 * BATCH) >= 4 * gap)
        clash = clash | same.astype(jnp.int32)
    notes[:, 0:slots] = where_to
    notes[:, slots : slots + LANE] = jnp.broadcast_to(
        jnp.max(clash, axis=1, keepdims=True), (ranks, LANE)
    )

    unroll = 8
    loads[2].wait()

    def flip(step, _):
        for at in range(unroll):
            start = pl.multiple_of((step * unroll + at) * LANE, LANE)
            part = values[:, pl.ds(start, LANE)]
            table[pl.ds(start, LANE), :] = jnp.concatenate([part] * 4, axis=0).T
        return 0

    lax.fori_loop(0, total // (LANE * unroll), flip, 0)

    for load in loads[3:]:
        load.wait()
    pack_up[...] = jnp.zeros_like(pack_up)
    pack_down[...] = jnp.zeros_like(pack_down)
    lane = lane_ids((rows_dev, LANE))
    to_right = jnp.zeros((rows_dev, LANE), jnp.float32)
    to_left = jnp.zeros((rows_dev, LANE), jnp.float32)
    for f in range(7):
        if f < 2:
            pack_up[5 * f : 5 * f + 5, :] = rim_high[f, 3:8, :]
            pack_down[4 * f : 4 * f + 4, :] = rim_low[f, 0:4, :]
        else:
            pack_up[8 + f : 9 + f, :] = rim_high[f, 7:8, :]
            if f >= 4:
                pack_down[4 + f : 5 + f, :] = rim_low[f, 0:1, :]
        mine = lane // 8 == f
        to_right = jnp.where(mine, pltpu.roll(rim_right[f], 8 * f + 5, 1), to_right)
        to_left = jnp.where(mine, pltpu.roll(rim_left[f], 8 * f, 1), to_left)
    pack_right[...] = to_right
    pack_left[...] = to_left
    load_weights.wait()
    pl.semaphore_wait(barrier, ranks - 1)

    halo = to_neighbours(
        [
            pack_up,
            pack_down,
            pack_right,
            pack_left,
            pack_right.at[top],
            pack_left.at[top],
            pack_right.at[low],
            pack_left.at[low],
        ],
        [s_dn, s_up, s_l, s_r, s_dl, s_dr, s_ul, s_ur],
        near_send,
        near_recv,
    )
    for copy in halo:
        copy.start()

    lane = lane_ids((1, LANE))
    first, second, third = lane < 32, lane < 64, lane < 96

    def fill(owner):
        for row in range(payload):
            part = [
                table[pl.ds(rows[0, owner, row * 4 + g], 1), :] * weights[owner, row * 4 + g]
                for g in range(4)
            ]
            merged = jnp.where(
                first, part[0], jnp.where(second, part[1], jnp.where(third, part[2], part[3]))
            )
            picked[owner, pl.ds(row, 1), :] = merged
        ids[owner] = notes[pl.ds(owner, 1), :]

    def one_owner(step, _):
        shift = lax.rem(step * STRIDE, ranks)
        to_old = lax.rem(old + shift // n_new, n_old)
        to_new = lax.rem(new + shift % n_new, n_new)
        owner = to_old * n_new + to_new
        fill(owner)
        for at, (source, target) in enumerate(((picked, arrived), (ids, arrived_ids))):
            pltpu.make_async_remote_copy(
                src_ref=source.at[owner],
                dst_ref=target.at[me],
                send_sem=pair_sem.at[2 * at],
                recv_sem=pair_sem.at[2 * at + 1],
                device_id=(to_old, to_new),
                device_id_type=MESH,
            ).start()
        return 0

    lax.fori_loop(1, ranks, one_owner, 0)
    fill(me)
    for at, (source, target) in enumerate(((picked, arrived), (ids, arrived_ids))):
        pltpu.make_async_copy(source.at[me], target.at[me], pair_sem.at[2 * at + 1]).start()
    for copy in halo:
        copy.wait()
    for at, (source, target) in enumerate(((picked, arrived), (ids, arrived_ids))):
        rest = pl.ds(0, ranks - 1)
        pltpu.make_async_copy(source.at[rest], source.at[rest], pair_sem.at[2 * at]).wait()
        pltpu.make_async_copy(source, target, pair_sem.at[2 * at + 1]).wait()


def send(counts, rows, targets, weights, values, area, thick, shift):
    ranks, slots = rows.shape[1:]
    payload = slots // 4
    rows_dev, cols_dev = area.shape[1:]
    halo = [(16, cols_dev)] * 2 + [(rows_dev, LANE)] * 2 + [(8, LANE)] * 4
    shapes = [jax.ShapeDtypeStruct(shape, jnp.float32) for shape in [(ranks, payload, LANE)] + halo]
    shapes.insert(1, jax.ShapeDtypeStruct((ranks, 1, slots + LANE), jnp.int32))

    def scratch(*shape):
        return pltpu.VMEM(shape, jnp.float32)

    result = pl.pallas_call(
        functools.partial(send_kernel, rows_dev, cols_dev),
        out_shape=tuple(shapes),
        in_specs=[VMEM] + [HBM] * 7,
        out_specs=(HBM,) * len(shapes),
        scratch_shapes=[
            scratch(values.shape[1], LANE),
            scratch(ranks, payload, LANE),
            pltpu.VMEM((ranks, 1, slots + LANE), jnp.int32),
            pltpu.VMEM((ranks, slots + LANE), jnp.int32),
            scratch(ranks, slots),
            pltpu.VMEM(targets.shape, jnp.int32),
            scratch(*weights.shape),
            scratch(*values.shape),
            scratch(7, 8, cols_dev),
            scratch(7, 8, cols_dev),
            scratch(7, rows_dev, LANE),
            scratch(7, rows_dev, LANE),
            scratch(16, cols_dev),
            scratch(16, cols_dev),
            scratch(rows_dev, LANE),
            scratch(rows_dev, LANE),
            pltpu.SMEM(rows.shape, jnp.int32),
            pltpu.SMEM((ranks, slots), jnp.float32),
            pltpu.SemaphoreType.DMA((17,)),
            pltpu.SemaphoreType.DMA((4,)),
            pltpu.SemaphoreType.DMA((8,)),
            pltpu.SemaphoreType.DMA((8,)),
        ],
        compiler_params=pltpu.CompilerParams(
            vmem_limit_bytes=24 * MIB, collective_id=1, has_side_effects=True
        ),
        name="send",
    )(counts, rows, targets, weights, values, area, thick, shift)
    return result[0], result[1], result[2:]


def scatter_kernel(rows_dev, cols_dev, ids_in, data_in, part, cols_right, cols_left, acc, carry, data, ids, sem):
    width = cols_dev + LANE
    ranks, payload, _ = data.shape
    size = acc.shape[0]
    chunk = width // 8
    load_ids = pltpu.make_async_copy(ids_in, ids, sem.at[0])
    load_data = pltpu.make_async_copy(data_in, data, sem.at[1])
    load_ids.start()
    load_data.start()
    zeros = jnp.zeros((chunk, LANE), jnp.float32)
    acc[pl.ds(0, FRONT), :] = jnp.zeros((FRONT, LANE), jnp.float32)
    carry[...] = jnp.zeros_like(carry)

    def clear(step, _):
        acc[pl.ds(pl.multiple_of(FRONT + step * chunk, 8), chunk), :] = zeros
        return 0

    lax.fori_loop(0, (size - FRONT) // chunk, clear, 0)
    load_ids.wait()
    load_data.wait()

    lane = lane_ids((1, LANE))
    masks = [(lane >= 32 * g) & (lane < 32 * g + 32) for g in range(4)]

    def add_rows(source, first, count):
        slots = [(r, g) for r in range(count) for g in range(4)]
        where_to = [ids[source, 0, (first + r) * 4 + g] for r, g in slots]
        new = [data[source, pl.ds(first + r, 1), :] for r in range(count)]
        old = [acc[pl.ds(row, 1), :] for row in where_to]
        for (r, g), row, have in zip(slots, where_to, old):
            pltpu.store(acc.at[pl.ds(row, 1), :], have + new[r], mask=masks[g])

    def one_source(source, _):
        clash = ids[source, 0, payload * 4]

        @pl.when(clash == 0)
        def _():
            for first in range(0, payload, BATCH):
                add_rows(source, first, BATCH)

        @pl.when(clash != 0)
        def _():
            def slow(row, _):
                add_rows(source, row, 1)
                return 0

            lax.fori_loop(0, payload, slow, 0)

        return 0

    lax.fori_loop(0, ranks, one_source, 0)

    def fold(total):
        flipped = total.T
        return (flipped[0:32] + flipped[32:64]) + (flipped[64:96] + flipped[96:128])

    upper_base = rows_dev * width
    lane = lane_ids((part.shape[1], LANE))

    def pack(i, own_near, own_far, ghost):
        tile, place = i // 16, i % 16
        mine = lane // 8 == place
        ends = pltpu.roll(jnp.where(lane == 0, ghost, own_far), 8 * place + 4, 1)
        cols_right[tile] = jnp.where(mine, ends, cols_right[tile])
        cols_left[tile] = jnp.where(mine, pltpu.roll(own_near, 8 * place, 1), cols_left[tile])

    cols_right[...] = jnp.zeros_like(cols_right)
    cols_left[...] = jnp.zeros_like(cols_left)
    tiles = width // LANE

    def one_row(i, _):
        done = []
        for tile in range(tiles):
            span = slice(tile * LANE, (tile + 1) * LANE)
            base = pl.multiple_of(i * width + tile * LANE + FRONT, 8)
            lower = acc[pl.ds(base, LANE), :]
            upper = acc[pl.ds(pl.multiple_of(base + upper_base, 8), LANE), :]
            shared = upper + acc[pl.ds(base - 1, LANE), :]
            summed = lower + shared + carry[span, :]
            carry[span, :] = shared + acc[pl.ds(base + upper_base - 1, LANE), :]
            folded = fold(summed)
            part[i, :, span] = folded
            done.append(folded)
        pack(i, done[0], done[-2], done[-1])
        return 0

    lax.fori_loop(0, rows_dev, one_row, 0)
    done = [fold(carry[tile * LANE : (tile + 1) * LANE, :]) for tile in range(tiles)]
    for tile in range(tiles):
        part[rows_dev, :, tile * LANE : (tile + 1) * LANE] = done[tile]
    pack(rows_dev, done[0], done[-2], done[-1])


def scatter(ids, data, rows_dev, cols_dev):
    channels = LANE // 4
    width = cols_dev + LANE
    return pl.pallas_call(
        functools.partial(scatter_kernel, rows_dev, cols_dev),
        out_shape=(
            jax.ShapeDtypeStruct((rows_dev + 1, channels, width), jnp.float32),
            jax.ShapeDtypeStruct((rows_dev // 16 + 1, channels, LANE), jnp.float32),
            jax.ShapeDtypeStruct((rows_dev // 16 + 1, channels, LANE), jnp.float32),
        ),
        in_specs=[HBM, HBM],
        out_specs=(VMEM, VMEM, VMEM),
        scratch_shapes=[
            pltpu.VMEM((FRONT + 2 * rows_dev * width, LANE), jnp.float32),
            pltpu.VMEM((width, LANE), jnp.float32),
            pltpu.VMEM(data.shape, jnp.float32),
            pltpu.SMEM(ids.shape, jnp.int32),
            pltpu.SemaphoreType.DMA((2,)),
        ],
        compiler_params=pltpu.CompilerParams(vmem_limit_bytes=56 * MIB),
        name="scatter",
    )(ids, data)


def first_piola(stretch_x, stretch_y, fields):
    gram_xx = sum(x * x for x in stretch_x)
    gram_xy = sum(x * y for x, y in zip(stretch_x, stretch_y))
    gram_yy = sum(y * y for y in stretch_y)
    determinant = gram_xx * gram_yy - gram_xy * gram_xy
    inverse = 1.0 / determinant
    inv_xx = gram_yy * inverse
    inv_xy = -gram_xy * inverse
    inv_yy = gram_xx * inverse
    shear_mod = MU_BASE * (1.5 + jnp.tanh(fields[3]))
    bulk = LAMBDA_BULK * 0.5 * jnp.log(determinant)
    piola_x, piola_y = [], []
    for along_x, along_y in zip(stretch_x, stretch_y):
        push_x = along_x * inv_xx + along_y * inv_xy
        push_y = along_x * inv_xy + along_y * inv_yy
        piola_x.append(
            shear_mod * (along_x - push_x)
            + bulk * push_x
            + PRESTRESS * (along_x * fields[0] + along_y * fields[2])
        )
        piola_y.append(
            shear_mod * (along_y - push_y)
            + bulk * push_y
            + PRESTRESS * (along_x * fields[2] + along_y * fields[1])
        )
    return piola_x, piola_y


def sheet_kernel(n_rows, n_cols, *refs):
    part_in, cols_right, cols_left, area_in, thick_in, shift_in = refs[:6]
    s_in = refs[6:14]
    total_out, speed_out = refs[14:16]
    p_halo, s_halo, refs = refs[16:24], refs[24:32], refs[32:]
    part, resid, dir_a, dir_b, dir_c, total, field, mem, mass, coef, speed = refs[:11]
    load_sem, save_sem, send_sem, recv_sem = refs[11:]
    p_dn, p_up, p_l, p_r, p_dl, p_dr, p_ul, p_ur = p_halo
    s_dn, s_up, s_l, s_r, s_dl, s_dr, s_ul, s_ur = s_halo
    rows_dev, cols_dev = area_in.shape[1:]
    channels, width = part.shape[1:]
    tall = rows_dev + 16
    middle, main = pl.ds(8, rows_dev), pl.ds(0, cols_dev)

    barrier = pltpu.get_barrier_semaphore()
    for device in neighbours():
        pl.semaphore_signal(barrier, inc=1, device_id=device, device_id_type=MESH)

    field[:, 0:8, :] = jnp.zeros((7, 8, width), jnp.float32)
    field[:, 8 + rows_dev : tall, :] = jnp.zeros((7, 8, width), jnp.float32)
    loads = [
        (area_in, field.at[pl.ds(0, 2), middle, main]),
        (thick_in, field.at[pl.ds(2, 2), middle, main]),
        (shift_in, field.at[pl.ds(4, 3), middle, main]),
    ] + list(zip(s_in, s_halo))
    loads.append((part_in, part))
    loads = [
        pltpu.make_async_copy(source, target, load_sem.at[at])
        for at, (source, target) in enumerate(loads)
    ]
    for load in loads:
        load.start()

    high, low = pl.ds(part_in.shape[0] - HALO - 1, HALO + 1), pl.ds(0, HALO)
    tiles_high, tiles_low = pl.ds((rows_dev - 1) // 16, 2), pl.ds(0, 1)
    pl.semaphore_wait(barrier, 8)
    copies = to_neighbours(
        [
            part_in.at[high],
            part_in.at[low],
            cols_right,
            cols_left,
            cols_right.at[tiles_high],
            cols_left.at[tiles_high],
            cols_right.at[tiles_low],
            cols_left.at[tiles_low],
        ],
        p_halo,
        send_sem,
        recv_sem,
    )
    for copy in copies[2:] + copies[:2]:
        copy.start()

    for load in loads[:-1]:
        load.wait()
    sides = []
    for left, right, size in ((s_l, s_r, rows_dev), (s_dl, s_dr, 8), (s_ul, s_ur, 8)):
        sides.append((left[...], right[...], lane_ids((size, LANE))))
    for f in range(7):
        if f < 2:
            field[f, 3:8, 0:cols_dev] = s_dn[5 * f : 5 * f + 5, :]
            field[f, 8 + rows_dev : 12 + rows_dev, 0:cols_dev] = s_up[4 * f : 4 * f + 4, :]
        else:
            field[f, 7:8, 0:cols_dev] = s_dn[8 + f : 9 + f, :]
            if f >= 4:
                field[f, 8 + rows_dev : 9 + rows_dev, 0:cols_dev] = s_up[4 + f : 5 + f, :]
        wide, narrow = (5, 4) if f < 2 else (1, 0 if f < 4 else 1)
        back = 5 if f < 2 else 5
        made = []
        for left, right, lane in sides:
            from_l = pltpu.roll(left, LANE - back - 8 * f, 1)
            from_r = pltpu.roll(right, (LANE - 8 * f) % LANE, 1)
            made.append(
                jnp.where(lane >= LANE - wide, from_l, jnp.where(lane < narrow, from_r, 0.0))
            )
        field[f, 8 : 8 + rows_dev, cols_dev:width] = made[0]
        row8 = lax.broadcasted_iota(jnp.int32, (8, LANE), 0)
        under = row8 >= 8 - wide
        over = row8 < narrow
        field[f, 0:8, cols_dev:width] = jnp.where(under, made[1], 0.0)
        field[f, 8 + rows_dev : tall, cols_dev:width] = jnp.where(over, made[2], 0.0)

    shape = (tall, width)
    row = lax.broadcasted_iota(jnp.int32, shape, 0) - 8 + lax.axis_index("new") * rows_dev
    lane = lax.broadcasted_iota(jnp.int32, shape, 1)
    col = jnp.where(lane < cols_dev + 64, lane, lane - width) + lax.axis_index("old") * cols_dev
    valid = (row >= 0) & (row < n_rows - 1) & (col >= 0) & (col < n_cols - 1)

    def from_left(x):
        return pltpu.roll(x, 1, 1)

    def from_right(x):
        return pltpu.roll(x, width - 1, 1)

    def from_below(x):
        return pltpu.roll(x, 1, 0)

    def from_above(x):
        return pltpu.roll(x, tall - 1, 0)

    area_low = jnp.where(valid, field[0], 0.0)
    area_up = jnp.where(valid, field[1], 0.0)
    field[2] = field[2] * area_low
    field[3] = field[3] * area_up
    lower, upper = area_low / 12.0, area_up / 12.0
    both = lower + upper
    lower_left, upper_below = from_left(lower), from_below(upper)
    weight = both + lower_left + upper_below + from_below(from_left(both))
    inv = jnp.where(weight > 0.0, 1.0 / (2.0 * weight), 0.0)
    inv_right = from_right(inv)
    east, north = lower + upper_below, upper + lower_left
    coef[0] = inv * (1.0 / 3.0)
    coef[1] = inv * north
    coef[2] = inv * from_below(north)
    coef[3] = from_left(inv * east)
    coef[4] = from_left(inv * both)
    coef[5] = inv_right * east
    coef[6] = inv_right * from_below(both)
    vol_low, vol_up = field[2], field[3]
    mass[...] = (
        vol_low
        + vol_up
        + from_left(vol_low)
        + from_below(vol_up)
        + from_below(from_left(vol_low + vol_up))
    ) * (1.0 / 3.0)
    mem[...] = jnp.zeros_like(mem)

    centre = 0.5 * (EIG_HIGH + EIG_LOW)
    half_width = 0.5 * (EIG_HIGH - EIG_LOW)
    ratio_eig = centre / half_width
    edge = lane_ids((channels, LANE))

    def widen(inner, left, right, place):
        left = pltpu.roll(left, lax.rem(2 * LANE - 4 - 8 * place, LANE), 1)
        right = pltpu.roll(right, lax.rem(LANE - 8 * place, LANE), 1)
        first = inner[:, 0:LANE] + jnp.where(edge == 0, left, 0.0)
        last = inner[:, cols_dev:width] + jnp.where(
            edge >= LANE - HALO, left, jnp.where(edge < HALO, right, 0.0)
        )
        return jnp.concatenate([first, inner[:, LANE:cols_dev], last], axis=1)

    def begin(e, rhs):
        scaled = rhs * coef[0, pl.ds(e + 4, 1), :]
        resid[e] = scaled
        dir_a[e] = scaled * (1.0 / centre)

    def own(i):
        i = jnp.int32(i)
        return widen(part[i], p_l[i // 16], p_r[i // 16], i % 16)

    def under(k):
        i = rows_dev - HALO + k
        tile = i // 16 - (rows_dev - 1) // 16
        return widen(p_dn[k], p_dl[tile], p_dr[tile], jnp.int32(i % 16))

    def over(k):
        return widen(p_up[k], p_ul[0], p_ur[0], jnp.int32(k))

    rhos = [1.0 / ratio_eig]
    for _ in range(ITERS):
        rhos.append(1.0 / (2.0 * ratio_eig - rhos[-1]))
    directions = [dir_a, dir_b, dir_c]

    def sweep_row(sweep, e):
        keep = rhos[sweep + 1] * rhos[sweep]
        gain = 2.0 * rhos[sweep + 1] / half_width
        final = sweep == ITERS - 1
        source = directions[sweep]
        k = [coef[c, pl.ds(e + 4, 1), :] for c in range(1, 7)]
        through = None
        for group in range(0, channels, 8):
            at = slice(group, group + 8)
            here, up, down = source[e, at, :], source[e + 1, at, :], source[e - 1, at, :]
            to_left = k[2] * here + k[3] * up
            to_right = k[4] * here + k[5] * down
            left = resid[e, at, :] - (
                here
                + k[0] * up
                + k[1] * down
                + pltpu.roll(to_left, width - 1, 1)
                + pltpu.roll(to_right, 1, 1)
            )
            new = keep * here + gain * left
            if final:
                summed = (dir_a[e, at, :] + dir_b[e, at, :]) + (here + new)
                total[e, at, :] = summed
                through = summed if through is None else through + summed
            else:
                resid[e, at, :] = left
                directions[sweep + 1][e, at, :] = new
        if final:
            through = through * (1.0 / POINTS)
            for at, value in enumerate((0, 1, 5, 7)):
                mem[at, pl.ds(e + 4, 1), :] = through[value : value + 1, :]

    for copy in copies[2:]:
        copy.wait()
    loads[-1].wait()

    def inner_row(i, _):
        begin(i + HALO, own(i))
        return 0

    lax.fori_loop(1, rows_dev, inner_row, 0)
    for sweep in range(ITERS):

        def inner_sweep(e, _, sweep=sweep):
            sweep_row(sweep, e)
            return 0

        lax.fori_loop(HALO + 2 + sweep, rows_dev + HALO - 1 - sweep, inner_sweep, 0)

    for copy in copies[:2]:
        copy.wait()
    for e in range(HALO):
        begin(e, under(e))
    begin(HALO, own(0) + under(HALO))
    begin(rows_dev + HALO, own(rows_dev) + over(0))
    for e in range(1, HALO):
        begin(rows_dev + HALO + e, over(e))
    for sweep in range(ITERS):
        def outer_sweep(k, _, sweep=sweep):
            low_end = HALO + 1
            sweep_row(
                sweep,
                jnp.where(k < low_end, 1 + sweep + k, rows_dev + HALO - 1 - sweep + k - low_end),
            )
            return 0

        lax.fori_loop(0, 2 * HALO + 1, outer_sweep, 0)

    saves = [pltpu.make_async_copy(total.at[pl.ds(HALO, rows_dev)], total_out, save_sem.at[0])]
    saves[0].start()

    anchor = [field[4 + c] for c in range(3)]
    beside = [from_right(x) for x in anchor]
    upward = [from_above(x) for x in anchor]
    across = [from_above(x) for x in beside]
    m_anchor = [mem[c] for c in range(4)]
    m_beside = [from_right(x) for x in m_anchor]
    m_upward = [from_above(x) for x in m_anchor]
    m_across = [from_above(x) for x in m_beside]
    third = 1.0 / 3.0
    m_low = [(a + b + x) * third for a, b, x in zip(m_anchor, m_beside, m_across)]
    m_up = [(a + x + u) * third for a, x, u in zip(m_anchor, m_across, m_upward)]
    low_x = [b - a for a, b in zip(anchor, beside)]
    low_y = [x - b for b, x in zip(beside, across)]
    up_x = [x - u for u, x in zip(upward, across)]
    up_y = [u - a for a, u in zip(anchor, upward)]
    low_x[0], up_x[0] = 1.0 + low_x[0], 1.0 + up_x[0]
    low_y[1], up_y[1] = 1.0 + low_y[1], 1.0 + up_y[1]
    piola_lx, piola_ly = first_piola(low_x, low_y, m_low)
    piola_ux, piola_uy = first_piola(up_x, up_y, m_up)
    vol_low, vol_up = field[2], field[3]
    node_mass = mass[8 : 8 + rows_dev, 0:cols_dev]
    for c in range(3):
        f_beside = -vol_low * (piola_lx[c] - piola_ly[c])
        f_across_low = -vol_low * piola_ly[c]
        f_across_up = -vol_up * piola_ux[c]
        f_upward = -vol_up * (piola_uy[c] - piola_ux[c])
        f_anchor = -(f_beside + f_across_low) - (f_across_up + f_upward)
        force = (
            f_anchor
            + from_left(f_beside)
            + from_below(f_upward)
            + from_below(from_left(f_across_low + f_across_up))
        )
        speed_up = force[8 : 8 + rows_dev, 0:cols_dev] / node_mass
        speed[c] = speed_up + GRAVITY if c == 2 else speed_up
    saves.append(pltpu.make_async_copy(speed, speed_out, save_sem.at[1]))
    saves[1].start()
    for save in saves:
        save.wait()


def sheet(part, cols_right, cols_left, fields, halo, n_rows, n_cols):
    channels, width = part.shape[1:]
    rows_dev, cols_dev = fields[0].shape[1:]
    tall, long = rows_dev + 16, rows_dev + 2 * HALO
    tiles = cols_right.shape[0]

    def scratch(*shape):
        return pltpu.VMEM(shape, jnp.float32)

    block = scratch(long, channels, width)
    part_halo = [(HALO + 1, channels, width), (HALO, channels, width)]
    part_halo += [(tiles, channels, LANE)] * 2 + [(2, channels, LANE)] * 2
    part_halo += [(1, channels, LANE)] * 2
    return pl.pallas_call(
        functools.partial(sheet_kernel, n_rows, n_cols),
        out_shape=(
            jax.ShapeDtypeStruct((rows_dev, channels, width), jnp.float32),
            jax.ShapeDtypeStruct((3, rows_dev, cols_dev), jnp.float32),
        ),
        in_specs=[HBM] * 14,
        out_specs=(HBM, HBM),
        scratch_shapes=[scratch(*shape) for shape in part_halo]
        + [scratch(*x.shape) for x in halo]
        + [
            scratch(*part.shape),
            block,
            block,
            block,
            block,
            block,
            scratch(7, tall, width),
            scratch(4, tall, width),
            scratch(tall, width),
            scratch(7, tall, width),
            scratch(3, rows_dev, cols_dev),
            pltpu.SemaphoreType.DMA((12,)),
            pltpu.SemaphoreType.DMA((2,)),
            pltpu.SemaphoreType.DMA((8,)),
            pltpu.SemaphoreType.DMA((8,)),
        ],
        compiler_params=pltpu.CompilerParams(
            vmem_limit_bytes=58 * MIB, collective_id=2, has_side_effects=True
        ),
        name="sheet",
    )(part, cols_right, cols_left, *fields, *halo)


def finish_kernel(total, speed_up, velocity, out, vel_out):
    rows, channels, _ = total.shape
    cols = out.shape[2]
    for channel in range(channels):
        out[channel] = total[:, channel, 0:cols]
    vel_out[...] = velocity[...] + TIME_STEP * speed_up[...]


def finish(total, speed_up, velocity):
    rows_dev, channels, width = total.shape
    cols_dev = velocity.shape[2]

    def plane(count):
        return pl.BlockSpec((count, 8, cols_dev), lambda i: (0, i, 0))

    return pl.pallas_call(
        finish_kernel,
        grid=(rows_dev // 8,),
        out_shape=(
            jax.ShapeDtypeStruct((channels, rows_dev, cols_dev), jnp.float32),
            jax.ShapeDtypeStruct(velocity.shape, jnp.float32),
        ),
        in_specs=[pl.BlockSpec((8, channels, width), lambda i: (i, 0, 0)), plane(3), plane(3)],
        out_specs=(plane(channels), plane(3)),
        compiler_params=pltpu.CompilerParams(vmem_limit_bytes=24 * MIB),
        name="finish",
    )(total, speed_up, velocity)


def local(
    old_values,
    pair_rows,
    pair_targets,
    pair_weights,
    pair_counts,
    cell_area,
    thickness,
    displacement,
    velocity,
):
    rows_dev, cols_dev = cell_area.shape[1:]
    n_old, n_new = lax.axis_size("old"), lax.axis_size("new")
    arrived, ids, halo = send(
        pair_counts,
        pair_rows,
        pair_targets,
        pair_weights,
        old_values,
        cell_area,
        thickness,
        displacement,
    )
    part, cols_right, cols_left = scatter(ids, arrived, rows_dev, cols_dev)
    fields = (cell_area, thickness, displacement)
    total, speed_up = sheet(
        part, cols_right, cols_left, fields, halo, n_new * rows_dev, n_old * cols_dev
    )
    return finish(total, speed_up, velocity)


def solution(mesh):
    return jax.shard_map(
        local,
        mesh=mesh,
        in_specs=(
            P(None, ("old", "new")),
            P(("old", "new"), None, None),
            P(("old", "new"), None, None),
            P(("old", "new"), None, None),
            P(("old", "new"), None),
            P(None, "new", "old"),
            P(None, "new", "old"),
            P(None, "new", "old"),
            P(None, "new", "old"),
        ),
        out_specs=(P(None, "new", "old"), P(None, "new", "old")),
        check_vma=False,
    )
```

```python
import functools

import jax
import jax.numpy as jnp
from jax import lax
from jax.experimental import pallas as pl
from jax.experimental.pallas import tpu as pltpu
from jax.sharding import PartitionSpec as P

POINTS = 4
COMP = 8
ITERS = 3
MU_BASE = 10.0
LAMBDA_BULK = 20.0
PRESTRESS = 4.0
TIME_STEP = 1.0
GRAVITY = -1.0
EIG_LOW = 0.5
EIG_HIGH = 2.0

LANE = 128
FRONT = 8
BATCH = 4
HALO = 4
STRIDE = 37
MESH = pl.DeviceIdType.MESH
MIB = 1024 * 1024

VMEM = pl.BlockSpec(memory_space=pltpu.VMEM)
SMEM = pl.BlockSpec(memory_space=pltpu.SMEM)
HBM = pl.BlockSpec(memory_space=pltpu.HBM)


def lane_ids(shape):
    return lax.broadcasted_iota(jnp.int32, shape, len(shape) - 1)


def neighbours():
    n_old, n_new = lax.axis_size("old"), lax.axis_size("new")
    old, new = lax.axis_index("old"), lax.axis_index("new")
    left, right = lax.rem(old + n_old - 1, n_old), lax.rem(old + 1, n_old)
    below, above = lax.rem(new + n_new - 1, n_new), lax.rem(new + 1, n_new)
    return [
        (old, above),
        (old, below),
        (right, new),
        (left, new),
        (right, above),
        (left, above),
        (right, below),
        (left, below),
    ]


def to_neighbours(sources, targets, send_sem, recv_sem):
    return [
        pltpu.make_async_remote_copy(
            src_ref=source,
            dst_ref=target,
            send_sem=send_sem.at[at],
            recv_sem=recv_sem.at[at],
            device_id=device,
            device_id_type=MESH,
        )
        for at, (source, target, device) in enumerate(zip(sources, targets, neighbours()))
    ]


def send_kernel(
    rows_dev,
    cols_dev,
    counts,
    rows_in,
    targets_in,
    weights_in,
    values_in,
    area,
    thick,
    shift_in,
    arrived,
    arrived_ids,
    s_dn,
    s_up,
    s_l,
    s_r,
    s_dl,
    s_dr,
    s_ul,
    s_ur,
    table,
    picked,
    ids,
    notes,
    weights_flat,
    targets,
    weights_raw,
    values,
    rim_low,
    rim_high,
    rim_left,
    rim_right,
    pack_up,
    pack_down,
    pack_right,
    pack_left,
    rows,
    weights,
    local_sem,
    pair_sem,
    near_send,
    near_recv,
):
    n_old, n_new = lax.axis_size("old"), lax.axis_size("new")
    old, new = lax.axis_index("old"), lax.axis_index("new")
    ranks, payload, _ = picked.shape
    slots = payload * 4
    width = cols_dev + LANE
    total = values.shape[1]
    me = old * n_new + new
    top, low = pl.ds(rows_dev - 8, 8), pl.ds(0, 8)
    near, far = pl.ds(0, LANE), pl.ds(cols_dev - LANE, LANE)

    loads = [
        (targets_in, targets),
        (weights_in, weights_raw),
        (values_in, values),
        (rows_in, rows),
    ]
    for source, at, count in ((area, 0, 2), (thick, 2, 2), (shift_in, 4, 3)):
        into = pl.ds(at, count)
        loads.append((source.at[:, top, :], rim_high.at[into]))
        loads.append((source.at[:, low, :], rim_low.at[into]))
        loads.append((source.at[:, :, far], rim_right.at[into]))
        loads.append((source.at[:, :, near], rim_left.at[into]))
    loads = [
        pltpu.make_async_copy(source, target, local_sem.at[at])
        for at, (source, target) in enumerate(loads)
    ]
    for load in loads:
        load.start()

    barrier = pltpu.get_barrier_semaphore()

    def greet(step, _):
        other = lax.rem(me + step, ranks)
        pl.semaphore_signal(
            barrier, inc=1, device_id=(other // n_new, other % n_new), device_id_type=MESH
        )
        return 0

    lax.fori_loop(1, ranks, greet, 0)

    slot = lane_ids((ranks, slots))
    owner = lax.broadcasted_iota(jnp.int32, (ranks, slots), 0)
    count = jnp.broadcast_to(counts[...].astype(jnp.float32), (ranks, ranks)).T.astype(jnp.int32)
    loads[0].wait()
    loads[1].wait()
    target = targets[0]
    cell, col = target // cols_dev, target % cols_dev
    outside = ((owner % n_new == n_new - 1) & (cell % rows_dev == rows_dev - 1)) | (
        (owner // n_new == n_old - 1) & (col == cols_dev - 1)
    )
    used = (slot < count) & jnp.logical_not(outside)
    weights_flat[...] = jnp.where(used, weights_raw[0], 0.0)
    load_weights = pltpu.make_async_copy(weights_flat, weights, local_sem.at[len(loads)])
    load_weights.start()
    where_to = jnp.where(used, FRONT + cell * width + col, FRONT + cols_dev + slot)
    clash = jnp.zeros((ranks, slots), jnp.int32)
    for gap in range(1, BATCH):
        same = (where_to == pltpu.roll(where_to, 4 * gap, 1)) & (slot % (4 * BATCH) >= 4 * gap)
        clash = clash | same.astype(jnp.int32)
    notes[:, 0:slots] = where_to
    notes[:, slots : slots + LANE] = jnp.broadcast_to(
        jnp.max(clash, axis=1, keepdims=True), (ranks, LANE)
    )

    unroll = 8
    loads[2].wait()

    def flip(step, _):
        for at in range(unroll):
            start = pl.multiple_of((step * unroll + at) * LANE, LANE)
            part = values[:, pl.ds(start, LANE)]
            table[pl.ds(start, LANE), :] = jnp.concatenate([part] * 4, axis=0).T
        return 0

    lax.fori_loop(0, total // (LANE * unroll), flip, 0)

    for load in loads[3:]:
        load.wait()
    pack_up[...] = jnp.zeros_like(pack_up)
    pack_down[...] = jnp.zeros_like(pack_down)
    lane = lane_ids((rows_dev, LANE))
    to_right = jnp.zeros((rows_dev, LANE), jnp.float32)
    to_left = jnp.zeros((rows_dev, LANE), jnp.float32)
    for f in range(7):
        if f < 2:
            pack_up[5 * f : 5 * f + 5, :] = rim_high[f, 3:8, :]
            pack_down[4 * f : 4 * f + 4, :] = rim_low[f, 0:4, :]
        else:
            pack_up[8 + f : 9 + f, :] = rim_high[f, 7:8, :]
            if f >= 4:
                pack_down[4 + f : 5 + f, :] = rim_low[f, 0:1, :]
        mine = lane // 8 == f
        to_right = jnp.where(mine, pltpu.roll(rim_right[f], 8 * f + 5, 1), to_right)
        to_left = jnp.where(mine, pltpu.roll(rim_left[f], 8 * f, 1), to_left)
    pack_right[...] = to_right
    pack_left[...] = to_left
    load_weights.wait()
    pl.semaphore_wait(barrier, ranks - 1)

    halo = to_neighbours(
        [
            pack_up,
            pack_down,
            pack_right,
            pack_left,
            pack_right.at[top],
            pack_left.at[top],
            pack_right.at[low],
            pack_left.at[low],
        ],
        [s_dn, s_up, s_l, s_r, s_dl, s_dr, s_ul, s_ur],
        near_send,
        near_recv,
    )
    for copy in halo:
        copy.start()

    lane = lane_ids((1, LANE))
    first, second, third = lane < 32, lane < 64, lane < 96

    def fill(owner):
        for row in range(payload):
            part = [
                table[pl.ds(rows[0, owner, row * 4 + g], 1), :] * weights[owner, row * 4 + g]
                for g in range(4)
            ]
            merged = jnp.where(
                first, part[0], jnp.where(second, part[1], jnp.where(third, part[2], part[3]))
            )
            picked[owner, pl.ds(row, 1), :] = merged
        ids[owner] = notes[pl.ds(owner, 1), :]

    def one_owner(step, _):
        shift = lax.rem(step * STRIDE, ranks)
        to_old = lax.rem(old + shift // n_new, n_old)
        to_new = lax.rem(new + shift % n_new, n_new)
        owner = to_old * n_new + to_new
        fill(owner)
        for at, (source, target) in enumerate(((picked, arrived), (ids, arrived_ids))):
            pltpu.make_async_remote_copy(
                src_ref=source.at[owner],
                dst_ref=target.at[me],
                send_sem=pair_sem.at[2 * at],
                recv_sem=pair_sem.at[2 * at + 1],
                device_id=(to_old, to_new),
                device_id_type=MESH,
            ).start()
        return 0

    lax.fori_loop(1, ranks, one_owner, 0)
    fill(me)
    for at, (source, target) in enumerate(((picked, arrived), (ids, arrived_ids))):
        pltpu.make_async_copy(source.at[me], target.at[me], pair_sem.at[2 * at + 1]).start()
    for copy in halo:
        copy.wait()
    for at, (source, target) in enumerate(((picked, arrived), (ids, arrived_ids))):
        rest = pl.ds(0, ranks - 1)
        pltpu.make_async_copy(source.at[rest], source.at[rest], pair_sem.at[2 * at]).wait()
        pltpu.make_async_copy(source, target, pair_sem.at[2 * at + 1]).wait()


def send(counts, rows, targets, weights, values, area, thick, shift):
    ranks, slots = rows.shape[1:]
    payload = slots // 4
    rows_dev, cols_dev = area.shape[1:]
    halo = [(16, cols_dev)] * 2 + [(rows_dev, LANE)] * 2 + [(8, LANE)] * 4
    shapes = [jax.ShapeDtypeStruct(shape, jnp.float32) for shape in [(ranks, payload, LANE)] + halo]
    shapes.insert(1, jax.ShapeDtypeStruct((ranks, 1, slots + LANE), jnp.int32))

    def scratch(*shape):
        return pltpu.VMEM(shape, jnp.float32)

    result = pl.pallas_call(
        functools.partial(send_kernel, rows_dev, cols_dev),
        out_shape=tuple(shapes),
        in_specs=[VMEM] + [HBM] * 7,
        out_specs=(HBM,) * len(shapes),
        scratch_shapes=[
            scratch(values.shape[1], LANE),
            scratch(ranks, payload, LANE),
            pltpu.VMEM((ranks, 1, slots + LANE), jnp.int32),
            pltpu.VMEM((ranks, slots + LANE), jnp.int32),
            scratch(ranks, slots),
            pltpu.VMEM(targets.shape, jnp.int32),
            scratch(*weights.shape),
            scratch(*values.shape),
            scratch(7, 8, cols_dev),
            scratch(7, 8, cols_dev),
            scratch(7, rows_dev, LANE),
            scratch(7, rows_dev, LANE),
            scratch(16, cols_dev),
            scratch(16, cols_dev),
            scratch(rows_dev, LANE),
            scratch(rows_dev, LANE),
            pltpu.SMEM(rows.shape, jnp.int32),
            pltpu.SMEM((ranks, slots), jnp.float32),
            pltpu.SemaphoreType.DMA((17,)),
            pltpu.SemaphoreType.DMA((4,)),
            pltpu.SemaphoreType.DMA((8,)),
            pltpu.SemaphoreType.DMA((8,)),
        ],
        compiler_params=pltpu.CompilerParams(
            vmem_limit_bytes=60 * MIB, collective_id=1, has_side_effects=True
        ),
        name="send",
    )(counts, rows, targets, weights, values, area, thick, shift)
    return result[0], result[1], result[2:]


def scatter_kernel(rows_dev, cols_dev, ids_in, data_in, part, cols_right, cols_left, acc, carry, data, ids, sem):
    width = cols_dev + LANE
    ranks, payload, _ = data.shape
    size = acc.shape[0]
    chunk = width // 8
    load_ids = pltpu.make_async_copy(ids_in, ids, sem.at[0])
    load_data = pltpu.make_async_copy(data_in, data, sem.at[1])
    load_ids.start()
    load_data.start()
    zeros = jnp.zeros((chunk, LANE), jnp.float32)
    acc[pl.ds(0, FRONT), :] = jnp.zeros((FRONT, LANE), jnp.float32)
    carry[...] = jnp.zeros_like(carry)

    def clear(step, _):
        acc[pl.ds(pl.multiple_of(FRONT + step * chunk, 8), chunk), :] = zeros
        return 0

    lax.fori_loop(0, (size - FRONT) // chunk, clear, 0)
    load_ids.wait()
    load_data.wait()

    lane = lane_ids((1, LANE))
    masks = [(lane >= 32 * g) & (lane < 32 * g + 32) for g in range(4)]

    def add_rows(source, first, count):
        slots = [(r, g) for r in range(count) for g in range(4)]
        where_to = [ids[source, 0, (first + r) * 4 + g] for r, g in slots]
        new = [data[source, pl.ds(first + r, 1), :] for r in range(count)]
        old = [acc[pl.ds(row, 1), :] for row in where_to]
        for (r, g), row, have in zip(slots, where_to, old):
            pltpu.store(acc.at[pl.ds(row, 1), :], have + new[r], mask=masks[g])

    def one_source(source, _):
        clash = ids[source, 0, payload * 4]

        @pl.when(clash == 0)
        def _():
            for first in range(0, payload, BATCH):
                add_rows(source, first, BATCH)

        @pl.when(clash != 0)
        def _():
            def slow(row, _):
                add_rows(source, row, 1)
                return 0

            lax.fori_loop(0, payload, slow, 0)

        return 0

    lax.fori_loop(0, ranks, one_source, 0)

    def fold(total):
        flipped = total.T
        return (flipped[0:32] + flipped[32:64]) + (flipped[64:96] + flipped[96:128])

    upper_base = rows_dev * width
    lane = lane_ids((part.shape[1], LANE))

    def pack(i, own_near, own_far, ghost):
        tile, place = i // 16, i % 16
        mine = lane // 8 == place
        ends = pltpu.roll(jnp.where(lane == 0, ghost, own_far), 8 * place + 4, 1)
        cols_right[tile] = jnp.where(mine, ends, cols_right[tile])
        cols_left[tile] = jnp.where(mine, pltpu.roll(own_near, 8 * place, 1), cols_left[tile])

    cols_right[...] = jnp.zeros_like(cols_right)
    cols_left[...] = jnp.zeros_like(cols_left)
    tiles = width // LANE

    def one_row(i, _):
        done = []
        for tile in range(tiles):
            span = slice(tile * LANE, (tile + 1) * LANE)
            base = pl.multiple_of(i * width + tile * LANE + FRONT, 8)
            lower = acc[pl.ds(base, LANE), :]
            upper = acc[pl.ds(pl.multiple_of(base + upper_base, 8), LANE), :]
            shared = upper + acc[pl.ds(base - 1, LANE), :]
            summed = lower + shared + carry[span, :]
            carry[span, :] = shared + acc[pl.ds(base + upper_base - 1, LANE), :]
            folded = fold(summed)
            part[i, :, span] = folded
            done.append(folded)
        pack(i, done[0], done[-2], done[-1])
        return 0

    lax.fori_loop(0, rows_dev, one_row, 0)
    done = [fold(carry[tile * LANE : (tile + 1) * LANE, :]) for tile in range(tiles)]
    for tile in range(tiles):
        part[rows_dev, :, tile * LANE : (tile + 1) * LANE] = done[tile]
    pack(rows_dev, done[0], done[-2], done[-1])


def scatter(ids, data, rows_dev, cols_dev):
    channels = LANE // 4
    width = cols_dev + LANE
    return pl.pallas_call(
        functools.partial(scatter_kernel, rows_dev, cols_dev),
        out_shape=(
            jax.ShapeDtypeStruct((rows_dev + 1, channels, width), jnp.float32),
            jax.ShapeDtypeStruct((rows_dev // 16 + 1, channels, LANE), jnp.float32),
            jax.ShapeDtypeStruct((rows_dev // 16 + 1, channels, LANE), jnp.float32),
        ),
        in_specs=[HBM, HBM],
        out_specs=(VMEM, VMEM, VMEM),
        scratch_shapes=[
            pltpu.VMEM((FRONT + 2 * rows_dev * width, LANE), jnp.float32),
            pltpu.VMEM((width, LANE), jnp.float32),
            pltpu.VMEM(data.shape, jnp.float32),
            pltpu.SMEM(ids.shape, jnp.int32),
            pltpu.SemaphoreType.DMA((2,)),
        ],
        compiler_params=pltpu.CompilerParams(vmem_limit_bytes=60 * MIB),
        name="scatter",
    )(ids, data)


def first_piola(stretch_x, stretch_y, fields):
    gram_xx = sum(x * x for x in stretch_x)
    gram_xy = sum(x * y for x, y in zip(stretch_x, stretch_y))
    gram_yy = sum(y * y for y in stretch_y)
    determinant = gram_xx * gram_yy - gram_xy * gram_xy
    inverse = 1.0 / determinant
    inv_xx = gram_yy * inverse
    inv_xy = -gram_xy * inverse
    inv_yy = gram_xx * inverse
    shear_mod = MU_BASE * (1.5 + jnp.tanh(fields[3]))
    bulk = LAMBDA_BULK * 0.5 * jnp.log(determinant)
    piola_x, piola_y = [], []
    for along_x, along_y in zip(stretch_x, stretch_y):
        push_x = along_x * inv_xx + along_y * inv_xy
        push_y = along_x * inv_xy + along_y * inv_yy
        piola_x.append(
            shear_mod * (along_x - push_x)
            + bulk * push_x
            + PRESTRESS * (along_x * fields[0] + along_y * fields[2])
        )
        piola_y.append(
            shear_mod * (along_y - push_y)
            + bulk * push_y
            + PRESTRESS * (along_x * fields[2] + along_y * fields[1])
        )
    return piola_x, piola_y


def sheet_kernel(n_rows, n_cols, *refs):
    part_in, cols_right, cols_left, area_in, thick_in, shift_in = refs[:6]
    s_in = refs[6:14]
    total_out, speed_out = refs[14:16]
    p_halo, s_halo, refs = refs[16:24], refs[24:32], refs[32:]
    part, resid, dir_a, dir_b, dir_c, total, field, mem, mass, coef, speed = refs[:11]
    load_sem, save_sem, send_sem, recv_sem = refs[11:]
    p_dn, p_up, p_l, p_r, p_dl, p_dr, p_ul, p_ur = p_halo
    s_dn, s_up, s_l, s_r, s_dl, s_dr, s_ul, s_ur = s_halo
    rows_dev, cols_dev = area_in.shape[1:]
    channels, width = part.shape[1:]
    tall = rows_dev + 16
    middle, main = pl.ds(8, rows_dev), pl.ds(0, cols_dev)

    barrier = pltpu.get_barrier_semaphore()
    for device in neighbours():
        pl.semaphore_signal(barrier, inc=1, device_id=device, device_id_type=MESH)

    field[:, 0:8, :] = jnp.zeros((7, 8, width), jnp.float32)
    field[:, 8 + rows_dev : tall, :] = jnp.zeros((7, 8, width), jnp.float32)
    loads = [
        (area_in, field.at[pl.ds(0, 2), middle, main]),
        (thick_in, field.at[pl.ds(2, 2), middle, main]),
        (shift_in, field.at[pl.ds(4, 3), middle, main]),
    ] + list(zip(s_in, s_halo))
    loads.append((part_in, part))
    loads = [
        pltpu.make_async_copy(source, target, load_sem.at[at])
        for at, (source, target) in enumerate(loads)
    ]
    for load in loads:
        load.start()

    high, low = pl.ds(part_in.shape[0] - HALO - 1, HALO + 1), pl.ds(0, HALO)
    tiles_high, tiles_low = pl.ds((rows_dev - 1) // 16, 2), pl.ds(0, 1)
    pl.semaphore_wait(barrier, 8)
    copies = to_neighbours(
        [
            part_in.at[high],
            part_in.at[low],
            cols_right,
            cols_left,
            cols_right.at[tiles_high],
            cols_left.at[tiles_high],
            cols_right.at[tiles_low],
            cols_left.at[tiles_low],
        ],
        p_halo,
        send_sem,
        recv_sem,
    )
    for copy in copies[2:] + copies[:2]:
        copy.start()

    for load in loads[:-1]:
        load.wait()
    sides = []
    for left, right, size in ((s_l, s_r, rows_dev), (s_dl, s_dr, 8), (s_ul, s_ur, 8)):
        sides.append((left[...], right[...], lane_ids((size, LANE))))
    for f in range(7):
        if f < 2:
            field[f, 3:8, 0:cols_dev] = s_dn[5 * f : 5 * f + 5, :]
            field[f, 8 + rows_dev : 12 + rows_dev, 0:cols_dev] = s_up[4 * f : 4 * f + 4, :]
        else:
            field[f, 7:8, 0:cols_dev] = s_dn[8 + f : 9 + f, :]
            if f >= 4:
                field[f, 8 + rows_dev : 9 + rows_dev, 0:cols_dev] = s_up[4 + f : 5 + f, :]
        wide, narrow = (5, 4) if f < 2 else (1, 0 if f < 4 else 1)
        back = 5 if f < 2 else 5
        made = []
        for left, right, lane in sides:
            from_l = pltpu.roll(left, LANE - back - 8 * f, 1)
            from_r = pltpu.roll(right, (LANE - 8 * f) % LANE, 1)
            made.append(
                jnp.where(lane >= LANE - wide, from_l, jnp.where(lane < narrow, from_r, 0.0))
            )
        field[f, 8 : 8 + rows_dev, cols_dev:width] = made[0]
        row8 = lax.broadcasted_iota(jnp.int32, (8, LANE), 0)
        under = row8 >= 8 - wide
        over = row8 < narrow
        field[f, 0:8, cols_dev:width] = jnp.where(under, made[1], 0.0)
        field[f, 8 + rows_dev : tall, cols_dev:width] = jnp.where(over, made[2], 0.0)

    shape = (tall, width)
    row = lax.broadcasted_iota(jnp.int32, shape, 0) - 8 + lax.axis_index("new") * rows_dev
    lane = lax.broadcasted_iota(jnp.int32, shape, 1)
    col = jnp.where(lane < cols_dev + 64, lane, lane - width) + lax.axis_index("old") * cols_dev
    valid = (row >= 0) & (row < n_rows - 1) & (col >= 0) & (col < n_cols - 1)

    def from_left(x):
        return pltpu.roll(x, 1, 1)

    def from_right(x):
        return pltpu.roll(x, width - 1, 1)

    def from_below(x):
        return pltpu.roll(x, 1, 0)

    def from_above(x):
        return pltpu.roll(x, tall - 1, 0)

    area_low = jnp.where(valid, field[0], 0.0)
    area_up = jnp.where(valid, field[1], 0.0)
    field[2] = field[2] * area_low
    field[3] = field[3] * area_up
    lower, upper = area_low / 12.0, area_up / 12.0
    both = lower + upper
    lower_left, upper_below = from_left(lower), from_below(upper)
    weight = both + lower_left + upper_below + from_below(from_left(both))
    inv = jnp.where(weight > 0.0, 1.0 / (2.0 * weight), 0.0)
    inv_right = from_right(inv)
    east, north = lower + upper_below, upper + lower_left
    coef[0] = inv * (1.0 / 3.0)
    coef[1] = inv * north
    coef[2] = inv * from_below(north)
    coef[3] = from_left(inv * east)
    coef[4] = from_left(inv * both)
    coef[5] = inv_right * east
    coef[6] = inv_right * from_below(both)
    vol_low, vol_up = field[2], field[3]
    mass[...] = (
        vol_low
        + vol_up
        + from_left(vol_low)
        + from_below(vol_up)
        + from_below(from_left(vol_low + vol_up))
    ) * (1.0 / 3.0)
    mem[...] = jnp.zeros_like(mem)

    centre = 0.5 * (EIG_HIGH + EIG_LOW)
    half_width = 0.5 * (EIG_HIGH - EIG_LOW)
    ratio_eig = centre / half_width
    edge = lane_ids((channels, LANE))

    def widen(inner, left, right, place):
        left = pltpu.roll(left, lax.rem(2 * LANE - 4 - 8 * place, LANE), 1)
        right = pltpu.roll(right, lax.rem(LANE - 8 * place, LANE), 1)
        first = inner[:, 0:LANE] + jnp.where(edge == 0, left, 0.0)
        last = inner[:, cols_dev:width] + jnp.where(
            edge >= LANE - HALO, left, jnp.where(edge < HALO, right, 0.0)
        )
        return jnp.concatenate([first, inner[:, LANE:cols_dev], last], axis=1)

    def begin(e, rhs):
        scaled = rhs * coef[0, pl.ds(e + 4, 1), :]
        resid[e] = scaled
        dir_a[e] = scaled * (1.0 / centre)

    def own(i):
        i = jnp.int32(i)
        return widen(part[i], p_l[i // 16], p_r[i // 16], i % 16)

    def under(k):
        i = rows_dev - HALO + k
        tile = i // 16 - (rows_dev - 1) // 16
        return widen(p_dn[k], p_dl[tile], p_dr[tile], jnp.int32(i % 16))

    def over(k):
        return widen(p_up[k], p_ul[0], p_ur[0], jnp.int32(k))

    rhos = [1.0 / ratio_eig]
    for _ in range(ITERS):
        rhos.append(1.0 / (2.0 * ratio_eig - rhos[-1]))
    directions = [dir_a, dir_b, dir_c]

    def sweep_row(sweep, e):
        keep = rhos[sweep + 1] * rhos[sweep]
        gain = 2.0 * rhos[sweep + 1] / half_width
        final = sweep == ITERS - 1
        source = directions[sweep]
        k = [coef[c, pl.ds(e + 4, 1), :] for c in range(1, 7)]
        through = None
        for group in range(0, channels, 8):
            at = slice(group, group + 8)
            here, up, down = source[e, at, :], source[e + 1, at, :], source[e - 1, at, :]
            to_left = k[2] * here + k[3] * up
            to_right = k[4] * here + k[5] * down
            left = resid[e, at, :] - (
                here
                + k[0] * up
                + k[1] * down
                + pltpu.roll(to_left, width - 1, 1)
                + pltpu.roll(to_right, 1, 1)
            )
            new = keep * here + gain * left
            if final:
                summed = (dir_a[e, at, :] + dir_b[e, at, :]) + (here + new)
                total[e, at, :] = summed
                through = summed if through is None else through + summed
            else:
                resid[e, at, :] = left
                directions[sweep + 1][e, at, :] = new
        if final:
            through = through * (1.0 / POINTS)
            for at, value in enumerate((0, 1, 5, 7)):
                mem[at, pl.ds(e + 4, 1), :] = through[value : value + 1, :]

    for copy in copies[2:]:
        copy.wait()
    loads[-1].wait()

    def inner_row(i, _):
        begin(i + HALO, own(i))
        return 0

    lax.fori_loop(1, rows_dev, inner_row, 0)
    for sweep in range(ITERS):

        def inner_sweep(e, _, sweep=sweep):
            sweep_row(sweep, e)
            return 0

        lax.fori_loop(HALO + 2 + sweep, rows_dev + HALO - 1 - sweep, inner_sweep, 0)

    for copy in copies[:2]:
        copy.wait()
    for e in range(HALO):
        begin(e, under(e))
    begin(HALO, own(0) + under(HALO))
    begin(rows_dev + HALO, own(rows_dev) + over(0))
    for e in range(1, HALO):
        begin(rows_dev + HALO + e, over(e))
    for sweep in range(ITERS):
        def outer_sweep(k, _, sweep=sweep):
            low_end = HALO + 1
            sweep_row(
                sweep,
                jnp.where(k < low_end, 1 + sweep + k, rows_dev + HALO - 1 - sweep + k - low_end),
            )
            return 0

        lax.fori_loop(0, 2 * HALO + 1, outer_sweep, 0)

    saves = [pltpu.make_async_copy(total.at[pl.ds(HALO, rows_dev)], total_out, save_sem.at[0])]
    saves[0].start()

    anchor = [field[4 + c] for c in range(3)]
    beside = [from_right(x) for x in anchor]
    upward = [from_above(x) for x in anchor]
    across = [from_above(x) for x in beside]
    m_anchor = [mem[c] for c in range(4)]
    m_beside = [from_right(x) for x in m_anchor]
    m_upward = [from_above(x) for x in m_anchor]
    m_across = [from_above(x) for x in m_beside]
    third = 1.0 / 3.0
    m_low = [(a + b + x) * third for a, b, x in zip(m_anchor, m_beside, m_across)]
    m_up = [(a + x + u) * third for a, x, u in zip(m_anchor, m_across, m_upward)]
    low_x = [b - a for a, b in zip(anchor, beside)]
    low_y = [x - b for b, x in zip(beside, across)]
    up_x = [x - u for u, x in zip(upward, across)]
    up_y = [u - a for a, u in zip(anchor, upward)]
    low_x[0], up_x[0] = 1.0 + low_x[0], 1.0 + up_x[0]
    low_y[1], up_y[1] = 1.0 + low_y[1], 1.0 + up_y[1]
    piola_lx, piola_ly = first_piola(low_x, low_y, m_low)
    piola_ux, piola_uy = first_piola(up_x, up_y, m_up)
    vol_low, vol_up = field[2], field[3]
    node_mass = mass[8 : 8 + rows_dev, 0:cols_dev]
    for c in range(3):
        f_beside = -vol_low * (piola_lx[c] - piola_ly[c])
        f_across_low = -vol_low * piola_ly[c]
        f_across_up = -vol_up * piola_ux[c]
        f_upward = -vol_up * (piola_uy[c] - piola_ux[c])
        f_anchor = -(f_beside + f_across_low) - (f_across_up + f_upward)
        force = (
            f_anchor
            + from_left(f_beside)
            + from_below(f_upward)
            + from_below(from_left(f_across_low + f_across_up))
        )
        speed_up = force[8 : 8 + rows_dev, 0:cols_dev] / node_mass
        speed[c] = speed_up + GRAVITY if c == 2 else speed_up
    saves.append(pltpu.make_async_copy(speed, speed_out, save_sem.at[1]))
    saves[1].start()
    for save in saves:
        save.wait()


def sheet(part, cols_right, cols_left, fields, halo, n_rows, n_cols):
    channels, width = part.shape[1:]
    rows_dev, cols_dev = fields[0].shape[1:]
    tall, long = rows_dev + 16, rows_dev + 2 * HALO
    tiles = cols_right.shape[0]

    def scratch(*shape):
        return pltpu.VMEM(shape, jnp.float32)

    block = scratch(long, channels, width)
    part_halo = [(HALO + 1, channels, width), (HALO, channels, width)]
    part_halo += [(tiles, channels, LANE)] * 2 + [(2, channels, LANE)] * 2
    part_halo += [(1, channels, LANE)] * 2
    return pl.pallas_call(
        functools.partial(sheet_kernel, n_rows, n_cols),
        out_shape=(
            jax.ShapeDtypeStruct((rows_dev, channels, width), jnp.float32),
            jax.ShapeDtypeStruct((3, rows_dev, cols_dev), jnp.float32),
        ),
        in_specs=[HBM] * 14,
        out_specs=(HBM, HBM),
        scratch_shapes=[scratch(*shape) for shape in part_halo]
        + [scratch(*x.shape) for x in halo]
        + [
            scratch(*part.shape),
            block,
            block,
            block,
            block,
            block,
            scratch(7, tall, width),
            scratch(4, tall, width),
            scratch(tall, width),
            scratch(7, tall, width),
            scratch(3, rows_dev, cols_dev),
            pltpu.SemaphoreType.DMA((12,)),
            pltpu.SemaphoreType.DMA((2,)),
            pltpu.SemaphoreType.DMA((8,)),
            pltpu.SemaphoreType.DMA((8,)),
        ],
        compiler_params=pltpu.CompilerParams(
            vmem_limit_bytes=60 * MIB, collective_id=2, has_side_effects=True
        ),
        name="sheet",
    )(part, cols_right, cols_left, *fields, *halo)


def finish_kernel(total, speed_up, velocity, out, vel_out):
    rows, channels, _ = total.shape
    cols = out.shape[2]
    for channel in range(channels):
        out[channel] = total[:, channel, 0:cols]
    vel_out[...] = velocity[...] + TIME_STEP * speed_up[...]


def finish(total, speed_up, velocity):
    rows_dev, channels, width = total.shape
    cols_dev = velocity.shape[2]

    def plane(count):
        return pl.BlockSpec((count, 8, cols_dev), lambda i: (0, i, 0))

    return pl.pallas_call(
        finish_kernel,
        grid=(rows_dev // 8,),
        out_shape=(
            jax.ShapeDtypeStruct((channels, rows_dev, cols_dev), jnp.float32),
            jax.ShapeDtypeStruct(velocity.shape, jnp.float32),
        ),
        in_specs=[pl.BlockSpec((8, channels, width), lambda i: (i, 0, 0)), plane(3), plane(3)],
        out_specs=(plane(channels), plane(3)),
        compiler_params=pltpu.CompilerParams(vmem_limit_bytes=60 * MIB),
        name="finish",
    )(total, speed_up, velocity)


def local(
    old_values,
    pair_rows,
    pair_targets,
    pair_weights,
    pair_counts,
    cell_area,
    thickness,
    displacement,
    velocity,
):
    rows_dev, cols_dev = cell_area.shape[1:]
    n_old, n_new = lax.axis_size("old"), lax.axis_size("new")
    arrived, ids, halo = send(
        pair_counts,
        pair_rows,
        pair_targets,
        pair_weights,
        old_values,
        cell_area,
        thickness,
        displacement,
    )
    part, cols_right, cols_left = scatter(ids, arrived, rows_dev, cols_dev)
    fields = (cell_area, thickness, displacement)
    total, speed_up = sheet(
        part, cols_right, cols_left, fields, halo, n_new * rows_dev, n_old * cols_dev
    )
    return finish(total, speed_up, velocity)


def solution(mesh):
    return jax.shard_map(
        local,
        mesh=mesh,
        in_specs=(
            P(None, ("old", "new")),
            P(("old", "new"), None, None),
            P(("old", "new"), None, None),
            P(("old", "new"), None, None),
            P(("old", "new"), None),
            P(None, "new", "old"),
            P(None, "new", "old"),
            P(None, "new", "old"),
            P(None, "new", "old"),
        ),
        out_specs=(P(None, "new", "old"), P(None, "new", "old")),
        check_vma=False,
    )
```

```python
import functools

import jax
import jax.numpy as jnp
from jax import lax
from jax.experimental import pallas as pl
from jax.experimental.pallas import tpu as pltpu
from jax.sharding import PartitionSpec as P

POINTS = 4
COMP = 8
ITERS = 3
MU_BASE = 10.0
LAMBDA_BULK = 20.0
PRESTRESS = 4.0
TIME_STEP = 1.0
GRAVITY = -1.0
EIG_LOW = 0.5
EIG_HIGH = 2.0

LANE = 128
FRONT = 8
BATCH = 4
HALO = 4
STRIDE = 37
MESH = pl.DeviceIdType.MESH
MIB = 1024 * 1024

VMEM = pl.BlockSpec(memory_space=pltpu.VMEM)
SMEM = pl.BlockSpec(memory_space=pltpu.SMEM)
HBM = pl.BlockSpec(memory_space=pltpu.HBM)


def lane_ids(shape):
    return lax.broadcasted_iota(jnp.int32, shape, len(shape) - 1)


def neighbours():
    n_old, n_new = lax.axis_size("old"), lax.axis_size("new")
    old, new = lax.axis_index("old"), lax.axis_index("new")
    left, right = lax.rem(old + n_old - 1, n_old), lax.rem(old + 1, n_old)
    below, above = lax.rem(new + n_new - 1, n_new), lax.rem(new + 1, n_new)
    return [
        (old, above),
        (old, below),
        (right, new),
        (left, new),
        (right, above),
        (left, above),
        (right, below),
        (left, below),
    ]


def to_neighbours(sources, targets, send_sem, recv_sem):
    return [
        pltpu.make_async_remote_copy(
            src_ref=source,
            dst_ref=target,
            send_sem=send_sem.at[at],
            recv_sem=recv_sem.at[at],
            device_id=device,
            device_id_type=MESH,
        )
        for at, (source, target, device) in enumerate(zip(sources, targets, neighbours()))
    ]


def send_kernel(
    rows_dev,
    cols_dev,
    counts,
    rows_in,
    targets_in,
    weights_in,
    values_in,
    area,
    thick,
    shift_in,
    arrived,
    arrived_ids,
    s_dn,
    s_up,
    s_l,
    s_r,
    s_dl,
    s_dr,
    s_ul,
    s_ur,
    acc,
    table,
    picked,
    ids,
    notes,
    weights_flat,
    targets,
    weights_raw,
    values,
    rim_low,
    rim_high,
    rim_left,
    rim_right,
    pack_up,
    pack_down,
    pack_right,
    pack_left,
    rows,
    weights,
    local_sem,
    pair_sem,
    near_send,
    near_recv,
):
    n_old, n_new = lax.axis_size("old"), lax.axis_size("new")
    old, new = lax.axis_index("old"), lax.axis_index("new")
    ranks, payload, _ = picked.shape
    slots = payload * 4
    width = cols_dev + LANE
    total = values.shape[1]
    me = old * n_new + new
    top, low = pl.ds(rows_dev - 8, 8), pl.ds(0, 8)
    near, far = pl.ds(0, LANE), pl.ds(cols_dev - LANE, LANE)

    loads = [
        (targets_in, targets),
        (weights_in, weights_raw),
        (values_in, values),
        (rows_in, rows),
    ]
    for source, at, count in ((area, 0, 2), (thick, 2, 2), (shift_in, 4, 3)):
        into = pl.ds(at, count)
        loads.append((source.at[:, top, :], rim_high.at[into]))
        loads.append((source.at[:, low, :], rim_low.at[into]))
        loads.append((source.at[:, :, far], rim_right.at[into]))
        loads.append((source.at[:, :, near], rim_left.at[into]))
    loads = [
        pltpu.make_async_copy(source, target, local_sem.at[at])
        for at, (source, target) in enumerate(loads)
    ]
    for load in loads:
        load.start()

    barrier = pltpu.get_barrier_semaphore()

    def greet(step, _):
        other = lax.rem(me + step, ranks)
        pl.semaphore_signal(
            barrier, inc=1, device_id=(other // n_new, other % n_new), device_id_type=MESH
        )
        return 0

    lax.fori_loop(1, ranks, greet, 0)

    slot = lane_ids((ranks, slots))
    owner = lax.broadcasted_iota(jnp.int32, (ranks, slots), 0)
    count = jnp.broadcast_to(counts[...].astype(jnp.float32), (ranks, ranks)).T.astype(jnp.int32)
    loads[0].wait()
    loads[1].wait()
    target = targets[0]
    cell, col = target // cols_dev, target % cols_dev
    outside = ((owner % n_new == n_new - 1) & (cell % rows_dev == rows_dev - 1)) | (
        (owner // n_new == n_old - 1) & (col == cols_dev - 1)
    )
    used = (slot < count) & jnp.logical_not(outside)
    weights_flat[...] = jnp.where(used, weights_raw[0], 0.0)
    load_weights = pltpu.make_async_copy(weights_flat, weights, local_sem.at[len(loads)])
    load_weights.start()
    where_to = jnp.where(used, FRONT + cell * width + col, FRONT + cols_dev + slot)
    clash = jnp.zeros((ranks, slots), jnp.int32)
    for gap in range(1, BATCH):
        same = (where_to == pltpu.roll(where_to, 4 * gap, 1)) & (slot % (4 * BATCH) >= 4 * gap)
        clash = clash | same.astype(jnp.int32)
    notes[:, 0:slots] = where_to
    notes[:, slots : slots + LANE] = jnp.broadcast_to(
        jnp.max(clash, axis=1, keepdims=True), (ranks, LANE)
    )

    unroll = 8
    loads[2].wait()

    def flip(step, _):
        for at in range(unroll):
            start = pl.multiple_of((step * unroll + at) * LANE, LANE)
            part = values[:, pl.ds(start, LANE)]
            table[pl.ds(start, LANE), :] = jnp.concatenate([part] * 4, axis=0).T
        return 0

    lax.fori_loop(0, total // (LANE * unroll), flip, 0)

    for load in loads[3:]:
        load.wait()
    pack_up[...] = jnp.zeros_like(pack_up)
    pack_down[...] = jnp.zeros_like(pack_down)
    lane = lane_ids((rows_dev, LANE))
    to_right = jnp.zeros((rows_dev, LANE), jnp.float32)
    to_left = jnp.zeros((rows_dev, LANE), jnp.float32)
    for f in range(7):
        if f < 2:
            pack_up[5 * f : 5 * f + 5, :] = rim_high[f, 3:8, :]
            pack_down[4 * f : 4 * f + 4, :] = rim_low[f, 0:4, :]
        else:
            pack_up[8 + f : 9 + f, :] = rim_high[f, 7:8, :]
            if f >= 4:
                pack_down[4 + f : 5 + f, :] = rim_low[f, 0:1, :]
        mine = lane // 8 == f
        to_right = jnp.where(mine, pltpu.roll(rim_right[f], 8 * f + 5, 1), to_right)
        to_left = jnp.where(mine, pltpu.roll(rim_left[f], 8 * f, 1), to_left)
    pack_right[...] = to_right
    pack_left[...] = to_left
    load_weights.wait()
    pl.semaphore_wait(barrier, ranks - 1)

    halo = to_neighbours(
        [
            pack_up,
            pack_down,
            pack_right,
            pack_left,
            pack_right.at[top],
            pack_left.at[top],
            pack_right.at[low],
            pack_left.at[low],
        ],
        [s_dn, s_up, s_l, s_r, s_dl, s_dr, s_ul, s_ur],
        near_send,
        near_recv,
    )
    for copy in halo:
        copy.start()

    lane = lane_ids((1, LANE))
    first, second, third = lane < 32, lane < 64, lane < 96

    def fill(owner):
        for row in range(payload):
            part = [
                table[pl.ds(rows[0, owner, row * 4 + g], 1), :] * weights[owner, row * 4 + g]
                for g in range(4)
            ]
            merged = jnp.where(
                first, part[0], jnp.where(second, part[1], jnp.where(third, part[2], part[3]))
            )
            picked[owner, pl.ds(row, 1), :] = merged
        ids[owner] = notes[pl.ds(owner, 1), :]

    chunk = (acc.shape[0] - FRONT) // ranks

    def clear(step):
        start = pl.multiple_of(FRONT + step * chunk, 8)
        acc[pl.ds(start, chunk), :] = jnp.zeros((chunk, LANE), jnp.float32)

    acc[pl.ds(0, FRONT), :] = jnp.zeros((FRONT, LANE), jnp.float32)
    clear(0)

    def one_owner(step, _):
        shift = lax.rem(step * STRIDE, ranks)
        to_old = lax.rem(old + shift // n_new, n_old)
        to_new = lax.rem(new + shift % n_new, n_new)
        owner = to_old * n_new + to_new
        fill(owner)
        clear(step)
        for at, (source, target) in enumerate(((picked, arrived), (ids, arrived_ids))):
            pltpu.make_async_remote_copy(
                src_ref=source.at[owner],
                dst_ref=target.at[me],
                send_sem=pair_sem.at[2 * at],
                recv_sem=pair_sem.at[2 * at + 1],
                device_id=(to_old, to_new),
                device_id_type=MESH,
            ).start()
        return 0

    lax.fori_loop(1, ranks, one_owner, 0)
    fill(me)
    for at, (source, target) in enumerate(((picked, arrived), (ids, arrived_ids))):
        pltpu.make_async_copy(source.at[me], target.at[me], pair_sem.at[2 * at + 1]).start()
    for copy in halo:
        copy.wait()
    for at, (source, target) in enumerate(((picked, arrived), (ids, arrived_ids))):
        rest = pl.ds(0, ranks - 1)
        pltpu.make_async_copy(source.at[rest], source.at[rest], pair_sem.at[2 * at]).wait()
        pltpu.make_async_copy(source, target, pair_sem.at[2 * at + 1]).wait()


def send(counts, rows, targets, weights, values, area, thick, shift):
    ranks, slots = rows.shape[1:]
    payload = slots // 4
    rows_dev, cols_dev = area.shape[1:]
    halo = [(16, cols_dev)] * 2 + [(rows_dev, LANE)] * 2 + [(8, LANE)] * 4
    shapes = [jax.ShapeDtypeStruct(shape, jnp.float32) for shape in halo]
    shapes.insert(0, jax.ShapeDtypeStruct((ranks, payload, LANE), jnp.float32))
    shapes.insert(1, jax.ShapeDtypeStruct((ranks, 1, slots + LANE), jnp.int32))
    shapes.append(pltpu.VMEM((FRONT + 2 * rows_dev * (cols_dev + LANE), LANE), jnp.float32))

    def scratch(*shape):
        return pltpu.VMEM(shape, jnp.float32)

    result = pl.pallas_call(
        functools.partial(send_kernel, rows_dev, cols_dev),
        out_shape=tuple(shapes),
        in_specs=[VMEM] + [HBM] * 7,
        out_specs=(HBM,) * (len(shapes) - 1) + (VMEM,),
        scratch_shapes=[
            scratch(values.shape[1], LANE),
            scratch(ranks, payload, LANE),
            pltpu.VMEM((ranks, 1, slots + LANE), jnp.int32),
            pltpu.VMEM((ranks, slots + LANE), jnp.int32),
            scratch(ranks, slots),
            pltpu.VMEM(targets.shape, jnp.int32),
            scratch(*weights.shape),
            scratch(*values.shape),
            scratch(7, 8, cols_dev),
            scratch(7, 8, cols_dev),
            scratch(7, rows_dev, LANE),
            scratch(7, rows_dev, LANE),
            scratch(16, cols_dev),
            scratch(16, cols_dev),
            scratch(rows_dev, LANE),
            scratch(rows_dev, LANE),
            pltpu.SMEM(rows.shape, jnp.int32),
            pltpu.SMEM((ranks, slots), jnp.float32),
            pltpu.SemaphoreType.DMA((17,)),
            pltpu.SemaphoreType.DMA((4,)),
            pltpu.SemaphoreType.DMA((8,)),
            pltpu.SemaphoreType.DMA((8,)),
        ],
        compiler_params=pltpu.CompilerParams(
            vmem_limit_bytes=24 * MIB, collective_id=1, has_side_effects=True
        ),
        name="send",
    )(counts, rows, targets, weights, values, area, thick, shift)
    return result[0], result[1], result[2:-1], result[-1]


def scatter_kernel(
    rows_dev,
    cols_dev,
    ids_in,
    data_in,
    _,
    part,
    cols_right,
    cols_left,
    acc,
    carry,
    data,
    ids,
    ids_sem,
    data_sem,
):
    width = cols_dev + LANE
    ranks, payload, _ = data.shape
    quarter = ranks // 4
    loads = []
    for at in range(4):
        some = pl.ds(at * quarter, quarter)
        for source, target, sem in ((ids_in, ids, ids_sem), (data_in, data, data_sem)):
            loads.append(pltpu.make_async_copy(source.at[some], target.at[some], sem.at[at]))
    for load in loads:
        load.start()
    carry[...] = jnp.zeros_like(carry)

    lane = lane_ids((1, LANE))
    masks = [(lane >= 32 * g) & (lane < 32 * g + 32) for g in range(4)]

    def add_rows(source, first, count):
        slots = [(r, g) for r in range(count) for g in range(4)]
        where_to = [ids[source, 0, (first + r) * 4 + g] for r, g in slots]
        new = [data[source, pl.ds(first + r, 1), :] for r in range(count)]
        old = [acc[pl.ds(row, 1), :] for row in where_to]
        for (r, g), row, have in zip(slots, where_to, old):
            pltpu.store(acc.at[pl.ds(row, 1), :], have + new[r], mask=masks[g])

    def one_source(source, _):
        clash = ids[source, 0, payload * 4]

        @pl.when(clash == 0)
        def _():
            for first in range(0, payload, BATCH):
                add_rows(source, first, BATCH)

        @pl.when(clash != 0)
        def _():
            def slow(row, _):
                add_rows(source, row, 1)
                return 0

            lax.fori_loop(0, payload, slow, 0)

        return 0

    for at in range(4):
        loads[2 * at].wait()
        loads[2 * at + 1].wait()
        lax.fori_loop(at * quarter, (at + 1) * quarter, one_source, 0)

    def fold(total):
        flipped = total.T
        return (flipped[0:32] + flipped[32:64]) + (flipped[64:96] + flipped[96:128])

    upper_base = rows_dev * width
    lane = lane_ids((part.shape[1], LANE))

    def pack(i, own_near, own_far, ghost):
        tile, place = i // 16, i % 16
        mine = lane // 8 == place
        ends = pltpu.roll(jnp.where(lane == 0, ghost, own_far), 8 * place + 4, 1)
        cols_right[tile] = jnp.where(mine, ends, cols_right[tile])
        cols_left[tile] = jnp.where(mine, pltpu.roll(own_near, 8 * place, 1), cols_left[tile])

    cols_right[...] = jnp.zeros_like(cols_right)
    cols_left[...] = jnp.zeros_like(cols_left)
    tiles = width // LANE

    def one_row(i, _):
        done = []
        for tile in range(tiles):
            span = slice(tile * LANE, (tile + 1) * LANE)
            base = pl.multiple_of(i * width + tile * LANE + FRONT, 8)
            lower = acc[pl.ds(base, LANE), :]
            upper = acc[pl.ds(pl.multiple_of(base + upper_base, 8), LANE), :]
            shared = upper + acc[pl.ds(base - 1, LANE), :]
            summed = lower + shared + carry[span, :]
            carry[span, :] = shared + acc[pl.ds(base + upper_base - 1, LANE), :]
            folded = fold(summed)
            part[i, :, span] = folded
            done.append(folded)
        pack(i, done[0], done[-2], done[-1])
        return 0

    lax.fori_loop(0, rows_dev, one_row, 0)
    done = [fold(carry[tile * LANE : (tile + 1) * LANE, :]) for tile in range(tiles)]
    for tile in range(tiles):
        part[rows_dev, :, tile * LANE : (tile + 1) * LANE] = done[tile]
    pack(rows_dev, done[0], done[-2], done[-1])


def scatter(ids, data, acc, rows_dev, cols_dev):
    channels = LANE // 4
    width = cols_dev + LANE
    return pl.pallas_call(
        functools.partial(scatter_kernel, rows_dev, cols_dev),
        out_shape=(
            jax.ShapeDtypeStruct((rows_dev + 1, channels, width), jnp.float32),
            jax.ShapeDtypeStruct((rows_dev // 16 + 1, channels, LANE), jnp.float32),
            jax.ShapeDtypeStruct((rows_dev // 16 + 1, channels, LANE), jnp.float32),
            pltpu.VMEM(acc.shape, jnp.float32),
        ),
        in_specs=[HBM, HBM, VMEM],
        out_specs=(VMEM, VMEM, VMEM, VMEM),
        input_output_aliases={2: 3},
        scratch_shapes=[
            pltpu.VMEM((width, LANE), jnp.float32),
            pltpu.VMEM(data.shape, jnp.float32),
            pltpu.SMEM(ids.shape, jnp.int32),
            pltpu.SemaphoreType.DMA((4,)),
            pltpu.SemaphoreType.DMA((4,)),
        ],
        compiler_params=pltpu.CompilerParams(vmem_limit_bytes=24 * MIB),
        name="scatter",
    )(ids, data, acc)[:3]


def first_piola(stretch_x, stretch_y, fields):
    gram_xx = sum(x * x for x in stretch_x)
    gram_xy = sum(x * y for x, y in zip(stretch_x, stretch_y))
    gram_yy = sum(y * y for y in stretch_y)
    determinant = gram_xx * gram_yy - gram_xy * gram_xy
    inverse = 1.0 / determinant
    inv_xx = gram_yy * inverse
    inv_xy = -gram_xy * inverse
    inv_yy = gram_xx * inverse
    shear_mod = MU_BASE * (1.5 + jnp.tanh(fields[3]))
    bulk = LAMBDA_BULK * 0.5 * jnp.log(determinant)
    piola_x, piola_y = [], []
    for along_x, along_y in zip(stretch_x, stretch_y):
        push_x = along_x * inv_xx + along_y * inv_xy
        push_y = along_x * inv_xy + along_y * inv_yy
        piola_x.append(
            shear_mod * (along_x - push_x)
            + bulk * push_x
            + PRESTRESS * (along_x * fields[0] + along_y * fields[2])
        )
        piola_y.append(
            shear_mod * (along_y - push_y)
            + bulk * push_y
            + PRESTRESS * (along_x * fields[2] + along_y * fields[1])
        )
    return piola_x, piola_y


def sheet_kernel(n_rows, n_cols, *refs):
    part_in, cols_right, cols_left, area_in, thick_in, shift_in = refs[:6]
    s_in = refs[6:14]
    total, speed = refs[14:16]
    p_halo, s_halo, refs = refs[16:24], refs[24:32], refs[32:]
    part, resid, dir_a, dir_b, dir_c, field, mem, mass, coef = refs[:9]
    load_sem, send_sem, recv_sem = refs[9:]
    p_dn, p_up, p_l, p_r, p_dl, p_dr, p_ul, p_ur = p_halo
    s_dn, s_up, s_l, s_r, s_dl, s_dr, s_ul, s_ur = s_halo
    rows_dev, cols_dev = area_in.shape[1:]
    channels, width = part.shape[1:]
    tall = rows_dev + 16
    middle, main = pl.ds(8, rows_dev), pl.ds(0, cols_dev)

    barrier = pltpu.get_barrier_semaphore()
    for device in neighbours():
        pl.semaphore_signal(barrier, inc=1, device_id=device, device_id_type=MESH)

    field[:, 0:8, :] = jnp.zeros((7, 8, width), jnp.float32)
    field[:, 8 + rows_dev : tall, :] = jnp.zeros((7, 8, width), jnp.float32)
    loads = [
        (area_in, field.at[pl.ds(0, 2), middle, main]),
        (thick_in, field.at[pl.ds(2, 2), middle, main]),
        (shift_in, field.at[pl.ds(4, 3), middle, main]),
    ] + list(zip(s_in, s_halo))
    loads.append((part_in, part))
    loads = [
        pltpu.make_async_copy(source, target, load_sem.at[at])
        for at, (source, target) in enumerate(loads)
    ]
    for load in loads:
        load.start()

    high, low = pl.ds(part_in.shape[0] - HALO - 1, HALO + 1), pl.ds(0, HALO)
    tiles_high, tiles_low = pl.ds((rows_dev - 1) // 16, 2), pl.ds(0, 1)
    pl.semaphore_wait(barrier, 8)
    copies = to_neighbours(
        [
            part_in.at[high],
            part_in.at[low],
            cols_right,
            cols_left,
            cols_right.at[tiles_high],
            cols_left.at[tiles_high],
            cols_right.at[tiles_low],
            cols_left.at[tiles_low],
        ],
        p_halo,
        send_sem,
        recv_sem,
    )
    for copy in copies[2:] + copies[:2]:
        copy.start()

    for load in loads[:-1]:
        load.wait()
    sides = []
    for left, right, size in ((s_l, s_r, rows_dev), (s_dl, s_dr, 8), (s_ul, s_ur, 8)):
        sides.append((left[...], right[...], lane_ids((size, LANE))))
    for f in range(7):
        if f < 2:
            field[f, 3:8, 0:cols_dev] = s_dn[5 * f : 5 * f + 5, :]
            field[f, 8 + rows_dev : 12 + rows_dev, 0:cols_dev] = s_up[4 * f : 4 * f + 4, :]
        else:
            field[f, 7:8, 0:cols_dev] = s_dn[8 + f : 9 + f, :]
            if f >= 4:
                field[f, 8 + rows_dev : 9 + rows_dev, 0:cols_dev] = s_up[4 + f : 5 + f, :]
        wide, narrow = (5, 4) if f < 2 else (1, 0 if f < 4 else 1)
        back = 5 if f < 2 else 5
        made = []
        for left, right, lane in sides:
            from_l = pltpu.roll(left, LANE - back - 8 * f, 1)
            from_r = pltpu.roll(right, (LANE - 8 * f) % LANE, 1)
            made.append(
                jnp.where(lane >= LANE - wide, from_l, jnp.where(lane < narrow, from_r, 0.0))
            )
        field[f, 8 : 8 + rows_dev, cols_dev:width] = made[0]
        row8 = lax.broadcasted_iota(jnp.int32, (8, LANE), 0)
        under = row8 >= 8 - wide
        over = row8 < narrow
        field[f, 0:8, cols_dev:width] = jnp.where(under, made[1], 0.0)
        field[f, 8 + rows_dev : tall, cols_dev:width] = jnp.where(over, made[2], 0.0)

    shape = (tall, width)
    row = lax.broadcasted_iota(jnp.int32, shape, 0) - 8 + lax.axis_index("new") * rows_dev
    lane = lax.broadcasted_iota(jnp.int32, shape, 1)
    col = jnp.where(lane < cols_dev + 64, lane, lane - width) + lax.axis_index("old") * cols_dev
    valid = (row >= 0) & (row < n_rows - 1) & (col >= 0) & (col < n_cols - 1)

    def from_left(x):
        return pltpu.roll(x, 1, 1)

    def from_right(x):
        return pltpu.roll(x, width - 1, 1)

    def from_below(x):
        return pltpu.roll(x, 1, 0)

    def from_above(x):
        return pltpu.roll(x, tall - 1, 0)

    area_low = jnp.where(valid, field[0], 0.0)
    area_up = jnp.where(valid, field[1], 0.0)
    field[2] = field[2] * area_low
    field[3] = field[3] * area_up
    lower, upper = area_low / 12.0, area_up / 12.0
    both = lower + upper
    lower_left, upper_below = from_left(lower), from_below(upper)
    weight = both + lower_left + upper_below + from_below(from_left(both))
    inv = jnp.where(weight > 0.0, 1.0 / (2.0 * weight), 0.0)
    inv_right = from_right(inv)
    east, north = lower + upper_below, upper + lower_left
    coef[0] = inv * (1.0 / 3.0)
    coef[1] = inv * north
    coef[2] = inv * from_below(north)
    coef[3] = from_left(inv * east)
    coef[4] = from_left(inv * both)
    coef[5] = inv_right * east
    coef[6] = inv_right * from_below(both)
    vol_low, vol_up = field[2], field[3]
    mass[...] = (
        vol_low
        + vol_up
        + from_left(vol_low)
        + from_below(vol_up)
        + from_below(from_left(vol_low + vol_up))
    ) * (1.0 / 3.0)
    mem[...] = jnp.zeros_like(mem)

    centre = 0.5 * (EIG_HIGH + EIG_LOW)
    half_width = 0.5 * (EIG_HIGH - EIG_LOW)
    ratio_eig = centre / half_width
    edge = lane_ids((channels, LANE))

    def widen(inner, left, right, place):
        left = pltpu.roll(left, lax.rem(2 * LANE - 4 - 8 * place, LANE), 1)
        right = pltpu.roll(right, lax.rem(LANE - 8 * place, LANE), 1)
        first = inner[:, 0:LANE] + jnp.where(edge == 0, left, 0.0)
        last = inner[:, cols_dev:width] + jnp.where(
            edge >= LANE - HALO, left, jnp.where(edge < HALO, right, 0.0)
        )
        return jnp.concatenate([first, inner[:, LANE:cols_dev], last], axis=1)

    def begin(e, rhs):
        scaled = rhs * coef[0, pl.ds(e + 4, 1), :]
        resid[e] = scaled
        dir_a[e] = scaled * (1.0 / centre)

    def own(i):
        i = jnp.int32(i)
        return widen(part[i], p_l[i // 16], p_r[i // 16], i % 16)

    def under(k):
        i = rows_dev - HALO + k
        tile = i // 16 - (rows_dev - 1) // 16
        return widen(p_dn[k], p_dl[tile], p_dr[tile], jnp.int32(i % 16))

    def over(k):
        return widen(p_up[k], p_ul[0], p_ur[0], jnp.int32(k))

    rhos = [1.0 / ratio_eig]
    for _ in range(ITERS):
        rhos.append(1.0 / (2.0 * ratio_eig - rhos[-1]))
    directions = [dir_a, dir_b, dir_c]

    def sweep_row(sweep, e):
        keep = rhos[sweep + 1] * rhos[sweep]
        gain = 2.0 * rhos[sweep + 1] / half_width
        final = sweep == ITERS - 1
        source = directions[sweep]
        k = [coef[c, pl.ds(e + 4, 1), :] for c in range(1, 7)]
        through = None
        for group in range(0, channels, 8):
            at = slice(group, group + 8)
            here, up, down = source[e, at, :], source[e + 1, at, :], source[e - 1, at, :]
            to_left = k[2] * here + k[3] * up
            to_right = k[4] * here + k[5] * down
            left = resid[e, at, :] - (
                here
                + k[0] * up
                + k[1] * down
                + pltpu.roll(to_left, width - 1, 1)
                + pltpu.roll(to_right, 1, 1)
            )
            new = keep * here + gain * left
            if final:
                summed = (dir_a[e, at, :] + dir_b[e, at, :]) + (here + new)
                total[e, at, :] = summed
                through = summed if through is None else through + summed
            else:
                resid[e, at, :] = left
                directions[sweep + 1][e, at, :] = new
        if final:
            through = through * (1.0 / POINTS)
            for at, value in enumerate((0, 1, 5, 7)):
                mem[at, pl.ds(e + 4, 1), :] = through[value : value + 1, :]

    for copy in copies[2:]:
        copy.wait()
    loads[-1].wait()

    def inner_row(i, _):
        begin(i + HALO, own(i))
        return 0

    lax.fori_loop(1, rows_dev, inner_row, 0)
    for sweep in range(ITERS):

        def inner_sweep(e, _, sweep=sweep):
            sweep_row(sweep, e)
            return 0

        lax.fori_loop(HALO + 2 + sweep, rows_dev + HALO - 1 - sweep, inner_sweep, 0)

    for copy in copies[:2]:
        copy.wait()
    for e in range(HALO):
        begin(e, under(e))
    begin(HALO, own(0) + under(HALO))
    begin(rows_dev + HALO, own(rows_dev) + over(0))
    for e in range(1, HALO):
        begin(rows_dev + HALO + e, over(e))
    for sweep in range(ITERS):
        def outer_sweep(k, _, sweep=sweep):
            low_end = HALO + 1
            sweep_row(
                sweep,
                jnp.where(k < low_end, 1 + sweep + k, rows_dev + HALO - 1 - sweep + k - low_end),
            )
            return 0

        lax.fori_loop(0, 2 * HALO + 1, outer_sweep, 0)

    anchor = [field[4 + c] for c in range(3)]
    beside = [from_right(x) for x in anchor]
    upward = [from_above(x) for x in anchor]
    across = [from_above(x) for x in beside]
    m_anchor = [mem[c] for c in range(4)]
    m_beside = [from_right(x) for x in m_anchor]
    m_upward = [from_above(x) for x in m_anchor]
    m_across = [from_above(x) for x in m_beside]
    third = 1.0 / 3.0
    m_low = [(a + b + x) * third for a, b, x in zip(m_anchor, m_beside, m_across)]
    m_up = [(a + x + u) * third for a, x, u in zip(m_anchor, m_across, m_upward)]
    low_x = [b - a for a, b in zip(anchor, beside)]
    low_y = [x - b for b, x in zip(beside, across)]
    up_x = [x - u for u, x in zip(upward, across)]
    up_y = [u - a for a, u in zip(anchor, upward)]
    low_x[0], up_x[0] = 1.0 + low_x[0], 1.0 + up_x[0]
    low_y[1], up_y[1] = 1.0 + low_y[1], 1.0 + up_y[1]
    piola_lx, piola_ly = first_piola(low_x, low_y, m_low)
    piola_ux, piola_uy = first_piola(up_x, up_y, m_up)
    vol_low, vol_up = field[2], field[3]
    node_mass = mass[8 : 8 + rows_dev, 0:cols_dev]
    for c in range(3):
        f_beside = -vol_low * (piola_lx[c] - piola_ly[c])
        f_across_low = -vol_low * piola_ly[c]
        f_across_up = -vol_up * piola_ux[c]
        f_upward = -vol_up * (piola_uy[c] - piola_ux[c])
        f_anchor = -(f_beside + f_across_low) - (f_across_up + f_upward)
        force = (
            f_anchor
            + from_left(f_beside)
            + from_below(f_upward)
            + from_below(from_left(f_across_low + f_across_up))
        )
        speed_up = force[8 : 8 + rows_dev, 0:cols_dev] / node_mass
        speed[c] = speed_up + GRAVITY if c == 2 else speed_up


def sheet(part, cols_right, cols_left, fields, halo, n_rows, n_cols):
    channels, width = part.shape[1:]
    rows_dev, cols_dev = fields[0].shape[1:]
    tall, long = rows_dev + 16, rows_dev + 2 * HALO
    tiles = cols_right.shape[0]

    def scratch(*shape):
        return pltpu.VMEM(shape, jnp.float32)

    block = scratch(long, channels, width)
    part_halo = [(HALO + 1, channels, width), (HALO, channels, width)]
    part_halo += [(tiles, channels, LANE)] * 2 + [(2, channels, LANE)] * 2
    part_halo += [(1, channels, LANE)] * 2
    return pl.pallas_call(
        functools.partial(sheet_kernel, n_rows, n_cols),
        out_shape=(
            block,
            scratch(3, rows_dev, cols_dev),
        ),
        in_specs=[HBM] * 14,
        out_specs=(VMEM, VMEM),
        scratch_shapes=[scratch(*shape) for shape in part_halo]
        + [scratch(*x.shape) for x in halo]
        + [
            scratch(*part.shape),
            block,
            block,
            block,
            block,
            scratch(7, tall, width),
            scratch(4, tall, width),
            scratch(tall, width),
            scratch(7, tall, width),
            pltpu.SemaphoreType.DMA((12,)),
            pltpu.SemaphoreType.DMA((8,)),
            pltpu.SemaphoreType.DMA((8,)),
        ],
        compiler_params=pltpu.CompilerParams(
            vmem_limit_bytes=54 * MIB, collective_id=2, has_side_effects=True
        ),
        name="sheet",
    )(part, cols_right, cols_left, *fields, *halo)


def finish_kernel(total, speed_up, velocity, out, vel_out):
    channels, rows, cols = out.shape
    here = pl.ds(HALO + pl.program_id(0) * rows, rows)
    for channel in range(channels):
        out[channel] = total[here, channel, 0:cols]
    vel_out[...] = velocity[...] + TIME_STEP * speed_up[...]


def finish(total, speed_up, velocity):
    channels = total.shape[1]
    rows_dev, cols_dev = velocity.shape[1:]

    def plane(count):
        return pl.BlockSpec((count, 8, cols_dev), lambda i: (0, i, 0))

    return pl.pallas_call(
        finish_kernel,
        grid=(rows_dev // 8,),
        out_shape=(
            jax.ShapeDtypeStruct((channels, rows_dev, cols_dev), jnp.float32),
            jax.ShapeDtypeStruct(velocity.shape, jnp.float32),
        ),
        in_specs=[VMEM, plane(3), plane(3)],
        out_specs=(plane(channels), plane(3)),
        compiler_params=pltpu.CompilerParams(vmem_limit_bytes=40 * MIB),
        name="finish",
    )(total, speed_up, velocity)


def local(
    old_values,
    pair_rows,
    pair_targets,
    pair_weights,
    pair_counts,
    cell_area,
    thickness,
    displacement,
    velocity,
):
    rows_dev, cols_dev = cell_area.shape[1:]
    n_old, n_new = lax.axis_size("old"), lax.axis_size("new")
    arrived, ids, halo, acc = send(
        pair_counts,
        pair_rows,
        pair_targets,
        pair_weights,
        old_values,
        cell_area,
        thickness,
        displacement,
    )
    part, cols_right, cols_left = scatter(ids, arrived, acc, rows_dev, cols_dev)
    fields = (cell_area, thickness, displacement)
    total, speed_up = sheet(
        part, cols_right, cols_left, fields, halo, n_new * rows_dev, n_old * cols_dev
    )
    return finish(total, speed_up, velocity)


def solution(mesh):
    return jax.shard_map(
        local,
        mesh=mesh,
        in_specs=(
            P(None, ("old", "new")),
            P(("old", "new"), None, None),
            P(("old", "new"), None, None),
            P(("old", "new"), None, None),
            P(("old", "new"), None),
            P(None, "new", "old"),
            P(None, "new", "old"),
            P(None, "new", "old"),
            P(None, "new", "old"),
        ),
        out_specs=(P(None, "new", "old"), P(None, "new", "old")),
        check_vma=False,
    )
```

```python
import functools

import jax
import jax.numpy as jnp
from jax import lax
from jax.experimental import pallas as pl
from jax.experimental.pallas import tpu as pltpu
from jax.sharding import PartitionSpec as P

POINTS = 4
COMP = 8
ITERS = 3
MU_BASE = 10.0
LAMBDA_BULK = 20.0
PRESTRESS = 4.0
TIME_STEP = 1.0
GRAVITY = -1.0
EIG_LOW = 0.5
EIG_HIGH = 2.0

LANE = 128
FRONT = 8
BATCH = 4
HALO = 4
STRIDE = 37
MESH = pl.DeviceIdType.MESH
MIB = 1024 * 1024

VMEM = pl.BlockSpec(memory_space=pltpu.VMEM)
SMEM = pl.BlockSpec(memory_space=pltpu.SMEM)
HBM = pl.BlockSpec(memory_space=pltpu.HBM)


def lane_ids(shape):
    return lax.broadcasted_iota(jnp.int32, shape, len(shape) - 1)


def neighbours():
    n_old, n_new = lax.axis_size("old"), lax.axis_size("new")
    old, new = lax.axis_index("old"), lax.axis_index("new")
    left, right = lax.rem(old + n_old - 1, n_old), lax.rem(old + 1, n_old)
    below, above = lax.rem(new + n_new - 1, n_new), lax.rem(new + 1, n_new)
    return [
        (old, above),
        (old, below),
        (right, new),
        (left, new),
        (right, above),
        (left, above),
        (right, below),
        (left, below),
    ]


def to_neighbours(sources, targets, send_sem, recv_sem):
    around = neighbours()
    return [
        pltpu.make_async_remote_copy(
            src_ref=source,
            dst_ref=target,
            send_sem=send_sem.at[at],
            recv_sem=recv_sem.at[at],
            device_id=device,
            device_id_type=MESH,
        )
        for at, (source, target, device) in enumerate(zip(sources, targets, around + around))
    ]


def send_kernel(
    rows_dev,
    cols_dev,
    counts,
    rows_in,
    targets_in,
    weights_in,
    values_in,
    area,
    thick,
    shift_in,
    arrived,
    arrived_ids,
    s_dn,
    s_up,
    s_l,
    s_r,
    s_dl,
    s_dr,
    s_ul,
    s_ur,
    acc,
    table,
    picked,
    ids,
    notes,
    weights_flat,
    targets,
    weights_raw,
    values,
    rim_low,
    rim_high,
    rim_left,
    rim_right,
    pack_up,
    pack_down,
    pack_right,
    pack_left,
    rows,
    weights,
    local_sem,
    pair_sem,
    near_send,
    near_recv,
):
    n_old, n_new = lax.axis_size("old"), lax.axis_size("new")
    old, new = lax.axis_index("old"), lax.axis_index("new")
    ranks, payload, _ = picked.shape
    slots = payload * 4
    total = values.shape[1]
    me = old * n_new + new
    top, low = pl.ds(rows_dev - 8, 8), pl.ds(0, 8)
    near, far = pl.ds(0, LANE), pl.ds(cols_dev - LANE, LANE)

    loads = [
        (targets_in, targets),
        (weights_in, weights_raw),
        (values_in, values),
        (rows_in, rows),
    ]
    for source, at, count in ((area, 0, 2), (thick, 2, 2), (shift_in, 4, 3)):
        into = pl.ds(at, count)
        loads.append((source.at[:, top, :], rim_high.at[into]))
        loads.append((source.at[:, low, :], rim_low.at[into]))
        loads.append((source.at[:, :, far], rim_right.at[into]))
        loads.append((source.at[:, :, near], rim_left.at[into]))
    loads = [
        pltpu.make_async_copy(source, target, local_sem.at[at])
        for at, (source, target) in enumerate(loads)
    ]
    for load in loads:
        load.start()

    barrier = pltpu.get_barrier_semaphore()

    def greet(step, _):
        other = lax.rem(me + step, ranks)
        pl.semaphore_signal(
            barrier, inc=1, device_id=(other // n_new, other % n_new), device_id_type=MESH
        )
        return 0

    lax.fori_loop(1, ranks, greet, 0)

    slot = lane_ids((ranks, slots))
    owner = lax.broadcasted_iota(jnp.int32, (ranks, slots), 0)
    count = jnp.broadcast_to(counts[...].astype(jnp.float32), (ranks, ranks)).T.astype(jnp.int32)
    loads[0].wait()
    loads[1].wait()
    target = targets[0]
    cell, col = target // cols_dev, target % cols_dev
    outside = ((owner % n_new == n_new - 1) & (cell % rows_dev == rows_dev - 1)) | (
        (owner // n_new == n_old - 1) & (col == cols_dev - 1)
    )
    used = (slot < count) & jnp.logical_not(outside)
    weights_flat[...] = jnp.where(used, weights_raw[0], 0.0)
    load_weights = pltpu.make_async_copy(weights_flat, weights, local_sem.at[len(loads)])
    load_weights.start()
    spare = slot // 4 % FRONT
    where_to = jnp.where(used, FRONT + target, spare)
    clash = jnp.zeros((ranks, slots), jnp.int32)
    for gap in range(1, BATCH):
        same = (where_to == pltpu.roll(where_to, 4 * gap, 1)) & (slot % (4 * BATCH) >= 4 * gap)
        clash = clash | same.astype(jnp.int32)
    found = jnp.broadcast_to(jnp.max(clash, axis=1, keepdims=True), (ranks, slots))
    notes[:, 0:slots] = jnp.where(clash > 0, spare, where_to)
    notes[:, slots : 2 * slots] = jnp.where(slot == 0, found, clash * where_to)

    unroll = 8
    loads[2].wait()

    def flip(step, _):
        for at in range(unroll):
            start = pl.multiple_of((step * unroll + at) * LANE, LANE)
            part = values[:, pl.ds(start, LANE)]
            table[pl.ds(start, LANE), :] = jnp.concatenate([part] * 4, axis=0).T
        return 0

    lax.fori_loop(0, total // (LANE * unroll), flip, 0)

    for load in loads[3:]:
        load.wait()
    pack_up[...] = jnp.zeros_like(pack_up)
    pack_down[...] = jnp.zeros_like(pack_down)
    lane = lane_ids((rows_dev, LANE))
    to_right = jnp.zeros((rows_dev, LANE), jnp.float32)
    to_left = jnp.zeros((rows_dev, LANE), jnp.float32)
    for f in range(7):
        if f < 2:
            pack_up[5 * f : 5 * f + 5, :] = rim_high[f, 3:8, :]
            pack_down[4 * f : 4 * f + 4, :] = rim_low[f, 0:4, :]
        else:
            pack_up[8 + f : 9 + f, :] = rim_high[f, 7:8, :]
            if f >= 4:
                pack_down[4 + f : 5 + f, :] = rim_low[f, 0:1, :]
        mine = lane // 8 == f
        to_right = jnp.where(mine, pltpu.roll(rim_right[f], 8 * f + 5, 1), to_right)
        to_left = jnp.where(mine, pltpu.roll(rim_left[f], 8 * f, 1), to_left)
    pack_right[...] = to_right
    pack_left[...] = to_left
    load_weights.wait()
    pl.semaphore_wait(barrier, ranks - 1)

    halo = to_neighbours(
        [
            pack_up,
            pack_down,
            pack_right,
            pack_left,
            pack_right.at[top],
            pack_left.at[top],
            pack_right.at[low],
            pack_left.at[low],
        ],
        [s_dn, s_up, s_l, s_r, s_dl, s_dr, s_ul, s_ur],
        near_send,
        near_recv,
    )
    for copy in halo:
        copy.start()

    lane = lane_ids((1, LANE))
    first, second, third = lane < 32, lane < 64, lane < 96

    def fill(owner):
        for row in range(payload):
            part = [
                table[pl.ds(rows[0, owner, row * 4 + g], 1), :] * weights[owner, row * 4 + g]
                for g in range(4)
            ]
            merged = jnp.where(
                first, part[0], jnp.where(second, part[1], jnp.where(third, part[2], part[3]))
            )
            picked[owner, pl.ds(row, 1), :] = merged
        ids[owner] = notes[pl.ds(owner, 1), :]

    chunk = (acc.shape[0] - 2 * FRONT) // ranks

    def clear(step):
        start = pl.multiple_of(FRONT + step * chunk, 8)
        acc[pl.ds(start, chunk), :] = jnp.zeros((chunk, LANE), jnp.float32)

    for end in (0, acc.shape[0] - FRONT):
        acc[pl.ds(end, FRONT), :] = jnp.zeros((FRONT, LANE), jnp.float32)
    clear(0)

    def one_owner(step, _):
        shift = lax.rem(step * STRIDE, ranks)
        to_old = lax.rem(old + shift // n_new, n_old)
        to_new = lax.rem(new + shift % n_new, n_new)
        owner = to_old * n_new + to_new
        fill(owner)
        clear(step)
        for at, (source, target) in enumerate(((picked, arrived), (ids, arrived_ids))):
            pltpu.make_async_remote_copy(
                src_ref=source.at[owner],
                dst_ref=target.at[me],
                send_sem=pair_sem.at[2 * at],
                recv_sem=pair_sem.at[2 * at + 1],
                device_id=(to_old, to_new),
                device_id_type=MESH,
            ).start()
        return 0

    lax.fori_loop(1, ranks, one_owner, 0)
    fill(me)
    for at, (source, target) in enumerate(((picked, arrived), (ids, arrived_ids))):
        pltpu.make_async_copy(source.at[me], target.at[me], pair_sem.at[2 * at + 1]).start()
    for copy in halo:
        copy.wait()
    for at, (source, target) in enumerate(((picked, arrived), (ids, arrived_ids))):
        rest = pl.ds(0, ranks - 1)
        pltpu.make_async_copy(source.at[rest], source.at[rest], pair_sem.at[2 * at]).wait()
        pltpu.make_async_copy(source, target, pair_sem.at[2 * at + 1]).wait()


def send(counts, rows, targets, weights, values, area, thick, shift):
    ranks, slots = rows.shape[1:]
    payload = slots // 4
    rows_dev, cols_dev = area.shape[1:]
    halo = [(16, cols_dev)] * 2 + [(rows_dev, LANE)] * 2 + [(8, LANE)] * 4
    shapes = [jax.ShapeDtypeStruct(shape, jnp.float32) for shape in halo]
    shapes.insert(0, jax.ShapeDtypeStruct((ranks, payload, LANE), jnp.float32))
    shapes.insert(1, jax.ShapeDtypeStruct((ranks, 1, 2 * slots), jnp.int32))
    shapes.append(pltpu.VMEM((2 * FRONT + 2 * rows_dev * cols_dev, LANE), jnp.float32))

    def scratch(*shape):
        return pltpu.VMEM(shape, jnp.float32)

    result = pl.pallas_call(
        functools.partial(send_kernel, rows_dev, cols_dev),
        out_shape=tuple(shapes),
        in_specs=[VMEM] + [HBM] * 7,
        out_specs=(HBM,) * (len(shapes) - 1) + (VMEM,),
        scratch_shapes=[
            scratch(values.shape[1], LANE),
            scratch(ranks, payload, LANE),
            pltpu.VMEM((ranks, 1, 2 * slots), jnp.int32),
            pltpu.VMEM((ranks, 2 * slots), jnp.int32),
            scratch(ranks, slots),
            pltpu.VMEM(targets.shape, jnp.int32),
            scratch(*weights.shape),
            scratch(*values.shape),
            scratch(7, 8, cols_dev),
            scratch(7, 8, cols_dev),
            scratch(7, rows_dev, LANE),
            scratch(7, rows_dev, LANE),
            scratch(16, cols_dev),
            scratch(16, cols_dev),
            scratch(rows_dev, LANE),
            scratch(rows_dev, LANE),
            pltpu.SMEM(rows.shape, jnp.int32),
            pltpu.SMEM((ranks, slots), jnp.float32),
            pltpu.SemaphoreType.DMA((17,)),
            pltpu.SemaphoreType.DMA((4,)),
            pltpu.SemaphoreType.DMA((8,)),
            pltpu.SemaphoreType.DMA((8,)),
        ],
        compiler_params=pltpu.CompilerParams(
            vmem_limit_bytes=24 * MIB, collective_id=1, has_side_effects=True
        ),
        name="send",
    )(counts, rows, targets, weights, values, area, thick, shift)
    return result[0], result[1], result[2:-1], result[-1]


def fold(total):
    flipped = total.T
    return (flipped[0:32] + flipped[32:64]) + (flipped[64:96] + flipped[96:128])


def node_parts(acc, rows_dev, cols_dev, i, first, size, cells, below):
    upper = rows_dev * cols_dev
    base = i * cols_dev + (FRONT + first)
    here, left = [], []
    if cells:
        here += [base, base + upper]
        left += [base - 1]
    if below:
        here += [base + upper - cols_dev]
        left += [base - cols_dev - 1, base + upper - cols_dev - 1]
    here, left = ([acc[pl.ds(at, size), :] for at in some] for some in (here, left))
    return functools.reduce(jnp.add, here), functools.reduce(jnp.add, left)


def node_tile(acc, rows_dev, cols_dev, i, tile, cells=True, below=True):
    here, left = node_parts(acc, rows_dev, cols_dev, i, tile * LANE, LANE, cells, below)
    if tile == 0:
        rows = lax.broadcasted_iota(jnp.int32, (LANE, LANE), 0)
        left = jnp.where(rows == 0, 0.0, left)
    return fold(here + left)


def scatter_kernel(
    rows_dev,
    cols_dev,
    ids_in,
    data_in,
    _,
    rim_high,
    rim_low,
    cols_right,
    cols_left,
    acc,
    flat_right,
    flat_left,
    data,
    ids,
    ids_sem,
    data_sem,
):
    ranks, payload, _ = data.shape
    slots = payload * 4
    quarter = ranks // 4
    loads = []
    for at in range(4):
        some = pl.ds(at * quarter, quarter)
        for source, target, sem in ((ids_in, ids, ids_sem), (data_in, data, data_sem)):
            loads.append(pltpu.make_async_copy(source.at[some], target.at[some], sem.at[at]))
    for load in loads:
        load.start()
    flat_right[...] = jnp.zeros_like(flat_right)
    flat_left[...] = jnp.zeros_like(flat_left)

    lane = lane_ids((1, LANE))
    masks = [lane // 32 == g for g in range(4)]

    def add_rows(source, first):
        where_to = [ids[source, 0, first * 4 + k] for k in range(4 * BATCH)]
        new = [data[source, pl.ds(first + r, 1), :] for r in range(BATCH)]
        old = [acc[pl.ds(row, 1), :] for row in where_to]
        for k, (row, have) in enumerate(zip(where_to, old)):
            pltpu.store(acc.at[pl.ds(row, 1), :], have + new[k // 4], mask=masks[k % 4])

    def one_source(source, _):
        for first in range(0, payload, BATCH):
            add_rows(source, first)
        return 0

    for at in range(4):
        loads[2 * at].wait()
        loads[2 * at + 1].wait()
        lax.fori_loop(at * quarter, (at + 1) * quarter, one_source, 0)

    def late(source, _):
        def one_slot(k, _):
            row = ids[source, 0, slots + k]

            @pl.when(row > 0)
            def _():
                new = data[source, pl.ds(k // 4, 1), :]
                acc[pl.ds(row, 1), :] += jnp.where(lane // 32 == k % 4, new, 0.0)

            return 0

        @pl.when(ids[source, 0, slots] > 0)
        def _():
            lax.fori_loop(1, slots, one_slot, 0)

        return 0

    def late_group(group, _):
        found = sum(ids[group * 8 + k, 0, slots] for k in range(8))

        @pl.when(found > 0)
        def _():
            lax.fori_loop(group * 8, group * 8 + 8, late, 0)

        return 0

    lax.fori_loop(0, ranks // 8, late_group, 0)

    tiles = cols_dev // LANE
    for at in range(HALO):
        for tile in range(tiles):
            span = slice(tile * LANE, (tile + 1) * LANE)
            rim_low[at, :, span] = node_tile(acc, rows_dev, cols_dev, at, tile, True, at > 0)
    for at in range(HALO + 1):
        i = rows_dev - HALO + at
        for tile in range(tiles):
            span = slice(tile * LANE, (tile + 1) * LANE)
            rim_high[at, :, span] = node_tile(acc, rows_dev, cols_dev, i, tile, i < rows_dev)

    row8 = lax.broadcasted_iota(jnp.int32, (8, LANE), 0)

    def rim_columns(i, cells, below):
        into = pl.ds(pl.multiple_of(i * 8, 8), 8)
        here, left = node_parts(acc, rows_dev, cols_dev, i, cols_dev - HALO, 8, cells, below)
        flat_right[into, :] = jnp.where(row8 < HALO, here, 0.0) + jnp.where(
            row8 < HALO + 1, left, 0.0
        )
        here, left = node_parts(acc, rows_dev, cols_dev, i, 0, 8, cells, below)
        flat_left[into, :] = jnp.where(
            row8 < HALO, here + jnp.where(row8 > 0, left, 0.0), 0.0
        )

    def inner_columns(i, _):
        rim_columns(i, True, True)
        return 0

    rim_columns(jnp.int32(0), True, False)
    lax.fori_loop(1, rows_dev, inner_columns, 0)
    rim_columns(jnp.int32(rows_dev), False, True)
    for tile in range(cols_right.shape[0]):
        span = slice(tile * LANE, (tile + 1) * LANE)
        cols_right[tile] = fold(flat_right[span, :])
        cols_left[tile] = fold(flat_left[span, :])


def scatter(ids, data, acc, rows_dev, cols_dev):
    channels = LANE // 4
    tiles = rows_dev // 16 + 1
    shapes = [(HALO + 1, channels, cols_dev), (HALO, channels, cols_dev)]
    shapes += [(tiles, channels, LANE)] * 2
    return pl.pallas_call(
        functools.partial(scatter_kernel, rows_dev, cols_dev),
        out_shape=tuple(jax.ShapeDtypeStruct(shape, jnp.float32) for shape in shapes)
        + (pltpu.VMEM(acc.shape, jnp.float32),),
        in_specs=[HBM, HBM, VMEM],
        out_specs=(VMEM,) * 5,
        input_output_aliases={2: 4},
        scratch_shapes=[
            pltpu.VMEM((tiles * LANE, LANE), jnp.float32),
            pltpu.VMEM((tiles * LANE, LANE), jnp.float32),
            pltpu.VMEM(data.shape, jnp.float32),
            pltpu.SMEM(ids.shape, jnp.int32),
            pltpu.SemaphoreType.DMA((4,)),
            pltpu.SemaphoreType.DMA((4,)),
        ],
        compiler_params=pltpu.CompilerParams(vmem_limit_bytes=24 * MIB),
        name="scatter",
    )(ids, data, acc)


def first_piola(stretch_x, stretch_y, fields):
    gram_xx = sum(x * x for x in stretch_x)
    gram_xy = sum(x * y for x, y in zip(stretch_x, stretch_y))
    gram_yy = sum(y * y for y in stretch_y)
    determinant = gram_xx * gram_yy - gram_xy * gram_xy
    inverse = 1.0 / determinant
    inv_xx = gram_yy * inverse
    inv_xy = -gram_xy * inverse
    inv_yy = gram_xx * inverse
    shear_mod = MU_BASE * (1.5 + jnp.tanh(fields[3]))
    bulk = LAMBDA_BULK * 0.5 * jnp.log(determinant)
    piola_x, piola_y = [], []
    for along_x, along_y in zip(stretch_x, stretch_y):
        push_x = along_x * inv_xx + along_y * inv_xy
        push_y = along_x * inv_xy + along_y * inv_yy
        piola_x.append(
            shear_mod * (along_x - push_x)
            + bulk * push_x
            + PRESTRESS * (along_x * fields[0] + along_y * fields[2])
        )
        piola_y.append(
            shear_mod * (along_y - push_y)
            + bulk * push_y
            + PRESTRESS * (along_x * fields[2] + along_y * fields[1])
        )
    return piola_x, piola_y


def sheet_kernel(n_rows, n_cols, *refs):
    acc, rim_high, rim_low, cols_right, cols_left, area_in, thick_in, shift_in = refs[:8]
    s_in = refs[8:16]
    total, speed = refs[16:18]
    p_halo, s_halo, refs = refs[18:28], refs[28:36], refs[36:]
    resid, first_sum, field, mem, mass, coef, p_own = refs[:7]
    load_sem, send_sem, recv_sem = refs[7:]
    p_dn, p_up, p_l, p_r, p_dl, p_dr, p_ul, p_ur, p_d, p_u = p_halo
    s_dn, s_up, s_l, s_r, s_dl, s_dr, s_ul, s_ur = s_halo
    rows_dev, cols_dev = area_in.shape[1:]
    channels, width = resid.shape[1:]
    tall = rows_dev + 16
    middle, main = pl.ds(8, rows_dev), pl.ds(0, cols_dev)

    barrier = pltpu.get_barrier_semaphore()
    for device in neighbours():
        pl.semaphore_signal(barrier, inc=1, device_id=device, device_id_type=MESH)

    field[:, 0:8, :] = jnp.zeros((7, 8, width), jnp.float32)
    field[:, 8 + rows_dev : tall, :] = jnp.zeros((7, 8, width), jnp.float32)
    loads = [
        (area_in, field.at[pl.ds(0, 2), middle, main]),
        (thick_in, field.at[pl.ds(2, 2), middle, main]),
        (shift_in, field.at[pl.ds(4, 3), middle, main]),
    ] + list(zip(s_in, s_halo))
    loads += [
        (cols_right, p_own),
        (rim_low, resid.at[pl.ds(HALO, HALO), :, main]),
        (rim_high, resid.at[pl.ds(rows_dev, HALO + 1), :, main]),
    ]
    loads = [
        pltpu.make_async_copy(source, target, load_sem.at[at])
        for at, (source, target) in enumerate(loads)
    ]
    for load in loads:
        load.start()

    tiles_high, tiles_low = pl.ds((rows_dev - 1) // 16, 2), pl.ds(0, 1)
    pl.semaphore_wait(barrier, 8)
    copies = to_neighbours(
        [
            rim_high,
            rim_low,
            cols_right,
            cols_left,
            cols_right.at[tiles_high],
            cols_left.at[tiles_high],
            cols_right.at[tiles_low],
            cols_left.at[tiles_low],
            cols_right.at[tiles_high],
            cols_right.at[tiles_low],
        ],
        p_halo,
        send_sem,
        recv_sem,
    )
    for copy in copies[2:] + copies[:2]:
        copy.start()

    def inner_fold(i, _):
        for tile in range(cols_dev // LANE):
            span = slice(tile * LANE, (tile + 1) * LANE)
            resid[i + HALO, :, span] = node_tile(acc, rows_dev, cols_dev, i, tile)
        return 0

    lax.fori_loop(HALO, rows_dev - HALO, inner_fold, 0)

    for load in loads:
        load.wait()
    sides = []
    for left, right, size in ((s_l, s_r, rows_dev), (s_dl, s_dr, 8), (s_ul, s_ur, 8)):
        sides.append((left[...], right[...], lane_ids((size, LANE))))
    for f in range(7):
        if f < 2:
            field[f, 3:8, 0:cols_dev] = s_dn[5 * f : 5 * f + 5, :]
            field[f, 8 + rows_dev : 12 + rows_dev, 0:cols_dev] = s_up[4 * f : 4 * f + 4, :]
        else:
            field[f, 7:8, 0:cols_dev] = s_dn[8 + f : 9 + f, :]
            if f >= 4:
                field[f, 8 + rows_dev : 9 + rows_dev, 0:cols_dev] = s_up[4 + f : 5 + f, :]
        wide, narrow = (5, 4) if f < 2 else (1, 0 if f < 4 else 1)
        back = 5 if f < 2 else 5
        made = []
        for left, right, lane in sides:
            from_l = pltpu.roll(left, LANE - back - 8 * f, 1)
            from_r = pltpu.roll(right, (LANE - 8 * f) % LANE, 1)
            made.append(
                jnp.where(lane >= LANE - wide, from_l, jnp.where(lane < narrow, from_r, 0.0))
            )
        field[f, 8 : 8 + rows_dev, cols_dev:width] = made[0]
        row8 = lax.broadcasted_iota(jnp.int32, (8, LANE), 0)
        under = row8 >= 8 - wide
        over = row8 < narrow
        field[f, 0:8, cols_dev:width] = jnp.where(under, made[1], 0.0)
        field[f, 8 + rows_dev : tall, cols_dev:width] = jnp.where(over, made[2], 0.0)

    shape = (tall, width)
    row = lax.broadcasted_iota(jnp.int32, shape, 0) - 8 + lax.axis_index("new") * rows_dev
    lane = lax.broadcasted_iota(jnp.int32, shape, 1)
    col = jnp.where(lane < cols_dev + 64, lane, lane - width) + lax.axis_index("old") * cols_dev
    valid = (row >= 0) & (row < n_rows - 1) & (col >= 0) & (col < n_cols - 1)

    def from_left(x):
        return pltpu.roll(x, 1, 1)

    def from_right(x):
        return pltpu.roll(x, width - 1, 1)

    def from_below(x):
        return pltpu.roll(x, 1, 0)

    def from_above(x):
        return pltpu.roll(x, tall - 1, 0)

    area_low = jnp.where(valid, field[0], 0.0)
    area_up = jnp.where(valid, field[1], 0.0)
    field[2] = field[2] * area_low
    field[3] = field[3] * area_up
    lower, upper = area_low / 12.0, area_up / 12.0
    both = lower + upper
    lower_left, upper_below = from_left(lower), from_below(upper)
    weight = both + lower_left + upper_below + from_below(from_left(both))
    inv = jnp.where(weight > 0.0, 1.0 / (2.0 * weight), 0.0)
    inv_right = from_right(inv)
    east, north = lower + upper_below, upper + lower_left
    coef[0] = inv * (1.0 / 3.0)
    coef[1] = inv * north
    coef[2] = inv * from_below(north)
    coef[3] = from_left(inv * east)
    coef[4] = from_left(inv * both)
    coef[5] = inv_right * east
    coef[6] = inv_right * from_below(both)
    vol_low, vol_up = field[2], field[3]
    mass[...] = (
        vol_low
        + vol_up
        + from_left(vol_low)
        + from_below(vol_up)
        + from_below(from_left(vol_low + vol_up))
    ) * (1.0 / 3.0)
    mem[...] = jnp.zeros_like(mem)

    centre = 0.5 * (EIG_HIGH + EIG_LOW)
    half_width = 0.5 * (EIG_HIGH - EIG_LOW)
    ratio_eig = centre / half_width
    edge = lane_ids((channels, LANE))

    def widen(inner, ends, left, right, place):
        ends = pltpu.roll(ends, lax.rem(2 * LANE - 4 - 8 * place, LANE), 1)
        left = pltpu.roll(left, lax.rem(2 * LANE - 4 - 8 * place, LANE), 1)
        right = pltpu.roll(right, lax.rem(LANE - 8 * place, LANE), 1)
        first = inner[:, 0:LANE] + jnp.where(edge == 0, left, 0.0)
        last = jnp.where(
            edge >= LANE - HALO,
            left,
            jnp.where(edge < HALO, right + jnp.where(edge == 0, ends, 0.0), 0.0),
        )
        return jnp.concatenate([first, inner[:, LANE:], last], axis=1)

    def begin(e, rhs):
        scaled = rhs * coef[0, pl.ds(e + 4, 1), :]
        resid[e] = scaled
        first_sum[e] = scaled * (1.0 / centre)

    def own(i):
        i = jnp.int32(i)
        tile = i // 16
        return widen(resid[i + HALO, :, 0:cols_dev], p_own[tile], p_l[tile], p_r[tile], i % 16)

    def under(k):
        i = rows_dev - HALO + k
        tile = i // 16 - (rows_dev - 1) // 16
        return widen(p_dn[k], p_d[tile], p_dl[tile], p_dr[tile], jnp.int32(i % 16))

    def over(k):
        return widen(p_up[k], p_u[0], p_ul[0], p_ur[0], jnp.int32(k))

    rhos = [1.0 / ratio_eig]
    for _ in range(ITERS):
        rhos.append(1.0 / (2.0 * ratio_eig - rhos[-1]))
    iterates = [first_sum, total]

    def sweep_row(sweep, e):
        keep = rhos[sweep + 1] * rhos[sweep]
        gain = 2.0 * rhos[sweep + 1] / half_width
        final = sweep == ITERS - 1
        source, other = iterates[sweep % 2], iterates[(sweep + 1) % 2]
        k = [coef[c, pl.ds(e + 4, 1), :] for c in range(1, 7)]
        through = None
        for group in range(0, channels, 8):
            at = slice(group, group + 8)
            here, up, down = source[e, at, :], source[e + 1, at, :], source[e - 1, at, :]
            to_left = k[2] * here + k[3] * up
            to_right = k[4] * here + k[5] * down
            left = resid[e, at, :] - (
                (k[0] * up + k[1] * down)
                + (pltpu.roll(to_left, width - 1, 1) + pltpu.roll(to_right, 1, 1))
            )
            new = (1.0 + keep - gain) * here + gain * left
            if sweep > 0:
                new = new - keep * other[e, at, :]
            other[e, at, :] = new
            if final:
                through = new if through is None else through + new
        if final:
            through = through * (1.0 / POINTS)
            for at, value in enumerate((0, 1, 5, 7)):
                mem[at, pl.ds(e + 4, 1), :] = through[value : value + 1, :]

    for copy in copies[2:]:
        copy.wait()

    def inner_row(i, _):
        begin(i + HALO, own(i))
        return 0

    lax.fori_loop(1, rows_dev, inner_row, 0)
    for sweep in range(ITERS):

        def inner_sweep(e, _, sweep=sweep):
            sweep_row(sweep, e)
            return 0

        lax.fori_loop(HALO + 2 + sweep, rows_dev + HALO - 1 - sweep, inner_sweep, 0)

    for copy in copies[:2]:
        copy.wait()
    for e in range(HALO):
        begin(e, under(e))
    begin(HALO, own(0) + under(HALO))
    begin(rows_dev + HALO, own(rows_dev) + over(0))
    for e in range(1, HALO):
        begin(rows_dev + HALO + e, over(e))
    for sweep in range(ITERS):
        def outer_sweep(k, _, sweep=sweep):
            low_end = HALO + 1
            sweep_row(
                sweep,
                jnp.where(k < low_end, 1 + sweep + k, rows_dev + HALO - 1 - sweep + k - low_end),
            )
            return 0

        lax.fori_loop(0, 2 * HALO + 1, outer_sweep, 0)

    anchor = [field[4 + c] for c in range(3)]
    beside = [from_right(x) for x in anchor]
    upward = [from_above(x) for x in anchor]
    across = [from_above(x) for x in beside]
    m_anchor = [mem[c] for c in range(4)]
    m_beside = [from_right(x) for x in m_anchor]
    m_upward = [from_above(x) for x in m_anchor]
    m_across = [from_above(x) for x in m_beside]
    third = 1.0 / 3.0
    m_low = [(a + b + x) * third for a, b, x in zip(m_anchor, m_beside, m_across)]
    m_up = [(a + x + u) * third for a, x, u in zip(m_anchor, m_across, m_upward)]
    low_x = [b - a for a, b in zip(anchor, beside)]
    low_y = [x - b for b, x in zip(beside, across)]
    up_x = [x - u for u, x in zip(upward, across)]
    up_y = [u - a for a, u in zip(anchor, upward)]
    low_x[0], up_x[0] = 1.0 + low_x[0], 1.0 + up_x[0]
    low_y[1], up_y[1] = 1.0 + low_y[1], 1.0 + up_y[1]
    piola_lx, piola_ly = first_piola(low_x, low_y, m_low)
    piola_ux, piola_uy = first_piola(up_x, up_y, m_up)
    vol_low, vol_up = field[2], field[3]
    node_mass = mass[8 : 8 + rows_dev, 0:cols_dev]
    for c in range(3):
        f_beside = -vol_low * (piola_lx[c] - piola_ly[c])
        f_across_low = -vol_low * piola_ly[c]
        f_across_up = -vol_up * piola_ux[c]
        f_upward = -vol_up * (piola_uy[c] - piola_ux[c])
        f_anchor = -(f_beside + f_across_low) - (f_across_up + f_upward)
        force = (
            f_anchor
            + from_left(f_beside)
            + from_below(f_upward)
            + from_below(from_left(f_across_low + f_across_up))
        )
        speed_up = force[8 : 8 + rows_dev, 0:cols_dev] / node_mass
        speed[c] = speed_up + GRAVITY if c == 2 else speed_up


def sheet(acc, rims, fields, halo, n_rows, n_cols):
    rows_dev, cols_dev = fields[0].shape[1:]
    width = cols_dev + LANE
    tall, long = rows_dev + 16, rows_dev + 2 * HALO
    tiles, channels, _ = rims[2].shape

    def scratch(*shape):
        return pltpu.VMEM(shape, jnp.float32)

    block = scratch(long, channels, width)
    part_halo = [rims[0].shape, rims[1].shape, rims[2].shape, rims[3].shape]
    part_halo += [(2, channels, LANE)] * 2 + [(1, channels, LANE)] * 2
    part_halo += [(2, channels, LANE), (1, channels, LANE)]
    return pl.pallas_call(
        functools.partial(sheet_kernel, n_rows, n_cols),
        out_shape=(
            block,
            scratch(3, rows_dev, cols_dev),
        ),
        in_specs=[VMEM] + [HBM] * 15,
        out_specs=(VMEM, VMEM),
        scratch_shapes=[scratch(*shape) for shape in part_halo]
        + [scratch(*x.shape) for x in halo]
        + [
            block,
            block,
            scratch(7, tall, width),
            scratch(4, tall, width),
            scratch(tall, width),
            scratch(7, tall, width),
            scratch(tiles, channels, LANE),
            pltpu.SemaphoreType.DMA((14,)),
            pltpu.SemaphoreType.DMA((10,)),
            pltpu.SemaphoreType.DMA((10,)),
        ],
        compiler_params=pltpu.CompilerParams(
            vmem_limit_bytes=24 * MIB, collective_id=2, has_side_effects=True
        ),
        name="sheet",
    )(acc, *rims, *fields, *halo)


def finish_kernel(total, speed_up, velocity, out, vel_out):
    channels, rows, cols = out.shape
    here = pl.ds(HALO + pl.program_id(0) * rows, rows)
    for channel in range(channels):
        out[channel] = total[here, channel, 0:cols]
    vel_out[...] = velocity[...] + TIME_STEP * speed_up[...]


def finish(total, speed_up, velocity):
    channels = total.shape[1]
    rows_dev, cols_dev = velocity.shape[1:]

    def plane(count):
        return pl.BlockSpec((count, 8, cols_dev), lambda i: (0, i, 0))

    return pl.pallas_call(
        finish_kernel,
        grid=(rows_dev // 8,),
        out_shape=(
            jax.ShapeDtypeStruct((channels, rows_dev, cols_dev), jnp.float32),
            jax.ShapeDtypeStruct(velocity.shape, jnp.float32),
        ),
        in_specs=[VMEM, plane(3), plane(3)],
        out_specs=(plane(channels), plane(3)),
        compiler_params=pltpu.CompilerParams(vmem_limit_bytes=40 * MIB),
        name="finish",
    )(total, speed_up, velocity)


def local(
    old_values,
    pair_rows,
    pair_targets,
    pair_weights,
    pair_counts,
    cell_area,
    thickness,
    displacement,
    velocity,
):
    rows_dev, cols_dev = cell_area.shape[1:]
    n_old, n_new = lax.axis_size("old"), lax.axis_size("new")
    arrived, ids, halo, acc = send(
        pair_counts,
        pair_rows,
        pair_targets,
        pair_weights,
        old_values,
        cell_area,
        thickness,
        displacement,
    )
    *rims, acc = scatter(ids, arrived, acc, rows_dev, cols_dev)
    fields = (cell_area, thickness, displacement)
    acc = pltpu.with_memory_space_constraint(acc, pltpu.VMEM)
    total, speed_up = sheet(acc, rims, fields, halo, n_new * rows_dev, n_old * cols_dev)
    return finish(total, speed_up, velocity)


def solution(mesh):
    return jax.shard_map(
        local,
        mesh=mesh,
        in_specs=(
            P(None, ("old", "new")),
            P(("old", "new"), None, None),
            P(("old", "new"), None, None),
            P(("old", "new"), None, None),
            P(("old", "new"), None),
            P(None, "new", "old"),
            P(None, "new", "old"),
            P(None, "new", "old"),
            P(None, "new", "old"),
        ),
        out_specs=(P(None, "new", "old"), P(None, "new", "old")),
        check_vma=False,
    )
```

```python
import functools

import jax
import jax.numpy as jnp
from jax import lax
from jax.experimental import pallas as pl
from jax.experimental.pallas import tpu as pltpu
from jax.sharding import PartitionSpec as P

POINTS = 4
COMP = 8
ITERS = 3
MU_BASE = 10.0
LAMBDA_BULK = 20.0
PRESTRESS = 4.0
TIME_STEP = 1.0
GRAVITY = -1.0
EIG_LOW = 0.5
EIG_HIGH = 2.0

LANE = 128
FRONT = 8
BATCH = 4
HALO = 4
STRIDE = 37
UNROLL = 4
MESH = pl.DeviceIdType.MESH
MIB = 1024 * 1024

VMEM = pl.BlockSpec(memory_space=pltpu.VMEM)
SMEM = pl.BlockSpec(memory_space=pltpu.SMEM)
HBM = pl.BlockSpec(memory_space=pltpu.HBM)


def rows_loop(start, stop, one_row, unroll=UNROLL):
    steps = (stop - start) // unroll

    def some(step, _):
        for k in range(unroll):
            one_row(start + step * unroll + k)
        return 0

    lax.fori_loop(0, steps, some, 0)
    for i in range(start + steps * unroll, stop):
        one_row(jnp.int32(i))


def lane_ids(shape):
    return lax.broadcasted_iota(jnp.int32, shape, len(shape) - 1)


def neighbours():
    n_old, n_new = lax.axis_size("old"), lax.axis_size("new")
    old, new = lax.axis_index("old"), lax.axis_index("new")
    left, right = lax.rem(old + n_old - 1, n_old), lax.rem(old + 1, n_old)
    below, above = lax.rem(new + n_new - 1, n_new), lax.rem(new + 1, n_new)
    return [
        (old, above),
        (old, below),
        (right, new),
        (left, new),
        (right, above),
        (left, above),
        (right, below),
        (left, below),
    ]


def to_neighbours(sources, targets, send_sem, recv_sem):
    around = neighbours()
    return [
        pltpu.make_async_remote_copy(
            src_ref=source,
            dst_ref=target,
            send_sem=send_sem.at[at],
            recv_sem=recv_sem.at[at],
            device_id=device,
            device_id_type=MESH,
        )
        for at, (source, target, device) in enumerate(zip(sources, targets, around + around))
    ]


def send_kernel(
    rows_dev,
    cols_dev,
    counts,
    rows_in,
    targets_in,
    weights_in,
    values_in,
    area,
    thick,
    shift_in,
    arrived,
    arrived_ids,
    s_dn,
    s_up,
    s_l,
    s_r,
    s_dl,
    s_dr,
    s_ul,
    s_ur,
    acc,
    table,
    picked,
    ids,
    notes,
    weights_flat,
    targets,
    weights_raw,
    values,
    rim_low,
    rim_high,
    rim_left,
    rim_right,
    pack_up,
    pack_down,
    pack_right,
    pack_left,
    rows,
    weights,
    local_sem,
    pair_sem,
    near_send,
    near_recv,
):
    n_old, n_new = lax.axis_size("old"), lax.axis_size("new")
    old, new = lax.axis_index("old"), lax.axis_index("new")
    ranks, payload, _ = picked.shape
    slots = payload * 4
    total = values.shape[1]
    me = old * n_new + new
    top, low = pl.ds(rows_dev - 8, 8), pl.ds(0, 8)
    near, far = pl.ds(0, LANE), pl.ds(cols_dev - LANE, LANE)

    loads = [
        (targets_in, targets),
        (weights_in, weights_raw),
        (values_in, values),
        (rows_in, rows),
    ]
    for source, at, count in ((area, 0, 2), (thick, 2, 2), (shift_in, 4, 3)):
        into = pl.ds(at, count)
        loads.append((source.at[:, top, :], rim_high.at[into]))
        loads.append((source.at[:, low, :], rim_low.at[into]))
        loads.append((source.at[:, :, far], rim_right.at[into]))
        loads.append((source.at[:, :, near], rim_left.at[into]))
    loads = [
        pltpu.make_async_copy(source, target, local_sem.at[at])
        for at, (source, target) in enumerate(loads)
    ]
    for load in loads:
        load.start()

    barrier = pltpu.get_barrier_semaphore()

    def greet(step, _):
        other = lax.rem(me + step, ranks)
        pl.semaphore_signal(
            barrier, inc=1, device_id=(other // n_new, other % n_new), device_id_type=MESH
        )
        return 0

    lax.fori_loop(1, ranks, greet, 0)

    slot = lane_ids((ranks, slots))
    owner = lax.broadcasted_iota(jnp.int32, (ranks, slots), 0)
    count = jnp.broadcast_to(counts[...].astype(jnp.float32), (ranks, ranks)).T.astype(jnp.int32)
    loads[0].wait()
    loads[1].wait()
    target = targets[0]
    cell, col = target // cols_dev, target % cols_dev
    outside = ((owner % n_new == n_new - 1) & (cell % rows_dev == rows_dev - 1)) | (
        (owner // n_new == n_old - 1) & (col == cols_dev - 1)
    )
    used = (slot < count) & jnp.logical_not(outside)
    weights_flat[...] = jnp.where(used, weights_raw[0], 0.0)
    load_weights = pltpu.make_async_copy(weights_flat, weights, local_sem.at[len(loads)])
    load_weights.start()
    spare = slot // 4 % FRONT
    where_to = jnp.where(used, FRONT + target, spare)
    clash = jnp.zeros((ranks, slots), jnp.int32)
    for gap in range(1, BATCH):
        same = (where_to == pltpu.roll(where_to, 4 * gap, 1)) & (slot % (4 * BATCH) >= 4 * gap)
        clash = clash | same.astype(jnp.int32)
    found = jnp.broadcast_to(jnp.max(clash, axis=1, keepdims=True), (ranks, slots))
    notes[:, 0:slots] = jnp.where(clash > 0, spare, where_to)
    notes[:, slots : 2 * slots] = jnp.where(slot == 0, found, clash * where_to)

    unroll = 8
    loads[2].wait()

    def flip(step, _):
        for at in range(unroll):
            start = pl.multiple_of((step * unroll + at) * LANE, LANE)
            part = values[:, pl.ds(start, LANE)]
            table[pl.ds(start, LANE), :] = jnp.concatenate([part] * 4, axis=0).T
        return 0

    lax.fori_loop(0, total // (LANE * unroll), flip, 0)

    for load in loads[3:]:
        load.wait()
    pack_up[...] = jnp.zeros_like(pack_up)
    pack_down[...] = jnp.zeros_like(pack_down)
    lane = lane_ids((rows_dev, LANE))
    to_right = jnp.zeros((rows_dev, LANE), jnp.float32)
    to_left = jnp.zeros((rows_dev, LANE), jnp.float32)
    for f in range(7):
        if f < 2:
            pack_up[5 * f : 5 * f + 5, :] = rim_high[f, 3:8, :]
            pack_down[4 * f : 4 * f + 4, :] = rim_low[f, 0:4, :]
        else:
            pack_up[8 + f : 9 + f, :] = rim_high[f, 7:8, :]
            if f >= 4:
                pack_down[4 + f : 5 + f, :] = rim_low[f, 0:1, :]
        mine = lane // 8 == f
        to_right = jnp.where(mine, pltpu.roll(rim_right[f], 8 * f + 5, 1), to_right)
        to_left = jnp.where(mine, pltpu.roll(rim_left[f], 8 * f, 1), to_left)
    pack_right[...] = to_right
    pack_left[...] = to_left
    load_weights.wait()
    pl.semaphore_wait(barrier, ranks - 1)

    halo = to_neighbours(
        [
            pack_up,
            pack_down,
            pack_right,
            pack_left,
            pack_right.at[top],
            pack_left.at[top],
            pack_right.at[low],
            pack_left.at[low],
        ],
        [s_dn, s_up, s_l, s_r, s_dl, s_dr, s_ul, s_ur],
        near_send,
        near_recv,
    )
    for copy in halo:
        copy.start()

    lane = lane_ids((1, LANE))
    first, second, third = lane < 32, lane < 64, lane < 96

    def fill(owner):
        for row in range(payload):
            part = [
                table[pl.ds(rows[0, owner, row * 4 + g], 1), :] * weights[owner, row * 4 + g]
                for g in range(4)
            ]
            merged = jnp.where(
                first, part[0], jnp.where(second, part[1], jnp.where(third, part[2], part[3]))
            )
            picked[owner, pl.ds(row, 1), :] = merged
        ids[owner] = notes[pl.ds(owner, 1), :]

    chunk = (acc.shape[0] - 2 * FRONT) // ranks

    def clear(step):
        start = pl.multiple_of(FRONT + step * chunk, 8)
        acc[pl.ds(start, chunk), :] = jnp.zeros((chunk, LANE), jnp.float32)

    for end in (0, acc.shape[0] - FRONT):
        acc[pl.ds(end, FRONT), :] = jnp.zeros((FRONT, LANE), jnp.float32)
    clear(0)

    def one_owner(step, _):
        shift = lax.rem(step * STRIDE, ranks)
        to_old = lax.rem(old + shift // n_new, n_old)
        to_new = lax.rem(new + shift % n_new, n_new)
        owner = to_old * n_new + to_new
        fill(owner)
        clear(step)
        for at, (source, target) in enumerate(((picked, arrived), (ids, arrived_ids))):
            pltpu.make_async_remote_copy(
                src_ref=source.at[owner],
                dst_ref=target.at[me],
                send_sem=pair_sem.at[2 * at],
                recv_sem=pair_sem.at[2 * at + 1],
                device_id=(to_old, to_new),
                device_id_type=MESH,
            ).start()
        return 0

    lax.fori_loop(1, ranks, one_owner, 0)
    fill(me)
    for at, (source, target) in enumerate(((picked, arrived), (ids, arrived_ids))):
        pltpu.make_async_copy(source.at[me], target.at[me], pair_sem.at[2 * at + 1]).start()
    for copy in halo:
        copy.wait()
    for at, (source, target) in enumerate(((picked, arrived), (ids, arrived_ids))):
        rest = pl.ds(0, ranks - 1)
        pltpu.make_async_copy(source.at[rest], source.at[rest], pair_sem.at[2 * at]).wait()
        pltpu.make_async_copy(source, target, pair_sem.at[2 * at + 1]).wait()


def send(counts, rows, targets, weights, values, area, thick, shift):
    ranks, slots = rows.shape[1:]
    payload = slots // 4
    rows_dev, cols_dev = area.shape[1:]
    halo = [(16, cols_dev)] * 2 + [(rows_dev, LANE)] * 2 + [(8, LANE)] * 4
    shapes = [jax.ShapeDtypeStruct(shape, jnp.float32) for shape in halo]
    shapes.insert(0, jax.ShapeDtypeStruct((ranks, payload, LANE), jnp.float32))
    shapes.insert(1, jax.ShapeDtypeStruct((ranks, 1, 2 * slots), jnp.int32))
    shapes.append(pltpu.VMEM((2 * FRONT + 2 * rows_dev * cols_dev, LANE), jnp.float32))

    def scratch(*shape):
        return pltpu.VMEM(shape, jnp.float32)

    result = pl.pallas_call(
        functools.partial(send_kernel, rows_dev, cols_dev),
        out_shape=tuple(shapes),
        in_specs=[VMEM] + [HBM] * 7,
        out_specs=(HBM,) * (len(shapes) - 1) + (VMEM,),
        scratch_shapes=[
            scratch(values.shape[1], LANE),
            scratch(ranks, payload, LANE),
            pltpu.VMEM((ranks, 1, 2 * slots), jnp.int32),
            pltpu.VMEM((ranks, 2 * slots), jnp.int32),
            scratch(ranks, slots),
            pltpu.VMEM(targets.shape, jnp.int32),
            scratch(*weights.shape),
            scratch(*values.shape),
            scratch(7, 8, cols_dev),
            scratch(7, 8, cols_dev),
            scratch(7, rows_dev, LANE),
            scratch(7, rows_dev, LANE),
            scratch(16, cols_dev),
            scratch(16, cols_dev),
            scratch(rows_dev, LANE),
            scratch(rows_dev, LANE),
            pltpu.SMEM(rows.shape, jnp.int32),
            pltpu.SMEM((ranks, slots), jnp.float32),
            pltpu.SemaphoreType.DMA((17,)),
            pltpu.SemaphoreType.DMA((4,)),
            pltpu.SemaphoreType.DMA((8,)),
            pltpu.SemaphoreType.DMA((8,)),
        ],
        compiler_params=pltpu.CompilerParams(
            vmem_limit_bytes=24 * MIB, collective_id=1, has_side_effects=True
        ),
        name="send",
    )(counts, rows, targets, weights, values, area, thick, shift)
    return result[0], result[1], result[2:-1], result[-1]


def fold(total):
    flipped = total.T
    return (flipped[0:32] + flipped[32:64]) + (flipped[64:96] + flipped[96:128])


def node_parts(acc, rows_dev, cols_dev, i, first, size, cells, below):
    upper = rows_dev * cols_dev
    base = i * cols_dev + (FRONT + first)
    here, left = [], []
    if cells:
        here += [base, base + upper]
        left += [base - 1]
    if below:
        here += [base + upper - cols_dev]
        left += [base - cols_dev - 1, base + upper - cols_dev - 1]
    here, left = ([acc[pl.ds(at, size), :] for at in some] for some in (here, left))
    return functools.reduce(jnp.add, here), functools.reduce(jnp.add, left)


def node_tile(acc, rows_dev, cols_dev, i, tile, cells=True, below=True):
    here, left = node_parts(acc, rows_dev, cols_dev, i, tile * LANE, LANE, cells, below)
    if tile == 0:
        rows = lax.broadcasted_iota(jnp.int32, (LANE, LANE), 0)
        left = jnp.where(rows == 0, 0.0, left)
    return fold(here + left)


def scatter_kernel(
    rows_dev,
    cols_dev,
    ids_in,
    data_in,
    _,
    rim_high,
    rim_low,
    cols_right,
    cols_left,
    acc,
    flat_right,
    flat_left,
    data,
    ids,
    ids_sem,
    data_sem,
):
    ranks, payload, _ = data.shape
    slots = payload * 4
    quarter = ranks // 4
    loads = []
    for at in range(4):
        some = pl.ds(at * quarter, quarter)
        for source, target, sem in ((ids_in, ids, ids_sem), (data_in, data, data_sem)):
            loads.append(pltpu.make_async_copy(source.at[some], target.at[some], sem.at[at]))
    for load in loads:
        load.start()
    flat_right[...] = jnp.zeros_like(flat_right)
    flat_left[...] = jnp.zeros_like(flat_left)

    lane = lane_ids((1, LANE))
    masks = [lane // 32 == g for g in range(4)]

    def add_rows(source, first):
        where_to = [ids[source, 0, first * 4 + k] for k in range(4 * BATCH)]
        new = [data[source, pl.ds(first + r, 1), :] for r in range(BATCH)]
        old = [acc[pl.ds(row, 1), :] for row in where_to]
        for k, (row, have) in enumerate(zip(where_to, old)):
            pltpu.store(acc.at[pl.ds(row, 1), :], have + new[k // 4], mask=masks[k % 4])

    def one_source(source, _):
        for first in range(0, payload, BATCH):
            add_rows(source, first)
        return 0

    for at in range(4):
        loads[2 * at].wait()
        loads[2 * at + 1].wait()
        lax.fori_loop(at * quarter, (at + 1) * quarter, one_source, 0)

    def late(source, _):
        def one_slot(k, _):
            row = ids[source, 0, slots + k]

            @pl.when(row > 0)
            def _():
                new = data[source, pl.ds(k // 4, 1), :]
                acc[pl.ds(row, 1), :] += jnp.where(lane // 32 == k % 4, new, 0.0)

            return 0

        def eight_slots(some, _):
            noted = sum(ids[source, 0, slots + some * 8 + k] for k in range(8))

            @pl.when(noted > 0)
            def _():
                lax.fori_loop(jnp.maximum(some * 8, 1), some * 8 + 8, one_slot, 0)

            return 0

        @pl.when(ids[source, 0, slots] > 0)
        def _():
            lax.fori_loop(0, slots // 8, eight_slots, 0)

        return 0

    def late_group(group, _):
        found = sum(ids[group * 8 + k, 0, slots] for k in range(8))

        @pl.when(found > 0)
        def _():
            lax.fori_loop(group * 8, group * 8 + 8, late, 0)

        return 0

    lax.fori_loop(0, ranks // 8, late_group, 0)

    tiles = cols_dev // LANE
    for at in range(HALO):
        for tile in range(tiles):
            span = slice(tile * LANE, (tile + 1) * LANE)
            rim_low[at, :, span] = node_tile(acc, rows_dev, cols_dev, at, tile, True, at > 0)
    for at in range(HALO + 1):
        i = rows_dev - HALO + at
        for tile in range(tiles):
            span = slice(tile * LANE, (tile + 1) * LANE)
            rim_high[at, :, span] = node_tile(acc, rows_dev, cols_dev, i, tile, i < rows_dev)

    row8 = lax.broadcasted_iota(jnp.int32, (8, LANE), 0)

    def rim_columns(i, cells, below):
        into = pl.ds(pl.multiple_of(i * 8, 8), 8)
        here, left = node_parts(acc, rows_dev, cols_dev, i, cols_dev - HALO, 8, cells, below)
        flat_right[into, :] = jnp.where(row8 < HALO, here, 0.0) + jnp.where(
            row8 < HALO + 1, left, 0.0
        )
        here, left = node_parts(acc, rows_dev, cols_dev, i, 0, 8, cells, below)
        flat_left[into, :] = jnp.where(
            row8 < HALO, here + jnp.where(row8 > 0, left, 0.0), 0.0
        )

    def inner_columns(i, _):
        rim_columns(i, True, True)
        return 0

    rim_columns(jnp.int32(0), True, False)
    lax.fori_loop(1, rows_dev, inner_columns, 0)
    rim_columns(jnp.int32(rows_dev), False, True)
    for tile in range(cols_right.shape[0]):
        span = slice(tile * LANE, (tile + 1) * LANE)
        cols_right[tile] = fold(flat_right[span, :])
        cols_left[tile] = fold(flat_left[span, :])


def scatter(ids, data, acc, rows_dev, cols_dev):
    channels = LANE // 4
    tiles = rows_dev // 16 + 1
    shapes = [(HALO + 1, channels, cols_dev), (HALO, channels, cols_dev)]
    shapes += [(tiles, channels, LANE)] * 2
    return pl.pallas_call(
        functools.partial(scatter_kernel, rows_dev, cols_dev),
        out_shape=tuple(jax.ShapeDtypeStruct(shape, jnp.float32) for shape in shapes)
        + (pltpu.VMEM(acc.shape, jnp.float32),),
        in_specs=[HBM, HBM, VMEM],
        out_specs=(VMEM,) * 5,
        input_output_aliases={2: 4},
        scratch_shapes=[
            pltpu.VMEM((tiles * LANE, LANE), jnp.float32),
            pltpu.VMEM((tiles * LANE, LANE), jnp.float32),
            pltpu.VMEM(data.shape, jnp.float32),
            pltpu.SMEM(ids.shape, jnp.int32),
            pltpu.SemaphoreType.DMA((4,)),
            pltpu.SemaphoreType.DMA((4,)),
        ],
        compiler_params=pltpu.CompilerParams(vmem_limit_bytes=24 * MIB),
        name="scatter",
    )(ids, data, acc)


def first_piola(stretch_x, stretch_y, fields):
    gram_xx = sum(x * x for x in stretch_x)
    gram_xy = sum(x * y for x, y in zip(stretch_x, stretch_y))
    gram_yy = sum(y * y for y in stretch_y)
    determinant = gram_xx * gram_yy - gram_xy * gram_xy
    inverse = 1.0 / determinant
    inv_xx = gram_yy * inverse
    inv_xy = -gram_xy * inverse
    inv_yy = gram_xx * inverse
    shear_mod = MU_BASE * (1.5 + jnp.tanh(fields[3]))
    bulk = LAMBDA_BULK * 0.5 * jnp.log(determinant)
    piola_x, piola_y = [], []
    for along_x, along_y in zip(stretch_x, stretch_y):
        push_x = along_x * inv_xx + along_y * inv_xy
        push_y = along_x * inv_xy + along_y * inv_yy
        piola_x.append(
            shear_mod * (along_x - push_x)
            + bulk * push_x
            + PRESTRESS * (along_x * fields[0] + along_y * fields[2])
        )
        piola_y.append(
            shear_mod * (along_y - push_y)
            + bulk * push_y
            + PRESTRESS * (along_x * fields[2] + along_y * fields[1])
        )
    return piola_x, piola_y


def sheet_kernel(n_rows, n_cols, *refs):
    acc, rim_high, rim_low, cols_right, cols_left, area_in, thick_in, shift_in = refs[:8]
    s_in = refs[8:16]
    total, speed = refs[16:18]
    p_halo, s_halo, refs = refs[18:28], refs[28:36], refs[36:]
    resid, first_sum, field, mem, mass, coef, p_own = refs[:7]
    load_sem, send_sem, recv_sem = refs[7:]
    p_dn, p_up, p_l, p_r, p_dl, p_dr, p_ul, p_ur, p_d, p_u = p_halo
    s_dn, s_up, s_l, s_r, s_dl, s_dr, s_ul, s_ur = s_halo
    rows_dev, cols_dev = area_in.shape[1:]
    channels, width = resid.shape[1:]
    tall = rows_dev + 16
    middle, main = pl.ds(8, rows_dev), pl.ds(0, cols_dev)

    barrier = pltpu.get_barrier_semaphore()
    for device in neighbours():
        pl.semaphore_signal(barrier, inc=1, device_id=device, device_id_type=MESH)

    field[:, 0:8, :] = jnp.zeros((7, 8, width), jnp.float32)
    field[:, 8 + rows_dev : tall, :] = jnp.zeros((7, 8, width), jnp.float32)
    loads = [
        (area_in, field.at[pl.ds(0, 2), middle, main]),
        (thick_in, field.at[pl.ds(2, 2), middle, main]),
        (shift_in, field.at[pl.ds(4, 3), middle, main]),
    ] + list(zip(s_in, s_halo))
    loads += [
        (cols_right, p_own),
        (rim_low, resid.at[pl.ds(HALO, HALO), :, main]),
        (rim_high, resid.at[pl.ds(rows_dev, HALO + 1), :, main]),
    ]
    loads = [
        pltpu.make_async_copy(source, target, load_sem.at[at])
        for at, (source, target) in enumerate(loads)
    ]
    for load in loads:
        load.start()

    tiles_high, tiles_low = pl.ds((rows_dev - 1) // 16, 2), pl.ds(0, 1)
    pl.semaphore_wait(barrier, 8)
    copies = to_neighbours(
        [
            rim_high,
            rim_low,
            cols_right,
            cols_left,
            cols_right.at[tiles_high],
            cols_left.at[tiles_high],
            cols_right.at[tiles_low],
            cols_left.at[tiles_low],
            cols_right.at[tiles_high],
            cols_right.at[tiles_low],
        ],
        p_halo,
        send_sem,
        recv_sem,
    )
    for copy in copies[2:] + copies[:2]:
        copy.start()

    def inner_fold(i):
        for tile in range(cols_dev // LANE):
            span = slice(tile * LANE, (tile + 1) * LANE)
            resid[i + HALO, :, span] = node_tile(acc, rows_dev, cols_dev, i, tile)

    rows_loop(HALO, rows_dev - HALO, inner_fold, 2)

    for load in loads:
        load.wait()
    sides = []
    for left, right, size in ((s_l, s_r, rows_dev), (s_dl, s_dr, 8), (s_ul, s_ur, 8)):
        sides.append((left[...], right[...], lane_ids((size, LANE))))
    for f in range(7):
        if f < 2:
            field[f, 3:8, 0:cols_dev] = s_dn[5 * f : 5 * f + 5, :]
            field[f, 8 + rows_dev : 12 + rows_dev, 0:cols_dev] = s_up[4 * f : 4 * f + 4, :]
        else:
            field[f, 7:8, 0:cols_dev] = s_dn[8 + f : 9 + f, :]
            if f >= 4:
                field[f, 8 + rows_dev : 9 + rows_dev, 0:cols_dev] = s_up[4 + f : 5 + f, :]
        wide, narrow = (5, 4) if f < 2 else (1, 0 if f < 4 else 1)
        back = 5 if f < 2 else 5
        made = []
        for left, right, lane in sides:
            from_l = pltpu.roll(left, LANE - back - 8 * f, 1)
            from_r = pltpu.roll(right, (LANE - 8 * f) % LANE, 1)
            made.append(
                jnp.where(lane >= LANE - wide, from_l, jnp.where(lane < narrow, from_r, 0.0))
            )
        field[f, 8 : 8 + rows_dev, cols_dev:width] = made[0]
        row8 = lax.broadcasted_iota(jnp.int32, (8, LANE), 0)
        under = row8 >= 8 - wide
        over = row8 < narrow
        field[f, 0:8, cols_dev:width] = jnp.where(under, made[1], 0.0)
        field[f, 8 + rows_dev : tall, cols_dev:width] = jnp.where(over, made[2], 0.0)

    shape = (tall, width)
    row = lax.broadcasted_iota(jnp.int32, shape, 0) - 8 + lax.axis_index("new") * rows_dev
    lane = lax.broadcasted_iota(jnp.int32, shape, 1)
    col = jnp.where(lane < cols_dev + 64, lane, lane - width) + lax.axis_index("old") * cols_dev
    valid = (row >= 0) & (row < n_rows - 1) & (col >= 0) & (col < n_cols - 1)

    def from_left(x):
        return pltpu.roll(x, 1, 1)

    def from_right(x):
        return pltpu.roll(x, width - 1, 1)

    def from_below(x):
        return pltpu.roll(x, 1, 0)

    def from_above(x):
        return pltpu.roll(x, tall - 1, 0)

    area_low = jnp.where(valid, field[0], 0.0)
    area_up = jnp.where(valid, field[1], 0.0)
    field[2] = field[2] * area_low
    field[3] = field[3] * area_up
    lower, upper = area_low / 12.0, area_up / 12.0
    both = lower + upper
    lower_left, upper_below = from_left(lower), from_below(upper)
    weight = both + lower_left + upper_below + from_below(from_left(both))
    inv = jnp.where(weight > 0.0, 1.0 / (2.0 * weight), 0.0)
    inv_right = from_right(inv)
    east, north = lower + upper_below, upper + lower_left
    coef[0] = inv * (1.0 / 3.0)
    coef[1] = inv * north
    coef[2] = inv * from_below(north)
    coef[3] = from_left(inv * east)
    coef[4] = from_left(inv * both)
    coef[5] = inv_right * east
    coef[6] = inv_right * from_below(both)
    vol_low, vol_up = field[2], field[3]
    mass[...] = (
        vol_low
        + vol_up
        + from_left(vol_low)
        + from_below(vol_up)
        + from_below(from_left(vol_low + vol_up))
    ) * (1.0 / 3.0)
    mem[...] = jnp.zeros_like(mem)

    centre = 0.5 * (EIG_HIGH + EIG_LOW)
    half_width = 0.5 * (EIG_HIGH - EIG_LOW)
    ratio_eig = centre / half_width
    edge = lane_ids((channels, LANE))

    def widen(inner, ends, left, right, place):
        ends = pltpu.roll(ends, lax.rem(2 * LANE - 4 - 8 * place, LANE), 1)
        left = pltpu.roll(left, lax.rem(2 * LANE - 4 - 8 * place, LANE), 1)
        right = pltpu.roll(right, lax.rem(LANE - 8 * place, LANE), 1)
        first = inner[:, 0:LANE] + jnp.where(edge == 0, left, 0.0)
        last = jnp.where(
            edge >= LANE - HALO,
            left,
            jnp.where(edge < HALO, right + jnp.where(edge == 0, ends, 0.0), 0.0),
        )
        return jnp.concatenate([first, inner[:, LANE:], last], axis=1)

    def begin(e, rhs):
        scaled = rhs * coef[0, pl.ds(e + 4, 1), :]
        resid[e] = scaled
        first_sum[e] = scaled * (1.0 / centre)

    def own(i):
        i = jnp.int32(i)
        tile = i // 16
        return widen(resid[i + HALO, :, 0:cols_dev], p_own[tile], p_l[tile], p_r[tile], i % 16)

    def under(k):
        i = rows_dev - HALO + k
        tile = i // 16 - (rows_dev - 1) // 16
        return widen(p_dn[k], p_d[tile], p_dl[tile], p_dr[tile], jnp.int32(i % 16))

    def over(k):
        return widen(p_up[k], p_u[0], p_ul[0], p_ur[0], jnp.int32(k))

    rhos = [1.0 / ratio_eig]
    for _ in range(ITERS):
        rhos.append(1.0 / (2.0 * ratio_eig - rhos[-1]))
    iterates = [first_sum, total]
    lane8 = lane_ids((8, LANE))
    first_lane, last_lane = lane8 == 0, lane8 == LANE - 1

    def sweep_row(sweep, e):
        keep = rhos[sweep + 1] * rhos[sweep]
        gain = 2.0 * rhos[sweep + 1] / half_width
        final = sweep == ITERS - 1
        source, other = iterates[sweep % 2], iterates[(sweep + 1) % 2]
        k_row = [coef[c, pl.ds(e + 4, 1), :] for c in range(1, 7)]
        tiles, groups = width // LANE, range(channels // 8)
        rest = [[None] * tiles for _ in groups]
        west = [[None] * tiles for _ in groups]
        east = [[None] * tiles for _ in groups]
        sums = [None] * tiles

        def close(t):
            span = slice(t * LANE, (t + 1) * LANE)
            for g in groups:
                from_east = jnp.where(last_lane, east[g][(t + 1) % tiles], east[g][t])
                from_west = jnp.where(first_lane, west[g][t - 1], west[g][t])
                new = rest[g][t] - gain * (from_east + from_west)
                other[e, 8 * g : 8 * g + 8, span] = new
                if final:
                    sums[t] = new if g == 0 else sums[t] + new

        for t in range(tiles):
            span = slice(t * LANE, (t + 1) * LANE)
            k = [jnp.broadcast_to(x[:, span], (8, LANE)) for x in k_row]
            for g in groups:
                at = slice(8 * g, 8 * g + 8)
                here, up, down = source[e, at, span], source[e + 1, at, span], source[e - 1, at, span]
                east[g][t] = pltpu.roll(k[2] * here + k[3] * up, LANE - 1, 1)
                west[g][t] = pltpu.roll(k[4] * here + k[5] * down, 1, 1)
                kept = (1.0 + keep - gain) * here
                kept = kept + gain * (resid[e, at, span] - (k[0] * up + k[1] * down))
                rest[g][t] = kept if sweep == 0 else kept - keep * other[e, at, span]
            if t > 1:
                close(t - 1)
        close(tiles - 1)
        close(0)
        if final:
            through = jnp.concatenate(sums, axis=1) * (1.0 / POINTS)
            for at, value in enumerate((0, 1, 5, 7)):
                mem[at, pl.ds(e + 4, 1), :] = through[value : value + 1, :]

    for copy in copies[2:]:
        copy.wait()

    rows_loop(1, rows_dev, lambda i: begin(i + HALO, own(i)))
    for sweep in range(ITERS):
        rows_loop(
            HALO + 2 + sweep, rows_dev + HALO - 1 - sweep, functools.partial(sweep_row, sweep)
        )

    for copy in copies[:2]:
        copy.wait()
    for e in range(HALO):
        begin(e, under(e))
    begin(HALO, own(0) + under(HALO))
    begin(rows_dev + HALO, own(rows_dev) + over(0))
    for e in range(1, HALO):
        begin(rows_dev + HALO + e, over(e))
    for sweep in range(ITERS):
        def outer_row(k, sweep=sweep):
            low_end = HALO + 1
            sweep_row(
                sweep,
                jnp.where(k < low_end, 1 + sweep + k, rows_dev + HALO - 1 - sweep + k - low_end),
            )

        rows_loop(0, 2 * HALO + 1, outer_row, 3)

    anchor = [field[4 + c] for c in range(3)]
    beside = [from_right(x) for x in anchor]
    upward = [from_above(x) for x in anchor]
    across = [from_above(x) for x in beside]
    m_anchor = [mem[c] for c in range(4)]
    m_beside = [from_right(x) for x in m_anchor]
    m_upward = [from_above(x) for x in m_anchor]
    m_across = [from_above(x) for x in m_beside]
    third = 1.0 / 3.0
    m_low = [(a + b + x) * third for a, b, x in zip(m_anchor, m_beside, m_across)]
    m_up = [(a + x + u) * third for a, x, u in zip(m_anchor, m_across, m_upward)]
    low_x = [b - a for a, b in zip(anchor, beside)]
    low_y = [x - b for b, x in zip(beside, across)]
    up_x = [x - u for u, x in zip(upward, across)]
    up_y = [u - a for a, u in zip(anchor, upward)]
    low_x[0], up_x[0] = 1.0 + low_x[0], 1.0 + up_x[0]
    low_y[1], up_y[1] = 1.0 + low_y[1], 1.0 + up_y[1]
    piola_lx, piola_ly = first_piola(low_x, low_y, m_low)
    piola_ux, piola_uy = first_piola(up_x, up_y, m_up)
    vol_low, vol_up = field[2], field[3]
    node_mass = mass[8 : 8 + rows_dev, 0:cols_dev]
    for c in range(3):
        f_beside = -vol_low * (piola_lx[c] - piola_ly[c])
        f_across_low = -vol_low * piola_ly[c]
        f_across_up = -vol_up * piola_ux[c]
        f_upward = -vol_up * (piola_uy[c] - piola_ux[c])
        f_anchor = -(f_beside + f_across_low) - (f_across_up + f_upward)
        force = (
            f_anchor
            + from_left(f_beside)
            + from_below(f_upward)
            + from_below(from_left(f_across_low + f_across_up))
        )
        speed_up = force[8 : 8 + rows_dev, 0:cols_dev] / node_mass
        speed[c] = speed_up + GRAVITY if c == 2 else speed_up


def sheet(acc, rims, fields, halo, n_rows, n_cols):
    rows_dev, cols_dev = fields[0].shape[1:]
    width = cols_dev + LANE
    tall, long = rows_dev + 16, rows_dev + 2 * HALO
    tiles, channels, _ = rims[2].shape

    def scratch(*shape):
        return pltpu.VMEM(shape, jnp.float32)

    block = scratch(long, channels, width)
    part_halo = [rims[0].shape, rims[1].shape, rims[2].shape, rims[3].shape]
    part_halo += [(2, channels, LANE)] * 2 + [(1, channels, LANE)] * 2
    part_halo += [(2, channels, LANE), (1, channels, LANE)]
    return pl.pallas_call(
        functools.partial(sheet_kernel, n_rows, n_cols),
        out_shape=(
            block,
            scratch(3, rows_dev, cols_dev),
        ),
        in_specs=[VMEM] + [HBM] * 15,
        out_specs=(VMEM, VMEM),
        scratch_shapes=[scratch(*shape) for shape in part_halo]
        + [scratch(*x.shape) for x in halo]
        + [
            block,
            block,
            scratch(7, tall, width),
            scratch(4, tall, width),
            scratch(tall, width),
            scratch(7, tall, width),
            scratch(tiles, channels, LANE),
            pltpu.SemaphoreType.DMA((14,)),
            pltpu.SemaphoreType.DMA((10,)),
            pltpu.SemaphoreType.DMA((10,)),
        ],
        compiler_params=pltpu.CompilerParams(
            vmem_limit_bytes=24 * MIB, collective_id=2, has_side_effects=True
        ),
        name="sheet",
    )(acc, *rims, *fields, *halo)


def finish_kernel(total, speed_up, velocity, out, vel_out):
    channels, rows, cols = out.shape
    here = pl.ds(HALO + pl.program_id(0) * rows, rows)
    for channel in range(channels):
        out[channel] = total[here, channel, 0:cols]
    vel_out[...] = velocity[...] + TIME_STEP * speed_up[...]


def finish(total, speed_up, velocity):
    channels = total.shape[1]
    rows_dev, cols_dev = velocity.shape[1:]

    def plane(count):
        return pl.BlockSpec((count, 8, cols_dev), lambda i: (0, i, 0))

    return pl.pallas_call(
        finish_kernel,
        grid=(rows_dev // 8,),
        out_shape=(
            jax.ShapeDtypeStruct((channels, rows_dev, cols_dev), jnp.float32),
            jax.ShapeDtypeStruct(velocity.shape, jnp.float32),
        ),
        in_specs=[VMEM, plane(3), plane(3)],
        out_specs=(plane(channels), plane(3)),
        compiler_params=pltpu.CompilerParams(vmem_limit_bytes=40 * MIB),
        name="finish",
    )(total, speed_up, velocity)


def local(
    old_values,
    pair_rows,
    pair_targets,
    pair_weights,
    pair_counts,
    cell_area,
    thickness,
    displacement,
    velocity,
):
    rows_dev, cols_dev = cell_area.shape[1:]
    n_old, n_new = lax.axis_size("old"), lax.axis_size("new")
    arrived, ids, halo, acc = send(
        pair_counts,
        pair_rows,
        pair_targets,
        pair_weights,
        old_values,
        cell_area,
        thickness,
        displacement,
    )
    *rims, acc = scatter(ids, arrived, acc, rows_dev, cols_dev)
    fields = (cell_area, thickness, displacement)
    acc = pltpu.with_memory_space_constraint(acc, pltpu.VMEM)
    total, speed_up = sheet(acc, rims, fields, halo, n_new * rows_dev, n_old * cols_dev)
    return finish(total, speed_up, velocity)


def solution(mesh):
    return jax.shard_map(
        local,
        mesh=mesh,
        in_specs=(
            P(None, ("old", "new")),
            P(("old", "new"), None, None),
            P(("old", "new"), None, None),
            P(("old", "new"), None, None),
            P(("old", "new"), None),
            P(None, "new", "old"),
            P(None, "new", "old"),
            P(None, "new", "old"),
            P(None, "new", "old"),
        ),
        out_specs=(P(None, "new", "old"), P(None, "new", "old")),
        check_vma=False,
    )
```

```python
import functools

import jax
import jax.numpy as jnp
from jax import lax
from jax.experimental import pallas as pl
from jax.experimental.pallas import tpu as pltpu
from jax.sharding import PartitionSpec as P

POINTS = 4
COMP = 8
ITERS = 3
MU_BASE = 10.0
LAMBDA_BULK = 20.0
PRESTRESS = 4.0
TIME_STEP = 1.0
GRAVITY = -1.0
EIG_LOW = 0.5
EIG_HIGH = 2.0

LANE = 128
FRONT = 8
BATCH = 4
HALO = 4
STRIDE = 37
UNROLL = 4
MESH = pl.DeviceIdType.MESH
MIB = 1024 * 1024

VMEM = pl.BlockSpec(memory_space=pltpu.VMEM)
SMEM = pl.BlockSpec(memory_space=pltpu.SMEM)
HBM = pl.BlockSpec(memory_space=pltpu.HBM)


def rows_loop(start, stop, one_row, unroll=UNROLL):
    steps = (stop - start) // unroll

    def some(step, _):
        for k in range(unroll):
            one_row(start + step * unroll + k)
        return 0

    lax.fori_loop(0, steps, some, 0)
    for i in range(start + steps * unroll, stop):
        one_row(jnp.int32(i))


def lane_ids(shape):
    return lax.broadcasted_iota(jnp.int32, shape, len(shape) - 1)


def shifters(tall, width):
    def from_left(x):
        return pltpu.roll(x, 1, 1)

    def from_right(x):
        return pltpu.roll(x, width - 1, 1)

    def from_below(x):
        return pltpu.roll(x, 1, 0)

    def from_above(x):
        return pltpu.roll(x, tall - 1, 0)

    return from_left, from_right, from_below, from_above


def cell_planes(n_rows, n_cols, field, coef, mass, s_halo):
    s_dn, s_up, s_l, s_r, s_dl, s_dr, s_ul, s_ur = s_halo
    tall, width = mass.shape
    rows_dev, cols_dev = tall - 16, width - LANE
    sides = []
    for left, right, size in ((s_l, s_r, rows_dev), (s_dl, s_dr, 8), (s_ul, s_ur, 8)):
        sides.append((left[...], right[...], lane_ids((size, LANE))))
    for f in range(7):
        if f < 2:
            field[f, 3:8, 0:cols_dev] = s_dn[5 * f : 5 * f + 5, :]
            field[f, 8 + rows_dev : 12 + rows_dev, 0:cols_dev] = s_up[4 * f : 4 * f + 4, :]
        else:
            field[f, 7:8, 0:cols_dev] = s_dn[8 + f : 9 + f, :]
            if f >= 4:
                field[f, 8 + rows_dev : 9 + rows_dev, 0:cols_dev] = s_up[4 + f : 5 + f, :]
        wide, narrow = (5, 4) if f < 2 else (1, 0 if f < 4 else 1)
        back = 5 if f < 2 else 5
        made = []
        for left, right, lane in sides:
            from_l = pltpu.roll(left, LANE - back - 8 * f, 1)
            from_r = pltpu.roll(right, (LANE - 8 * f) % LANE, 1)
            made.append(
                jnp.where(lane >= LANE - wide, from_l, jnp.where(lane < narrow, from_r, 0.0))
            )
        field[f, 8 : 8 + rows_dev, cols_dev:width] = made[0]
        row8 = lax.broadcasted_iota(jnp.int32, (8, LANE), 0)
        under = row8 >= 8 - wide
        over = row8 < narrow
        field[f, 0:8, cols_dev:width] = jnp.where(under, made[1], 0.0)
        field[f, 8 + rows_dev : tall, cols_dev:width] = jnp.where(over, made[2], 0.0)

    shape = (tall, width)
    row = lax.broadcasted_iota(jnp.int32, shape, 0) - 8 + lax.axis_index("new") * rows_dev
    lane = lax.broadcasted_iota(jnp.int32, shape, 1)
    col = jnp.where(lane < cols_dev + 64, lane, lane - width) + lax.axis_index("old") * cols_dev
    valid = (row >= 0) & (row < n_rows - 1) & (col >= 0) & (col < n_cols - 1)

    from_left, from_right, from_below, _ = shifters(tall, width)
    area_low = jnp.where(valid, field[0], 0.0)
    area_up = jnp.where(valid, field[1], 0.0)
    field[2] = field[2] * area_low
    field[3] = field[3] * area_up
    lower, upper = area_low / 12.0, area_up / 12.0
    both = lower + upper
    lower_left, upper_below = from_left(lower), from_below(upper)
    weight = both + lower_left + upper_below + from_below(from_left(both))
    inv = jnp.where(weight > 0.0, 1.0 / (2.0 * weight), 0.0)
    inv_right = from_right(inv)
    east, north = lower + upper_below, upper + lower_left
    coef[0] = inv * (1.0 / 3.0)
    coef[1] = inv * north
    coef[2] = inv * from_below(north)
    coef[3] = from_left(inv * east)
    coef[4] = from_left(inv * both)
    coef[5] = inv_right * east
    coef[6] = inv_right * from_below(both)
    vol_low, vol_up = field[2], field[3]
    mass[...] = (
        vol_low
        + vol_up
        + from_left(vol_low)
        + from_below(vol_up)
        + from_below(from_left(vol_low + vol_up))
    ) * (1.0 / 3.0)


def neighbours():
    n_old, n_new = lax.axis_size("old"), lax.axis_size("new")
    old, new = lax.axis_index("old"), lax.axis_index("new")
    left, right = lax.rem(old + n_old - 1, n_old), lax.rem(old + 1, n_old)
    below, above = lax.rem(new + n_new - 1, n_new), lax.rem(new + 1, n_new)
    return [
        (old, above),
        (old, below),
        (right, new),
        (left, new),
        (right, above),
        (left, above),
        (right, below),
        (left, below),
    ]


def to_neighbours(sources, targets, send_sem, recv_sem):
    around = neighbours()
    return [
        pltpu.make_async_remote_copy(
            src_ref=source,
            dst_ref=target,
            send_sem=send_sem.at[at],
            recv_sem=recv_sem.at[at],
            device_id=device,
            device_id_type=MESH,
        )
        for at, (source, target, device) in enumerate(zip(sources, targets, around + around))
    ]


def send_kernel(
    rows_dev,
    cols_dev,
    counts,
    rows_in,
    targets_in,
    weights_in,
    values_in,
    area,
    thick,
    shift_in,
    arrived,
    arrived_ids,
    field_out,
    coef_out,
    mass_out,
    acc,
    s_dn,
    s_up,
    s_l,
    s_r,
    s_dl,
    s_dr,
    s_ul,
    s_ur,
    field,
    coef,
    mass,
    table,
    picked,
    ids,
    notes,
    weights_flat,
    targets,
    weights_raw,
    values,
    rim_low,
    rim_high,
    rim_left,
    rim_right,
    pack_up,
    pack_down,
    pack_right,
    pack_left,
    rows,
    weights,
    local_sem,
    pair_sem,
    near_send,
    near_recv,
):
    n_old, n_new = lax.axis_size("old"), lax.axis_size("new")
    old, new = lax.axis_index("old"), lax.axis_index("new")
    ranks, payload, _ = picked.shape
    slots = payload * 4
    total = values.shape[1]
    me = old * n_new + new
    top, low = pl.ds(rows_dev - 8, 8), pl.ds(0, 8)
    near, far = pl.ds(0, LANE), pl.ds(cols_dev - LANE, LANE)

    loads = [
        (targets_in, targets),
        (weights_in, weights_raw),
        (values_in, values),
        (rows_in, rows),
    ]
    for source, at, count in ((area, 0, 2), (thick, 2, 2), (shift_in, 4, 3)):
        into = pl.ds(at, count)
        loads.append((source.at[:, top, :], rim_high.at[into]))
        loads.append((source.at[:, low, :], rim_low.at[into]))
        loads.append((source.at[:, :, far], rim_right.at[into]))
        loads.append((source.at[:, :, near], rim_left.at[into]))
        inner = field.at[into, pl.ds(8, rows_dev), pl.ds(0, cols_dev)]
        loads.append((source, inner))
    loads = [
        pltpu.make_async_copy(source, target, local_sem.at[at])
        for at, (source, target) in enumerate(loads)
    ]
    tall = rows_dev + 16
    field[:, 0:8, :] = jnp.zeros((7, 8, cols_dev + LANE), jnp.float32)
    field[:, 8 + rows_dev : tall, :] = jnp.zeros((7, 8, cols_dev + LANE), jnp.float32)
    for load in loads:
        load.start()

    barrier = pltpu.get_barrier_semaphore()

    def greet(step, _):
        other = lax.rem(me + step, ranks)
        pl.semaphore_signal(
            barrier, inc=1, device_id=(other // n_new, other % n_new), device_id_type=MESH
        )
        return 0

    lax.fori_loop(1, ranks, greet, 0)

    slot = lane_ids((ranks, slots))
    owner = lax.broadcasted_iota(jnp.int32, (ranks, slots), 0)
    count = jnp.broadcast_to(counts[...].astype(jnp.float32), (ranks, ranks)).T.astype(jnp.int32)
    loads[0].wait()
    loads[1].wait()
    target = targets[0]
    cell, col = target // cols_dev, target % cols_dev
    outside = ((owner % n_new == n_new - 1) & (cell % rows_dev == rows_dev - 1)) | (
        (owner // n_new == n_old - 1) & (col == cols_dev - 1)
    )
    used = (slot < count) & jnp.logical_not(outside)
    weights_flat[...] = jnp.where(used, weights_raw[0], 0.0)
    load_weights = pltpu.make_async_copy(weights_flat, weights, local_sem.at[len(loads)])
    load_weights.start()
    spare = slot // 4 % FRONT
    where_to = jnp.where(used, FRONT + target, spare)
    clash = jnp.zeros((ranks, slots), jnp.int32)
    for gap in range(1, BATCH):
        same = (where_to == pltpu.roll(where_to, 4 * gap, 1)) & (slot % (4 * BATCH) >= 4 * gap)
        clash = clash | same.astype(jnp.int32)
    found = jnp.broadcast_to(jnp.max(clash, axis=1, keepdims=True), (ranks, slots))
    notes[:, 0:slots] = jnp.where(clash > 0, spare, where_to)
    notes[:, slots : 2 * slots] = jnp.where(slot == 0, found, clash * where_to)

    unroll = 8
    loads[2].wait()

    def flip(step, _):
        for at in range(unroll):
            start = pl.multiple_of((step * unroll + at) * LANE, LANE)
            part = values[:, pl.ds(start, LANE)]
            table[pl.ds(start, LANE), :] = jnp.concatenate([part] * 4, axis=0).T
        return 0

    lax.fori_loop(0, total // (LANE * unroll), flip, 0)

    for load in loads[3:]:
        load.wait()
    pack_up[...] = jnp.zeros_like(pack_up)
    pack_down[...] = jnp.zeros_like(pack_down)
    lane = lane_ids((rows_dev, LANE))
    to_right = jnp.zeros((rows_dev, LANE), jnp.float32)
    to_left = jnp.zeros((rows_dev, LANE), jnp.float32)
    for f in range(7):
        if f < 2:
            pack_up[5 * f : 5 * f + 5, :] = rim_high[f, 3:8, :]
            pack_down[4 * f : 4 * f + 4, :] = rim_low[f, 0:4, :]
        else:
            pack_up[8 + f : 9 + f, :] = rim_high[f, 7:8, :]
            if f >= 4:
                pack_down[4 + f : 5 + f, :] = rim_low[f, 0:1, :]
        mine = lane // 8 == f
        to_right = jnp.where(mine, pltpu.roll(rim_right[f], 8 * f + 5, 1), to_right)
        to_left = jnp.where(mine, pltpu.roll(rim_left[f], 8 * f, 1), to_left)
    pack_right[...] = to_right
    pack_left[...] = to_left
    load_weights.wait()
    pl.semaphore_wait(barrier, ranks - 1)

    halo = to_neighbours(
        [
            pack_up,
            pack_down,
            pack_right,
            pack_left,
            pack_right.at[top],
            pack_left.at[top],
            pack_right.at[low],
            pack_left.at[low],
        ],
        [s_dn, s_up, s_l, s_r, s_dl, s_dr, s_ul, s_ur],
        near_send,
        near_recv,
    )
    for copy in halo:
        copy.start()

    lane = lane_ids((1, LANE))
    first, second, third = lane < 32, lane < 64, lane < 96

    def fill(owner):
        for row in range(payload):
            part = [
                table[pl.ds(rows[0, owner, row * 4 + g], 1), :] * weights[owner, row * 4 + g]
                for g in range(4)
            ]
            merged = jnp.where(
                first, part[0], jnp.where(second, part[1], jnp.where(third, part[2], part[3]))
            )
            picked[owner, pl.ds(row, 1), :] = merged
        ids[owner] = notes[pl.ds(owner, 1), :]

    chunk = (acc.shape[0] - 2 * FRONT) // ranks

    def clear(step):
        start = pl.multiple_of(FRONT + step * chunk, 8)
        acc[pl.ds(start, chunk), :] = jnp.zeros((chunk, LANE), jnp.float32)

    for end in (0, acc.shape[0] - FRONT):
        acc[pl.ds(end, FRONT), :] = jnp.zeros((FRONT, LANE), jnp.float32)
    clear(0)

    def one_owner(step, _):
        shift = lax.rem(step * STRIDE, ranks)
        to_old = lax.rem(old + shift // n_new, n_old)
        to_new = lax.rem(new + shift % n_new, n_new)
        owner = to_old * n_new + to_new
        fill(owner)
        clear(step)
        for at, (source, target) in enumerate(((picked, arrived), (ids, arrived_ids))):
            pltpu.make_async_remote_copy(
                src_ref=source.at[owner],
                dst_ref=target.at[me],
                send_sem=pair_sem.at[2 * at],
                recv_sem=pair_sem.at[2 * at + 1],
                device_id=(to_old, to_new),
                device_id_type=MESH,
            ).start()
        return 0

    lax.fori_loop(1, ranks, one_owner, 0)
    fill(me)
    for at, (source, target) in enumerate(((picked, arrived), (ids, arrived_ids))):
        pltpu.make_async_copy(source.at[me], target.at[me], pair_sem.at[2 * at + 1]).start()
    for copy in halo:
        copy.wait()
    around = (s_dn, s_up, s_l, s_r, s_dl, s_dr, s_ul, s_ur)
    cell_planes(n_new * rows_dev, n_old * cols_dev, field, coef, mass, around)
    saves = [
        pltpu.make_async_copy(source, target, near_send.at[at])
        for at, (source, target) in enumerate(
            ((field.at[pl.ds(2, 5)], field_out), (coef, coef_out), (mass, mass_out))
        )
    ]
    for save in saves:
        save.start()
    for save in saves:
        save.wait()
    for at, (source, target) in enumerate(((picked, arrived), (ids, arrived_ids))):
        rest = pl.ds(0, ranks - 1)
        pltpu.make_async_copy(source.at[rest], source.at[rest], pair_sem.at[2 * at]).wait()
        pltpu.make_async_copy(source, target, pair_sem.at[2 * at + 1]).wait()


def send(counts, rows, targets, weights, values, area, thick, shift):
    ranks, slots = rows.shape[1:]
    payload = slots // 4
    rows_dev, cols_dev = area.shape[1:]
    halo = [(16, cols_dev)] * 2 + [(rows_dev, LANE)] * 2 + [(8, LANE)] * 4
    tall, width = rows_dev + 16, cols_dev + LANE
    shapes = [(ranks, payload, LANE), (5, tall, width), (7, tall, width), (tall, width)]
    shapes = [jax.ShapeDtypeStruct(shape, jnp.float32) for shape in shapes]
    shapes.insert(1, jax.ShapeDtypeStruct((ranks, 1, 2 * slots), jnp.int32))
    shapes.append(pltpu.VMEM((2 * FRONT + 2 * rows_dev * cols_dev, LANE), jnp.float32))

    def scratch(*shape):
        return pltpu.VMEM(shape, jnp.float32)

    result = pl.pallas_call(
        functools.partial(send_kernel, rows_dev, cols_dev),
        out_shape=tuple(shapes),
        in_specs=[VMEM] + [HBM] * 7,
        out_specs=(HBM,) * (len(shapes) - 1) + (VMEM,),
        scratch_shapes=[scratch(*shape) for shape in halo]
        + [
            scratch(7, tall, width),
            scratch(7, tall, width),
            scratch(tall, width),
            scratch(values.shape[1], LANE),
            scratch(ranks, payload, LANE),
            pltpu.VMEM((ranks, 1, 2 * slots), jnp.int32),
            pltpu.VMEM((ranks, 2 * slots), jnp.int32),
            scratch(ranks, slots),
            pltpu.VMEM(targets.shape, jnp.int32),
            scratch(*weights.shape),
            scratch(*values.shape),
            scratch(7, 8, cols_dev),
            scratch(7, 8, cols_dev),
            scratch(7, rows_dev, LANE),
            scratch(7, rows_dev, LANE),
            scratch(16, cols_dev),
            scratch(16, cols_dev),
            scratch(rows_dev, LANE),
            scratch(rows_dev, LANE),
            pltpu.SMEM(rows.shape, jnp.int32),
            pltpu.SMEM((ranks, slots), jnp.float32),
            pltpu.SemaphoreType.DMA((20,)),
            pltpu.SemaphoreType.DMA((4,)),
            pltpu.SemaphoreType.DMA((8,)),
            pltpu.SemaphoreType.DMA((8,)),
        ],
        compiler_params=pltpu.CompilerParams(
            vmem_limit_bytes=24 * MIB, collective_id=1, has_side_effects=True
        ),
        name="send",
    )(counts, rows, targets, weights, values, area, thick, shift)
    return result[0], result[1], result[2:-1], result[-1]


def fold(total):
    flipped = total.T
    return (flipped[0:32] + flipped[32:64]) + (flipped[64:96] + flipped[96:128])


def node_parts(acc, rows_dev, cols_dev, i, first, size, cells, below):
    upper = rows_dev * cols_dev
    base = i * cols_dev + (FRONT + first)
    here, left = [], []
    if cells:
        here += [base, base + upper]
        left += [base - 1]
    if below:
        here += [base + upper - cols_dev]
        left += [base - cols_dev - 1, base + upper - cols_dev - 1]
    here, left = ([acc[pl.ds(at, size), :] for at in some] for some in (here, left))
    return functools.reduce(jnp.add, here), functools.reduce(jnp.add, left)


def node_tile(acc, rows_dev, cols_dev, i, tile, cells=True, below=True):
    here, left = node_parts(acc, rows_dev, cols_dev, i, tile * LANE, LANE, cells, below)
    if tile == 0:
        rows = lax.broadcasted_iota(jnp.int32, (LANE, LANE), 0)
        left = jnp.where(rows == 0, 0.0, left)
    return fold(here + left)


def scatter_kernel(
    rows_dev,
    cols_dev,
    ids_in,
    data_in,
    _,
    rim_high,
    rim_low,
    cols_right,
    cols_left,
    acc,
    flat_right,
    flat_left,
    data,
    ids,
    ids_sem,
    data_sem,
):
    ranks, payload, _ = data.shape
    slots = payload * 4
    quarter = ranks // 4
    loads = []
    for at in range(4):
        some = pl.ds(at * quarter, quarter)
        for source, target, sem in ((ids_in, ids, ids_sem), (data_in, data, data_sem)):
            loads.append(pltpu.make_async_copy(source.at[some], target.at[some], sem.at[at]))
    for load in loads:
        load.start()
    flat_right[...] = jnp.zeros_like(flat_right)
    flat_left[...] = jnp.zeros_like(flat_left)

    lane = lane_ids((1, LANE))
    masks = [lane // 32 == g for g in range(4)]

    def add_rows(source, first):
        where_to = [ids[source, 0, first * 4 + k] for k in range(4 * BATCH)]
        new = [data[source, pl.ds(first + r, 1), :] for r in range(BATCH)]
        old = [acc[pl.ds(row, 1), :] for row in where_to]
        for k, (row, have) in enumerate(zip(where_to, old)):
            pltpu.store(acc.at[pl.ds(row, 1), :], have + new[k // 4], mask=masks[k % 4])

    def one_source(source, _):
        for first in range(0, payload, BATCH):
            add_rows(source, first)
        return 0

    for at in range(4):
        loads[2 * at].wait()
        loads[2 * at + 1].wait()
        lax.fori_loop(at * quarter, (at + 1) * quarter, one_source, 0)

    def late(source, _):
        def one_slot(k, _):
            row = ids[source, 0, slots + k]

            @pl.when(row > 0)
            def _():
                new = data[source, pl.ds(k // 4, 1), :]
                acc[pl.ds(row, 1), :] += jnp.where(lane // 32 == k % 4, new, 0.0)

            return 0

        def eight_slots(some, _):
            noted = sum(ids[source, 0, slots + some * 8 + k] for k in range(8))

            @pl.when(noted > 0)
            def _():
                lax.fori_loop(jnp.maximum(some * 8, 1), some * 8 + 8, one_slot, 0)

            return 0

        @pl.when(ids[source, 0, slots] > 0)
        def _():
            lax.fori_loop(0, slots // 8, eight_slots, 0)

        return 0

    def late_group(group, _):
        found = sum(ids[group * 8 + k, 0, slots] for k in range(8))

        @pl.when(found > 0)
        def _():
            lax.fori_loop(group * 8, group * 8 + 8, late, 0)

        return 0

    lax.fori_loop(0, ranks // 8, late_group, 0)

    tiles = cols_dev // LANE
    for at in range(HALO):
        for tile in range(tiles):
            span = slice(tile * LANE, (tile + 1) * LANE)
            rim_low[at, :, span] = node_tile(acc, rows_dev, cols_dev, at, tile, True, at > 0)
    for at in range(HALO + 1):
        i = rows_dev - HALO + at
        for tile in range(tiles):
            span = slice(tile * LANE, (tile + 1) * LANE)
            rim_high[at, :, span] = node_tile(acc, rows_dev, cols_dev, i, tile, i < rows_dev)

    row8 = lax.broadcasted_iota(jnp.int32, (8, LANE), 0)

    def rim_columns(i, cells, below):
        into = pl.ds(pl.multiple_of(i * 8, 8), 8)
        here, left = node_parts(acc, rows_dev, cols_dev, i, cols_dev - HALO, 8, cells, below)
        flat_right[into, :] = jnp.where(row8 < HALO, here, 0.0) + jnp.where(
            row8 < HALO + 1, left, 0.0
        )
        here, left = node_parts(acc, rows_dev, cols_dev, i, 0, 8, cells, below)
        flat_left[into, :] = jnp.where(
            row8 < HALO, here + jnp.where(row8 > 0, left, 0.0), 0.0
        )

    def inner_columns(i, _):
        rim_columns(i, True, True)
        return 0

    rim_columns(jnp.int32(0), True, False)
    lax.fori_loop(1, rows_dev, inner_columns, 0)
    rim_columns(jnp.int32(rows_dev), False, True)
    for tile in range(cols_right.shape[0]):
        span = slice(tile * LANE, (tile + 1) * LANE)
        cols_right[tile] = fold(flat_right[span, :])
        cols_left[tile] = fold(flat_left[span, :])


def scatter(ids, data, acc, rows_dev, cols_dev):
    channels = LANE // 4
    tiles = rows_dev // 16 + 1
    shapes = [(HALO + 1, channels, cols_dev), (HALO, channels, cols_dev)]
    shapes += [(tiles, channels, LANE)] * 2
    return pl.pallas_call(
        functools.partial(scatter_kernel, rows_dev, cols_dev),
        out_shape=tuple(jax.ShapeDtypeStruct(shape, jnp.float32) for shape in shapes)
        + (pltpu.VMEM(acc.shape, jnp.float32),),
        in_specs=[HBM, HBM, VMEM],
        out_specs=(VMEM,) * 5,
        input_output_aliases={2: 4},
        scratch_shapes=[
            pltpu.VMEM((tiles * LANE, LANE), jnp.float32),
            pltpu.VMEM((tiles * LANE, LANE), jnp.float32),
            pltpu.VMEM(data.shape, jnp.float32),
            pltpu.SMEM(ids.shape, jnp.int32),
            pltpu.SemaphoreType.DMA((4,)),
            pltpu.SemaphoreType.DMA((4,)),
        ],
        compiler_params=pltpu.CompilerParams(vmem_limit_bytes=24 * MIB),
        name="scatter",
    )(ids, data, acc)


def first_piola(stretch_x, stretch_y, fields):
    gram_xx = sum(x * x for x in stretch_x)
    gram_xy = sum(x * y for x, y in zip(stretch_x, stretch_y))
    gram_yy = sum(y * y for y in stretch_y)
    determinant = gram_xx * gram_yy - gram_xy * gram_xy
    inverse = 1.0 / determinant
    inv_xx = gram_yy * inverse
    inv_xy = -gram_xy * inverse
    inv_yy = gram_xx * inverse
    shear_mod = MU_BASE * (1.5 + jnp.tanh(fields[3]))
    bulk = LAMBDA_BULK * 0.5 * jnp.log(determinant)
    piola_x, piola_y = [], []
    for along_x, along_y in zip(stretch_x, stretch_y):
        push_x = along_x * inv_xx + along_y * inv_xy
        push_y = along_x * inv_xy + along_y * inv_yy
        piola_x.append(
            shear_mod * (along_x - push_x)
            + bulk * push_x
            + PRESTRESS * (along_x * fields[0] + along_y * fields[2])
        )
        piola_y.append(
            shear_mod * (along_y - push_y)
            + bulk * push_y
            + PRESTRESS * (along_x * fields[2] + along_y * fields[1])
        )
    return piola_x, piola_y


def sheet_kernel(*refs):
    acc, rim_high, rim_low, cols_right, cols_left, field_in, coef_in, mass_in = refs[:8]
    total, speed = refs[8:10]
    p_halo, refs = refs[10:20], refs[20:]
    resid, first_sum, field, mem, mass, coef, p_own = refs[:7]
    load_sem, send_sem, recv_sem = refs[7:]
    p_dn, p_up, p_l, p_r, p_dl, p_dr, p_ul, p_ur, p_d, p_u = p_halo
    channels, width = resid.shape[1:]
    tall = mass.shape[0]
    rows_dev, cols_dev = tall - 16, width - LANE
    main = pl.ds(0, cols_dev)
    from_left, from_right, from_below, from_above = shifters(tall, width)

    barrier = pltpu.get_barrier_semaphore()
    for device in neighbours():
        pl.semaphore_signal(barrier, inc=1, device_id=device, device_id_type=MESH)

    loads = [
        (field_in, field),
        (coef_in, coef),
        (mass_in, mass),
        (cols_right, p_own),
        (rim_low, resid.at[pl.ds(HALO, HALO), :, main]),
        (rim_high, resid.at[pl.ds(rows_dev, HALO + 1), :, main]),
    ]
    loads = [
        pltpu.make_async_copy(source, target, load_sem.at[at])
        for at, (source, target) in enumerate(loads)
    ]
    for load in loads:
        load.start()

    tiles_high, tiles_low = pl.ds((rows_dev - 1) // 16, 2), pl.ds(0, 1)
    pl.semaphore_wait(barrier, 8)
    copies = to_neighbours(
        [
            rim_high,
            rim_low,
            cols_right,
            cols_left,
            cols_right.at[tiles_high],
            cols_left.at[tiles_high],
            cols_right.at[tiles_low],
            cols_left.at[tiles_low],
            cols_right.at[tiles_high],
            cols_right.at[tiles_low],
        ],
        p_halo,
        send_sem,
        recv_sem,
    )
    for copy in copies[2:] + copies[:2]:
        copy.start()

    def inner_fold(i):
        for tile in range(cols_dev // LANE):
            span = slice(tile * LANE, (tile + 1) * LANE)
            resid[i + HALO, :, span] = node_tile(acc, rows_dev, cols_dev, i, tile)

    rows_loop(HALO, rows_dev - HALO, inner_fold, 2)

    for load in loads:
        load.wait()
    mem[...] = jnp.zeros_like(mem)

    centre = 0.5 * (EIG_HIGH + EIG_LOW)
    half_width = 0.5 * (EIG_HIGH - EIG_LOW)
    ratio_eig = centre / half_width
    edge = lane_ids((channels, LANE))

    def widen(inner, ends, left, right, place):
        ends = pltpu.roll(ends, lax.rem(2 * LANE - 4 - 8 * place, LANE), 1)
        left = pltpu.roll(left, lax.rem(2 * LANE - 4 - 8 * place, LANE), 1)
        right = pltpu.roll(right, lax.rem(LANE - 8 * place, LANE), 1)
        first = inner[:, 0:LANE] + jnp.where(edge == 0, left, 0.0)
        last = jnp.where(
            edge >= LANE - HALO,
            left,
            jnp.where(edge < HALO, right + jnp.where(edge == 0, ends, 0.0), 0.0),
        )
        return jnp.concatenate([first, inner[:, LANE:], last], axis=1)

    def begin(e, rhs):
        scaled = rhs * coef[0, pl.ds(e + 4, 1), :]
        resid[e] = scaled
        first_sum[e] = scaled * (1.0 / centre)

    def own(i):
        i = jnp.int32(i)
        tile = i // 16
        return widen(resid[i + HALO, :, 0:cols_dev], p_own[tile], p_l[tile], p_r[tile], i % 16)

    def under(k):
        i = rows_dev - HALO + k
        tile = i // 16 - (rows_dev - 1) // 16
        return widen(p_dn[k], p_d[tile], p_dl[tile], p_dr[tile], jnp.int32(i % 16))

    def over(k):
        return widen(p_up[k], p_u[0], p_ul[0], p_ur[0], jnp.int32(k))

    rhos = [1.0 / ratio_eig]
    for _ in range(ITERS):
        rhos.append(1.0 / (2.0 * ratio_eig - rhos[-1]))
    iterates = [first_sum, total]
    lane8 = lane_ids((8, LANE))
    first_lane, last_lane = lane8 == 0, lane8 == LANE - 1

    def sweep_row(sweep, e):
        keep = rhos[sweep + 1] * rhos[sweep]
        gain = 2.0 * rhos[sweep + 1] / half_width
        final = sweep == ITERS - 1
        source, other = iterates[sweep % 2], iterates[(sweep + 1) % 2]
        k_row = [coef[c, pl.ds(e + 4, 1), :] for c in range(1, 7)]
        tiles, groups = width // LANE, range(channels // 8)
        rest = [[None] * tiles for _ in groups]
        west = [[None] * tiles for _ in groups]
        east = [[None] * tiles for _ in groups]
        sums = [None] * tiles

        def close(t):
            span = slice(t * LANE, (t + 1) * LANE)
            for g in groups:
                from_east = jnp.where(last_lane, east[g][(t + 1) % tiles], east[g][t])
                from_west = jnp.where(first_lane, west[g][t - 1], west[g][t])
                new = rest[g][t] - gain * (from_east + from_west)
                other[e, 8 * g : 8 * g + 8, span] = new
                if final:
                    sums[t] = new if g == 0 else sums[t] + new

        for t in range(tiles):
            span = slice(t * LANE, (t + 1) * LANE)
            k = [jnp.broadcast_to(x[:, span], (8, LANE)) for x in k_row]
            for g in groups:
                at = slice(8 * g, 8 * g + 8)
                here, up, down = source[e, at, span], source[e + 1, at, span], source[e - 1, at, span]
                east[g][t] = pltpu.roll(k[2] * here + k[3] * up, LANE - 1, 1)
                west[g][t] = pltpu.roll(k[4] * here + k[5] * down, 1, 1)
                kept = (1.0 + keep - gain) * here
                kept = kept + gain * (resid[e, at, span] - (k[0] * up + k[1] * down))
                rest[g][t] = kept if sweep == 0 else kept - keep * other[e, at, span]
            if t > 1:
                close(t - 1)
        close(tiles - 1)
        close(0)
        if final:
            through = jnp.concatenate(sums, axis=1) * (1.0 / POINTS)
            for at, value in enumerate((0, 1, 5, 7)):
                mem[at, pl.ds(e + 4, 1), :] = through[value : value + 1, :]

    for copy in copies[2:]:
        copy.wait()

    rows_loop(1, rows_dev, lambda i: begin(i + HALO, own(i)))
    for sweep in range(ITERS):
        rows_loop(
            HALO + 2 + sweep, rows_dev + HALO - 1 - sweep, functools.partial(sweep_row, sweep)
        )

    for copy in copies[:2]:
        copy.wait()
    for e in range(HALO):
        begin(e, under(e))
    begin(HALO, own(0) + under(HALO))
    begin(rows_dev + HALO, own(rows_dev) + over(0))
    for e in range(1, HALO):
        begin(rows_dev + HALO + e, over(e))
    for sweep in range(ITERS):
        def outer_row(k, sweep=sweep):
            low_end = HALO + 1
            sweep_row(
                sweep,
                jnp.where(k < low_end, 1 + sweep + k, rows_dev + HALO - 1 - sweep + k - low_end),
            )

        rows_loop(0, 2 * HALO + 1, outer_row, 3)

    anchor = [field[2 + c] for c in range(3)]
    beside = [from_right(x) for x in anchor]
    upward = [from_above(x) for x in anchor]
    across = [from_above(x) for x in beside]
    m_anchor = [mem[c] for c in range(4)]
    m_beside = [from_right(x) for x in m_anchor]
    m_upward = [from_above(x) for x in m_anchor]
    m_across = [from_above(x) for x in m_beside]
    third = 1.0 / 3.0
    m_low = [(a + b + x) * third for a, b, x in zip(m_anchor, m_beside, m_across)]
    m_up = [(a + x + u) * third for a, x, u in zip(m_anchor, m_across, m_upward)]
    low_x = [b - a for a, b in zip(anchor, beside)]
    low_y = [x - b for b, x in zip(beside, across)]
    up_x = [x - u for u, x in zip(upward, across)]
    up_y = [u - a for a, u in zip(anchor, upward)]
    low_x[0], up_x[0] = 1.0 + low_x[0], 1.0 + up_x[0]
    low_y[1], up_y[1] = 1.0 + low_y[1], 1.0 + up_y[1]
    piola_lx, piola_ly = first_piola(low_x, low_y, m_low)
    piola_ux, piola_uy = first_piola(up_x, up_y, m_up)
    vol_low, vol_up = field[0], field[1]
    node_mass = mass[8 : 8 + rows_dev, 0:cols_dev]
    for c in range(3):
        f_beside = -vol_low * (piola_lx[c] - piola_ly[c])
        f_across_low = -vol_low * piola_ly[c]
        f_across_up = -vol_up * piola_ux[c]
        f_upward = -vol_up * (piola_uy[c] - piola_ux[c])
        f_anchor = -(f_beside + f_across_low) - (f_across_up + f_upward)
        force = (
            f_anchor
            + from_left(f_beside)
            + from_below(f_upward)
            + from_below(from_left(f_across_low + f_across_up))
        )
        speed_up = force[8 : 8 + rows_dev, 0:cols_dev] / node_mass
        speed[c] = speed_up + GRAVITY if c == 2 else speed_up


def sheet(acc, rims, planes):
    tall, width = planes[2].shape
    rows_dev, cols_dev = tall - 16, width - LANE
    long = rows_dev + 2 * HALO
    tiles, channels, _ = rims[2].shape

    def scratch(*shape):
        return pltpu.VMEM(shape, jnp.float32)

    block = scratch(long, channels, width)
    part_halo = [rims[0].shape, rims[1].shape, rims[2].shape, rims[3].shape]
    part_halo += [(2, channels, LANE)] * 2 + [(1, channels, LANE)] * 2
    part_halo += [(2, channels, LANE), (1, channels, LANE)]
    return pl.pallas_call(
        sheet_kernel,
        out_shape=(
            block,
            scratch(3, rows_dev, cols_dev),
        ),
        in_specs=[VMEM] + [HBM] * 7,
        out_specs=(VMEM, VMEM),
        scratch_shapes=[scratch(*shape) for shape in part_halo]
        + [
            block,
            block,
            scratch(5, tall, width),
            scratch(4, tall, width),
            scratch(tall, width),
            scratch(7, tall, width),
            scratch(tiles, channels, LANE),
            pltpu.SemaphoreType.DMA((6,)),
            pltpu.SemaphoreType.DMA((10,)),
            pltpu.SemaphoreType.DMA((10,)),
        ],
        compiler_params=pltpu.CompilerParams(
            vmem_limit_bytes=24 * MIB, collective_id=2, has_side_effects=True
        ),
        name="sheet",
    )(acc, *rims, *planes)


def finish_kernel(total, speed_up, velocity, out, vel_out):
    channels, rows, cols = out.shape
    here = pl.ds(HALO + pl.program_id(0) * rows, rows)
    for channel in range(channels):
        out[channel] = total[here, channel, 0:cols]
    vel_out[...] = velocity[...] + TIME_STEP * speed_up[...]


def finish(total, speed_up, velocity):
    channels = total.shape[1]
    rows_dev, cols_dev = velocity.shape[1:]

    def plane(count):
        return pl.BlockSpec((count, 8, cols_dev), lambda i: (0, i, 0))

    return pl.pallas_call(
        finish_kernel,
        grid=(rows_dev // 8,),
        out_shape=(
            jax.ShapeDtypeStruct((channels, rows_dev, cols_dev), jnp.float32),
            jax.ShapeDtypeStruct(velocity.shape, jnp.float32),
        ),
        in_specs=[VMEM, plane(3), plane(3)],
        out_specs=(plane(channels), plane(3)),
        compiler_params=pltpu.CompilerParams(vmem_limit_bytes=40 * MIB),
        name="finish",
    )(total, speed_up, velocity)


def local(
    old_values,
    pair_rows,
    pair_targets,
    pair_weights,
    pair_counts,
    cell_area,
    thickness,
    displacement,
    velocity,
):
    rows_dev, cols_dev = cell_area.shape[1:]
    arrived, ids, planes, acc = send(
        pair_counts,
        pair_rows,
        pair_targets,
        pair_weights,
        old_values,
        cell_area,
        thickness,
        displacement,
    )
    *rims, acc = scatter(ids, arrived, acc, rows_dev, cols_dev)
    acc = pltpu.with_memory_space_constraint(acc, pltpu.VMEM)
    total, speed_up = sheet(acc, rims, planes)
    return finish(total, speed_up, velocity)


def solution(mesh):
    return jax.shard_map(
        local,
        mesh=mesh,
        in_specs=(
            P(None, ("old", "new")),
            P(("old", "new"), None, None),
            P(("old", "new"), None, None),
            P(("old", "new"), None, None),
            P(("old", "new"), None),
            P(None, "new", "old"),
            P(None, "new", "old"),
            P(None, "new", "old"),
            P(None, "new", "old"),
        ),
        out_specs=(P(None, "new", "old"), P(None, "new", "old")),
        check_vma=False,
    )
```

```python
import functools

import jax
import jax.numpy as jnp
from jax import lax
from jax.experimental import pallas as pl
from jax.experimental.pallas import tpu as pltpu
from jax.sharding import PartitionSpec as P

POINTS = 4
COMP = 8
ITERS = 3
MU_BASE = 10.0
LAMBDA_BULK = 20.0
PRESTRESS = 4.0
TIME_STEP = 1.0
GRAVITY = -1.0
EIG_LOW = 0.5
EIG_HIGH = 2.0

LANE = 128
FRONT = 8
BATCH = 4
HALO = 4
STRIDE = 37
UNROLL = 4
MESH = pl.DeviceIdType.MESH
MIB = 1024 * 1024

VMEM = pl.BlockSpec(memory_space=pltpu.VMEM)
SMEM = pl.BlockSpec(memory_space=pltpu.SMEM)
HBM = pl.BlockSpec(memory_space=pltpu.HBM)


def rows_loop(start, stop, one_row, unroll=UNROLL):
    steps = (stop - start) // unroll

    def some(step, _):
        for k in range(unroll):
            one_row(start + step * unroll + k)
        return 0

    lax.fori_loop(0, steps, some, 0)
    for i in range(start + steps * unroll, stop):
        one_row(jnp.int32(i))


def lane_ids(shape):
    return lax.broadcasted_iota(jnp.int32, shape, len(shape) - 1)


def shifters(tall, width):
    def from_left(x):
        return pltpu.roll(x, 1, 1)

    def from_right(x):
        return pltpu.roll(x, width - 1, 1)

    def from_below(x):
        return pltpu.roll(x, 1, 0)

    def from_above(x):
        return pltpu.roll(x, tall - 1, 0)

    return from_left, from_right, from_below, from_above


def cell_planes(n_rows, n_cols, field, coef, mass, s_halo):
    s_dn, s_up, s_l, s_r, s_dl, s_dr, s_ul, s_ur = s_halo
    tall, width = mass.shape
    rows_dev, cols_dev = tall - 16, width - LANE
    sides = []
    for left, right, size in ((s_l, s_r, rows_dev), (s_dl, s_dr, 8), (s_ul, s_ur, 8)):
        sides.append((left[...], right[...], lane_ids((size, LANE))))
    for f in range(7):
        if f < 2:
            field[f, 3:8, 0:cols_dev] = s_dn[5 * f : 5 * f + 5, :]
            field[f, 8 + rows_dev : 12 + rows_dev, 0:cols_dev] = s_up[4 * f : 4 * f + 4, :]
        else:
            field[f, 7:8, 0:cols_dev] = s_dn[8 + f : 9 + f, :]
            if f >= 4:
                field[f, 8 + rows_dev : 9 + rows_dev, 0:cols_dev] = s_up[4 + f : 5 + f, :]
        wide, narrow = (5, 4) if f < 2 else (1, 0 if f < 4 else 1)
        back = 5 if f < 2 else 5
        made = []
        for left, right, lane in sides:
            from_l = pltpu.roll(left, LANE - back - 8 * f, 1)
            from_r = pltpu.roll(right, (LANE - 8 * f) % LANE, 1)
            made.append(
                jnp.where(lane >= LANE - wide, from_l, jnp.where(lane < narrow, from_r, 0.0))
            )
        field[f, 8 : 8 + rows_dev, cols_dev:width] = made[0]
        row8 = lax.broadcasted_iota(jnp.int32, (8, LANE), 0)
        under = row8 >= 8 - wide
        over = row8 < narrow
        field[f, 0:8, cols_dev:width] = jnp.where(under, made[1], 0.0)
        field[f, 8 + rows_dev : tall, cols_dev:width] = jnp.where(over, made[2], 0.0)

    shape = (tall, width)
    row = lax.broadcasted_iota(jnp.int32, shape, 0) - 8 + lax.axis_index("new") * rows_dev
    lane = lax.broadcasted_iota(jnp.int32, shape, 1)
    col = jnp.where(lane < cols_dev + 64, lane, lane - width) + lax.axis_index("old") * cols_dev
    valid = (row >= 0) & (row < n_rows - 1) & (col >= 0) & (col < n_cols - 1)

    from_left, from_right, from_below, _ = shifters(tall, width)
    area_low = jnp.where(valid, field[0], 0.0)
    area_up = jnp.where(valid, field[1], 0.0)
    field[2] = field[2] * area_low
    field[3] = field[3] * area_up
    lower, upper = area_low / 12.0, area_up / 12.0
    both = lower + upper
    lower_left, upper_below = from_left(lower), from_below(upper)
    weight = both + lower_left + upper_below + from_below(from_left(both))
    inv = jnp.where(weight > 0.0, 1.0 / (2.0 * weight), 0.0)
    inv_right = from_right(inv)
    east, north = lower + upper_below, upper + lower_left
    coef[0] = inv * (1.0 / 3.0)
    coef[1] = inv * north
    coef[2] = inv * from_below(north)
    coef[3] = from_left(inv * east)
    coef[4] = from_left(inv * both)
    coef[5] = inv_right * east
    coef[6] = inv_right * from_below(both)
    vol_low, vol_up = field[2], field[3]
    mass[...] = (
        vol_low
        + vol_up
        + from_left(vol_low)
        + from_below(vol_up)
        + from_below(from_left(vol_low + vol_up))
    ) * (1.0 / 3.0)


def neighbours():
    n_old, n_new = lax.axis_size("old"), lax.axis_size("new")
    old, new = lax.axis_index("old"), lax.axis_index("new")
    left, right = lax.rem(old + n_old - 1, n_old), lax.rem(old + 1, n_old)
    below, above = lax.rem(new + n_new - 1, n_new), lax.rem(new + 1, n_new)
    return [
        (old, above),
        (old, below),
        (right, new),
        (left, new),
        (right, above),
        (left, above),
        (right, below),
        (left, below),
    ]


def to_neighbours(sources, targets, send_sem, recv_sem):
    around = neighbours()
    return [
        pltpu.make_async_remote_copy(
            src_ref=source,
            dst_ref=target,
            send_sem=send_sem.at[at],
            recv_sem=recv_sem.at[at],
            device_id=device,
            device_id_type=MESH,
        )
        for at, (source, target, device) in enumerate(zip(sources, targets, around + around))
    ]


def send_kernel(
    rows_dev,
    cols_dev,
    counts,
    rows_in,
    targets_in,
    weights_in,
    values_in,
    area,
    thick,
    shift_in,
    arrived,
    arrived_ids,
    field_out,
    coef_out,
    mass_out,
    acc,
    s_dn,
    s_up,
    s_l,
    s_r,
    s_dl,
    s_dr,
    s_ul,
    s_ur,
    field,
    coef,
    mass,
    table,
    picked,
    ids,
    notes,
    weights_flat,
    targets,
    weights_raw,
    values,
    rim_low,
    rim_high,
    rim_left,
    rim_right,
    pack_up,
    pack_down,
    pack_right,
    pack_left,
    rows,
    weights,
    local_sem,
    pair_sem,
    near_send,
    near_recv,
):
    n_old, n_new = lax.axis_size("old"), lax.axis_size("new")
    old, new = lax.axis_index("old"), lax.axis_index("new")
    ranks, payload, _ = picked.shape
    slots = payload * 4
    total = values.shape[1]
    me = old * n_new + new
    top, low = pl.ds(rows_dev - 8, 8), pl.ds(0, 8)
    near, far = pl.ds(0, LANE), pl.ds(cols_dev - LANE, LANE)

    loads = [
        (targets_in, targets),
        (weights_in, weights_raw),
        (values_in, values),
        (rows_in, rows),
    ]
    for source, at, count in ((area, 0, 2), (thick, 2, 2), (shift_in, 4, 3)):
        into = pl.ds(at, count)
        loads.append((source.at[:, top, :], rim_high.at[into]))
        loads.append((source.at[:, low, :], rim_low.at[into]))
        loads.append((source.at[:, :, far], rim_right.at[into]))
        loads.append((source.at[:, :, near], rim_left.at[into]))
        inner = field.at[into, pl.ds(8, rows_dev), pl.ds(0, cols_dev)]
        loads.append((source, inner))
    loads = [
        pltpu.make_async_copy(source, target, local_sem.at[at])
        for at, (source, target) in enumerate(loads)
    ]
    tall = rows_dev + 16
    field[:, 0:8, :] = jnp.zeros((7, 8, cols_dev + LANE), jnp.float32)
    field[:, 8 + rows_dev : tall, :] = jnp.zeros((7, 8, cols_dev + LANE), jnp.float32)
    for load in loads:
        load.start()

    barrier = pltpu.get_barrier_semaphore()

    def greet(step, _):
        other = lax.rem(me + step, ranks)
        pl.semaphore_signal(
            barrier, inc=1, device_id=(other // n_new, other % n_new), device_id_type=MESH
        )
        return 0

    lax.fori_loop(1, ranks, greet, 0)

    slot = lane_ids((ranks, slots))
    owner = lax.broadcasted_iota(jnp.int32, (ranks, slots), 0)
    count = jnp.broadcast_to(counts[...].astype(jnp.float32), (ranks, ranks)).T.astype(jnp.int32)
    loads[0].wait()
    loads[1].wait()
    target = targets[0]
    cell, col = target // cols_dev, target % cols_dev
    outside = ((owner % n_new == n_new - 1) & (cell % rows_dev == rows_dev - 1)) | (
        (owner // n_new == n_old - 1) & (col == cols_dev - 1)
    )
    used = (slot < count) & jnp.logical_not(outside)
    weights_flat[...] = jnp.where(used, weights_raw[0], 0.0)
    load_weights = pltpu.make_async_copy(weights_flat, weights, local_sem.at[len(loads)])
    load_weights.start()
    spare = slot // 4 % FRONT
    where_to = jnp.where(used, FRONT + target, spare)
    clash = jnp.zeros((ranks, slots), jnp.int32)
    for gap in range(1, BATCH):
        same = (where_to == pltpu.roll(where_to, 4 * gap, 1)) & (slot % (4 * BATCH) >= 4 * gap)
        clash = clash | same.astype(jnp.int32)
    found = jnp.broadcast_to(jnp.max(clash, axis=1, keepdims=True), (ranks, slots))
    notes[:, 0:slots] = jnp.where(clash > 0, spare, where_to)
    notes[:, slots : 2 * slots] = jnp.where(slot == 0, found, clash * where_to)

    unroll = 8
    loads[2].wait()

    def flip(step, _):
        for at in range(unroll):
            start = pl.multiple_of((step * unroll + at) * LANE, LANE)
            part = values[:, pl.ds(start, LANE)]
            table[pl.ds(start, LANE), :] = jnp.concatenate([part] * 4, axis=0).T
        return 0

    lax.fori_loop(0, total // (LANE * unroll), flip, 0)

    for load in loads[3:]:
        load.wait()
    pack_up[...] = jnp.zeros_like(pack_up)
    pack_down[...] = jnp.zeros_like(pack_down)
    lane = lane_ids((rows_dev, LANE))
    to_right = jnp.zeros((rows_dev, LANE), jnp.float32)
    to_left = jnp.zeros((rows_dev, LANE), jnp.float32)
    for f in range(7):
        if f < 2:
            pack_up[5 * f : 5 * f + 5, :] = rim_high[f, 3:8, :]
            pack_down[4 * f : 4 * f + 4, :] = rim_low[f, 0:4, :]
        else:
            pack_up[8 + f : 9 + f, :] = rim_high[f, 7:8, :]
            if f >= 4:
                pack_down[4 + f : 5 + f, :] = rim_low[f, 0:1, :]
        mine = lane // 8 == f
        to_right = jnp.where(mine, pltpu.roll(rim_right[f], 8 * f + 5, 1), to_right)
        to_left = jnp.where(mine, pltpu.roll(rim_left[f], 8 * f, 1), to_left)
    pack_right[...] = to_right
    pack_left[...] = to_left
    load_weights.wait()
    pl.semaphore_wait(barrier, ranks - 1)

    halo = to_neighbours(
        [
            pack_up,
            pack_down,
            pack_right,
            pack_left,
            pack_right.at[top],
            pack_left.at[top],
            pack_right.at[low],
            pack_left.at[low],
        ],
        [s_dn, s_up, s_l, s_r, s_dl, s_dr, s_ul, s_ur],
        near_send,
        near_recv,
    )
    for copy in halo:
        copy.start()

    lane = lane_ids((1, LANE))
    first, second, third = lane < 32, lane < 64, lane < 96

    def fill(owner):
        for row in range(payload):
            part = [
                table[pl.ds(rows[0, owner, row * 4 + g], 1), :] * weights[owner, row * 4 + g]
                for g in range(4)
            ]
            merged = jnp.where(
                first, part[0], jnp.where(second, part[1], jnp.where(third, part[2], part[3]))
            )
            picked[owner, pl.ds(row, 1), :] = merged
        ids[owner] = notes[pl.ds(owner, 1), :]

    chunk = (acc.shape[0] - 2 * FRONT) // ranks

    def clear(step):
        start = pl.multiple_of(FRONT + step * chunk, 8)
        acc[pl.ds(start, chunk), :] = jnp.zeros((chunk, LANE), jnp.float32)

    for end in (0, acc.shape[0] - FRONT):
        acc[pl.ds(end, FRONT), :] = jnp.zeros((FRONT, LANE), jnp.float32)
    clear(0)

    def one_owner(step, _):
        shift = lax.rem(step * STRIDE, ranks)
        to_old = lax.rem(old + shift // n_new, n_old)
        to_new = lax.rem(new + shift % n_new, n_new)
        owner = to_old * n_new + to_new
        fill(owner)
        clear(step)
        for at, (source, target) in enumerate(((picked, arrived), (ids, arrived_ids))):
            pltpu.make_async_remote_copy(
                src_ref=source.at[owner],
                dst_ref=target.at[me],
                send_sem=pair_sem.at[2 * at],
                recv_sem=pair_sem.at[2 * at + 1],
                device_id=(to_old, to_new),
                device_id_type=MESH,
            ).start()
        return 0

    lax.fori_loop(1, ranks, one_owner, 0)
    fill(me)
    for at, (source, target) in enumerate(((picked, arrived), (ids, arrived_ids))):
        pltpu.make_async_copy(source.at[me], target.at[me], pair_sem.at[2 * at + 1]).start()
    for copy in halo:
        copy.wait()
    around = (s_dn, s_up, s_l, s_r, s_dl, s_dr, s_ul, s_ur)
    cell_planes(n_new * rows_dev, n_old * cols_dev, field, coef, mass, around)
    saves = [
        pltpu.make_async_copy(source, target, near_send.at[at])
        for at, (source, target) in enumerate(
            ((field.at[pl.ds(2, 5)], field_out), (coef, coef_out), (mass, mass_out))
        )
    ]
    for save in saves:
        save.start()
    for save in saves:
        save.wait()
    for at, (source, target) in enumerate(((picked, arrived), (ids, arrived_ids))):
        rest = pl.ds(0, ranks - 1)
        pltpu.make_async_copy(source.at[rest], source.at[rest], pair_sem.at[2 * at]).wait()
        pltpu.make_async_copy(source, target, pair_sem.at[2 * at + 1]).wait()


def send(counts, rows, targets, weights, values, area, thick, shift):
    ranks, slots = rows.shape[1:]
    payload = slots // 4
    rows_dev, cols_dev = area.shape[1:]
    halo = [(16, cols_dev)] * 2 + [(rows_dev, LANE)] * 2 + [(8, LANE)] * 4
    tall, width = rows_dev + 16, cols_dev + LANE
    shapes = [(ranks, payload, LANE), (5, tall, width), (7, tall, width), (tall, width)]
    shapes = [jax.ShapeDtypeStruct(shape, jnp.float32) for shape in shapes]
    shapes.insert(1, jax.ShapeDtypeStruct((ranks, 1, 2 * slots), jnp.int32))
    shapes.append(pltpu.VMEM((2 * FRONT + 2 * rows_dev * cols_dev, LANE), jnp.float32))

    def scratch(*shape):
        return pltpu.VMEM(shape, jnp.float32)

    result = pl.pallas_call(
        functools.partial(send_kernel, rows_dev, cols_dev),
        out_shape=tuple(shapes),
        in_specs=[VMEM] + [HBM] * 7,
        out_specs=(HBM,) * (len(shapes) - 1) + (VMEM,),
        scratch_shapes=[scratch(*shape) for shape in halo]
        + [
            scratch(7, tall, width),
            scratch(7, tall, width),
            scratch(tall, width),
            scratch(values.shape[1], LANE),
            scratch(ranks, payload, LANE),
            pltpu.VMEM((ranks, 1, 2 * slots), jnp.int32),
            pltpu.VMEM((ranks, 2 * slots), jnp.int32),
            scratch(ranks, slots),
            pltpu.VMEM(targets.shape, jnp.int32),
            scratch(*weights.shape),
            scratch(*values.shape),
            scratch(7, 8, cols_dev),
            scratch(7, 8, cols_dev),
            scratch(7, rows_dev, LANE),
            scratch(7, rows_dev, LANE),
            scratch(16, cols_dev),
            scratch(16, cols_dev),
            scratch(rows_dev, LANE),
            scratch(rows_dev, LANE),
            pltpu.SMEM(rows.shape, jnp.int32),
            pltpu.SMEM((ranks, slots), jnp.float32),
            pltpu.SemaphoreType.DMA((20,)),
            pltpu.SemaphoreType.DMA((4,)),
            pltpu.SemaphoreType.DMA((8,)),
            pltpu.SemaphoreType.DMA((8,)),
        ],
        compiler_params=pltpu.CompilerParams(
            vmem_limit_bytes=24 * MIB, collective_id=1, has_side_effects=True
        ),
        name="send",
    )(counts, rows, targets, weights, values, area, thick, shift)
    return result[0], result[1], result[2:-1], result[-1]


def fold(total):
    flipped = total.T
    return (flipped[0:32] + flipped[32:64]) + (flipped[64:96] + flipped[96:128])


def node_parts(acc, rows_dev, cols_dev, i, first, size, cells, below):
    upper = rows_dev * cols_dev
    base = i * cols_dev + (FRONT + first)
    here, left = [], []
    if cells:
        here += [base, base + upper]
        left += [base - 1]
    if below:
        here += [base + upper - cols_dev]
        left += [base - cols_dev - 1, base + upper - cols_dev - 1]
    here, left = ([acc[pl.ds(at, size), :] for at in some] for some in (here, left))
    return functools.reduce(jnp.add, here), functools.reduce(jnp.add, left)


def node_tile(acc, rows_dev, cols_dev, i, tile, cells=True, below=True):
    here, left = node_parts(acc, rows_dev, cols_dev, i, tile * LANE, LANE, cells, below)
    if tile == 0:
        rows = lax.broadcasted_iota(jnp.int32, (LANE, LANE), 0)
        left = jnp.where(rows == 0, 0.0, left)
    return fold(here + left)


def scatter_kernel(
    rows_dev,
    cols_dev,
    ids_in,
    data_in,
    _,
    rim_high,
    rim_low,
    cols_right,
    cols_left,
    acc,
    flat_right,
    flat_left,
    data,
    ids,
    ids_sem,
    data_sem,
):
    ranks, payload, _ = data.shape
    slots = payload * 4
    quarter = ranks // 4
    loads = []
    for at in range(4):
        some = pl.ds(at * quarter, quarter)
        for source, target, sem in ((ids_in, ids, ids_sem), (data_in, data, data_sem)):
            loads.append(pltpu.make_async_copy(source.at[some], target.at[some], sem.at[at]))
    for load in loads:
        load.start()
    flat_right[...] = jnp.zeros_like(flat_right)
    flat_left[...] = jnp.zeros_like(flat_left)

    lane = lane_ids((1, LANE))
    masks = [lane // 32 == g for g in range(4)]

    def add_rows(source, first):
        where_to = [ids[source, 0, first * 4 + k] for k in range(4 * BATCH)]
        new = [data[source, pl.ds(first + r, 1), :] for r in range(BATCH)]
        old = [acc[pl.ds(row, 1), :] for row in where_to]
        for k, (row, have) in enumerate(zip(where_to, old)):
            pltpu.store(acc.at[pl.ds(row, 1), :], have + new[k // 4], mask=masks[k % 4])

    def one_source(source, _):
        for first in range(0, payload, BATCH):
            add_rows(source, first)
        return 0

    for at in range(4):
        loads[2 * at].wait()
        loads[2 * at + 1].wait()
        lax.fori_loop(at * quarter, (at + 1) * quarter, one_source, 0)

    def late(source, _):
        def one_slot(k, _):
            row = ids[source, 0, slots + k]

            @pl.when(row > 0)
            def _():
                new = data[source, pl.ds(k // 4, 1), :]
                acc[pl.ds(row, 1), :] += jnp.where(lane // 32 == k % 4, new, 0.0)

            return 0

        def eight_slots(some, _):
            noted = sum(ids[source, 0, slots + some * 8 + k] for k in range(8))

            @pl.when(noted > 0)
            def _():
                lax.fori_loop(jnp.maximum(some * 8, 1), some * 8 + 8, one_slot, 0)

            return 0

        @pl.when(ids[source, 0, slots] > 0)
        def _():
            lax.fori_loop(0, slots // 8, eight_slots, 0)

        return 0

    def late_group(group, _):
        found = sum(ids[group * 8 + k, 0, slots] for k in range(8))

        @pl.when(found > 0)
        def _():
            lax.fori_loop(group * 8, group * 8 + 8, late, 0)

        return 0

    lax.fori_loop(0, ranks // 8, late_group, 0)

    tiles = cols_dev // LANE
    for at in range(HALO):
        for tile in range(tiles):
            span = slice(tile * LANE, (tile + 1) * LANE)
            rim_low[at, :, span] = node_tile(acc, rows_dev, cols_dev, at, tile, True, at > 0)
    for at in range(HALO + 1):
        i = rows_dev - HALO + at
        for tile in range(tiles):
            span = slice(tile * LANE, (tile + 1) * LANE)
            rim_high[at, :, span] = node_tile(acc, rows_dev, cols_dev, i, tile, i < rows_dev)

    row8 = lax.broadcasted_iota(jnp.int32, (8, LANE), 0)

    def rim_columns(i, cells, below):
        into = pl.ds(pl.multiple_of(i * 8, 8), 8)
        here, left = node_parts(acc, rows_dev, cols_dev, i, cols_dev - HALO, 8, cells, below)
        flat_right[into, :] = jnp.where(row8 < HALO, here, 0.0) + jnp.where(
            row8 < HALO + 1, left, 0.0
        )
        here, left = node_parts(acc, rows_dev, cols_dev, i, 0, 8, cells, below)
        flat_left[into, :] = jnp.where(
            row8 < HALO, here + jnp.where(row8 > 0, left, 0.0), 0.0
        )

    def inner_columns(i, _):
        rim_columns(i, True, True)
        return 0

    rim_columns(jnp.int32(0), True, False)
    lax.fori_loop(1, rows_dev, inner_columns, 0)
    rim_columns(jnp.int32(rows_dev), False, True)
    for tile in range(cols_right.shape[0]):
        span = slice(tile * LANE, (tile + 1) * LANE)
        cols_right[tile] = fold(flat_right[span, :])
        cols_left[tile] = fold(flat_left[span, :])


def scatter(ids, data, acc, rows_dev, cols_dev):
    channels = LANE // 4
    tiles = rows_dev // 16 + 1
    shapes = [(HALO + 1, channels, cols_dev), (HALO, channels, cols_dev)]
    shapes += [(tiles, channels, LANE)] * 2
    return pl.pallas_call(
        functools.partial(scatter_kernel, rows_dev, cols_dev),
        out_shape=tuple(jax.ShapeDtypeStruct(shape, jnp.float32) for shape in shapes)
        + (pltpu.VMEM(acc.shape, jnp.float32),),
        in_specs=[HBM, HBM, VMEM],
        out_specs=(VMEM,) * 5,
        input_output_aliases={2: 4},
        scratch_shapes=[
            pltpu.VMEM((tiles * LANE, LANE), jnp.float32),
            pltpu.VMEM((tiles * LANE, LANE), jnp.float32),
            pltpu.VMEM(data.shape, jnp.float32),
            pltpu.SMEM(ids.shape, jnp.int32),
            pltpu.SemaphoreType.DMA((4,)),
            pltpu.SemaphoreType.DMA((4,)),
        ],
        compiler_params=pltpu.CompilerParams(vmem_limit_bytes=24 * MIB),
        name="scatter",
    )(ids, data, acc)


def first_piola(stretch_x, stretch_y, fields):
    gram_xx = sum(x * x for x in stretch_x)
    gram_xy = sum(x * y for x, y in zip(stretch_x, stretch_y))
    gram_yy = sum(y * y for y in stretch_y)
    determinant = gram_xx * gram_yy - gram_xy * gram_xy
    inverse = 1.0 / determinant
    inv_xx = gram_yy * inverse
    inv_xy = -gram_xy * inverse
    inv_yy = gram_xx * inverse
    shear_mod = MU_BASE * (1.5 + jnp.tanh(fields[3]))
    bulk = LAMBDA_BULK * 0.5 * jnp.log(determinant)
    piola_x, piola_y = [], []
    for along_x, along_y in zip(stretch_x, stretch_y):
        push_x = along_x * inv_xx + along_y * inv_xy
        push_y = along_x * inv_xy + along_y * inv_yy
        piola_x.append(
            shear_mod * (along_x - push_x)
            + bulk * push_x
            + PRESTRESS * (along_x * fields[0] + along_y * fields[2])
        )
        piola_y.append(
            shear_mod * (along_y - push_y)
            + bulk * push_y
            + PRESTRESS * (along_x * fields[2] + along_y * fields[1])
        )
    return piola_x, piola_y


def sheet_kernel(*refs):
    acc, rim_high, rim_low, cols_right, cols_left, field_in, coef_in, mass_in = refs[:8]
    total, speed = refs[8:10]
    p_halo, refs = refs[10:20], refs[20:]
    resid, first_sum, field, mem, mass, coef, p_own = refs[:7]
    load_sem, send_sem, recv_sem, far_send, far_recv = refs[7:]
    p_dn, p_up, p_l, p_r, p_dl, p_dr, p_ul, p_ur, p_d, p_u = p_halo
    channels, width = resid.shape[1:]
    tall = mass.shape[0]
    rows_dev, cols_dev = tall - 16, width - LANE
    main = pl.ds(0, cols_dev)
    from_left, from_right, from_below, from_above = shifters(tall, width)

    barrier = pltpu.get_barrier_semaphore()
    for device in neighbours():
        pl.semaphore_signal(barrier, inc=1, device_id=device, device_id_type=MESH)

    loads = [
        (field_in, field),
        (coef_in, coef),
        (mass_in, mass),
        (cols_right, p_own),
        (rim_low, resid.at[pl.ds(HALO, HALO), :, main]),
        (rim_high, resid.at[pl.ds(rows_dev, HALO + 1), :, main]),
    ]
    loads = [
        pltpu.make_async_copy(source, target, load_sem.at[at])
        for at, (source, target) in enumerate(loads)
    ]
    for load in loads:
        load.start()

    tiles_high, tiles_low = pl.ds((rows_dev - 1) // 16, 2), pl.ds(0, 1)
    pl.semaphore_wait(barrier, 8)
    copies = to_neighbours(
        [
            rim_high.at[pl.ds(1, HALO)],
            rim_low.at[pl.ds(0, HALO - 1)],
            cols_right,
            cols_left,
            cols_right.at[tiles_high],
            cols_left.at[tiles_high],
            cols_right.at[tiles_low],
            cols_left.at[tiles_low],
            cols_right.at[tiles_high],
            cols_right.at[tiles_low],
        ],
        [p_dn.at[pl.ds(1, HALO)], p_up.at[pl.ds(0, HALO - 1)]] + list(p_halo[2:]),
        send_sem,
        recv_sem,
    )
    far_copies = to_neighbours(
        [rim_high.at[pl.ds(0, 1)], rim_low.at[pl.ds(HALO - 1, 1)]],
        [p_dn.at[pl.ds(0, 1)], p_up.at[pl.ds(HALO - 1, 1)]],
        far_send,
        far_recv,
    )
    for copy in copies[2:] + copies[:2]:
        copy.start()

    def inner_fold(i):
        for tile in range(cols_dev // LANE):
            span = slice(tile * LANE, (tile + 1) * LANE)
            resid[i + HALO, :, span] = node_tile(acc, rows_dev, cols_dev, i, tile)

    rows_loop(HALO, rows_dev - HALO, inner_fold, 2)

    for load in loads:
        load.wait()
    mem[...] = jnp.zeros_like(mem)

    centre = 0.5 * (EIG_HIGH + EIG_LOW)
    half_width = 0.5 * (EIG_HIGH - EIG_LOW)
    ratio_eig = centre / half_width
    edge = lane_ids((channels, LANE))

    def widen(inner, ends, left, right, place):
        ends = pltpu.roll(ends, lax.rem(2 * LANE - 4 - 8 * place, LANE), 1)
        left = pltpu.roll(left, lax.rem(2 * LANE - 4 - 8 * place, LANE), 1)
        right = pltpu.roll(right, lax.rem(LANE - 8 * place, LANE), 1)
        first = inner[:, 0:LANE] + jnp.where(edge == 0, left, 0.0)
        last = jnp.where(
            edge >= LANE - HALO,
            left,
            jnp.where(edge < HALO, right + jnp.where(edge == 0, ends, 0.0), 0.0),
        )
        return jnp.concatenate([first, inner[:, LANE:], last], axis=1)

    def begin(e, rhs):
        scaled = rhs * coef[0, pl.ds(e + 4, 1), :]
        resid[e] = scaled
        first_sum[e] = scaled * (1.0 / centre)

    def own(i):
        i = jnp.int32(i)
        tile = i // 16
        return widen(resid[i + HALO, :, 0:cols_dev], p_own[tile], p_l[tile], p_r[tile], i % 16)

    def under(k):
        i = rows_dev - HALO + k
        tile = i // 16 - (rows_dev - 1) // 16
        return widen(p_dn[k], p_d[tile], p_dl[tile], p_dr[tile], jnp.int32(i % 16))

    def over(k):
        return widen(p_up[k], p_u[0], p_ul[0], p_ur[0], jnp.int32(k))

    rhos = [1.0 / ratio_eig]
    for _ in range(ITERS):
        rhos.append(1.0 / (2.0 * ratio_eig - rhos[-1]))
    iterates = [first_sum, total]
    lane8 = lane_ids((8, LANE))
    first_lane, last_lane = lane8 == 0, lane8 == LANE - 1

    def sweep_row(sweep, e):
        keep = rhos[sweep + 1] * rhos[sweep]
        gain = 2.0 * rhos[sweep + 1] / half_width
        final = sweep == ITERS - 1
        source, other = iterates[sweep % 2], iterates[(sweep + 1) % 2]
        k_row = [coef[c, pl.ds(e + 4, 1), :] for c in range(1, 7)]
        tiles, groups = width // LANE, range(channels // 8)
        rest = [[None] * tiles for _ in groups]
        west = [[None] * tiles for _ in groups]
        east = [[None] * tiles for _ in groups]
        sums = [None] * tiles

        def close(t):
            span = slice(t * LANE, (t + 1) * LANE)
            for g in groups:
                from_east = jnp.where(last_lane, east[g][(t + 1) % tiles], east[g][t])
                from_west = jnp.where(first_lane, west[g][t - 1], west[g][t])
                new = rest[g][t] - gain * (from_east + from_west)
                other[e, 8 * g : 8 * g + 8, span] = new
                if final:
                    sums[t] = new if g == 0 else sums[t] + new

        for t in range(tiles):
            span = slice(t * LANE, (t + 1) * LANE)
            k = [jnp.broadcast_to(x[:, span], (8, LANE)) for x in k_row]
            for g in groups:
                at = slice(8 * g, 8 * g + 8)
                here, up, down = source[e, at, span], source[e + 1, at, span], source[e - 1, at, span]
                east[g][t] = pltpu.roll(k[2] * here + k[3] * up, LANE - 1, 1)
                west[g][t] = pltpu.roll(k[4] * here + k[5] * down, 1, 1)
                kept = (1.0 + keep - gain) * here
                kept = kept + gain * (resid[e, at, span] - (k[0] * up + k[1] * down))
                rest[g][t] = kept if sweep == 0 else kept - keep * other[e, at, span]
            if t > 1:
                close(t - 1)
        close(tiles - 1)
        close(0)
        if final:
            through = jnp.concatenate(sums, axis=1) * (1.0 / POINTS)
            for at, value in enumerate((0, 1, 5, 7)):
                mem[at, pl.ds(e + 4, 1), :] = through[value : value + 1, :]

    for copy in copies[2:]:
        copy.wait()

    rows_loop(1, rows_dev, lambda i: begin(i + HALO, own(i)))
    for sweep in range(ITERS):
        rows_loop(
            HALO + 2 + sweep, rows_dev + HALO - 1 - sweep, functools.partial(sweep_row, sweep)
        )
        if sweep == 0:
            for copy in far_copies:
                copy.start()

    for copy in copies[:2]:
        copy.wait()
    for e in range(1, HALO):
        begin(e, under(e))
    begin(HALO, own(0) + under(HALO))
    begin(rows_dev + HALO, own(rows_dev) + over(0))
    for e in range(1, HALO - 1):
        begin(rows_dev + HALO + e, over(e))
    for sweep in range(ITERS):

        def outer_row(k, sweep=sweep):
            sweep_row(
                sweep, jnp.where(k < HALO, 2 + sweep + k, rows_dev - 1 - sweep + k)
            )

        rows_loop(0, 2 * HALO - 1, outer_row)

    for copy in far_copies:
        copy.wait()
    begin(0, under(0))
    begin(rows_dev + 2 * HALO - 1, over(HALO - 1))
    for sweep in range(ITERS):
        sweep_row(sweep, 1 + sweep)
        sweep_row(sweep, rows_dev + 2 * HALO - 2 - sweep)

    anchor = [field[2 + c] for c in range(3)]
    beside = [from_right(x) for x in anchor]
    upward = [from_above(x) for x in anchor]
    across = [from_above(x) for x in beside]
    m_anchor = [mem[c] for c in range(4)]
    m_beside = [from_right(x) for x in m_anchor]
    m_upward = [from_above(x) for x in m_anchor]
    m_across = [from_above(x) for x in m_beside]
    third = 1.0 / 3.0
    m_low = [(a + b + x) * third for a, b, x in zip(m_anchor, m_beside, m_across)]
    m_up = [(a + x + u) * third for a, x, u in zip(m_anchor, m_across, m_upward)]
    low_x = [b - a for a, b in zip(anchor, beside)]
    low_y = [x - b for b, x in zip(beside, across)]
    up_x = [x - u for u, x in zip(upward, across)]
    up_y = [u - a for a, u in zip(anchor, upward)]
    low_x[0], up_x[0] = 1.0 + low_x[0], 1.0 + up_x[0]
    low_y[1], up_y[1] = 1.0 + low_y[1], 1.0 + up_y[1]
    piola_lx, piola_ly = first_piola(low_x, low_y, m_low)
    piola_ux, piola_uy = first_piola(up_x, up_y, m_up)
    vol_low, vol_up = field[0], field[1]
    node_mass = mass[8 : 8 + rows_dev, 0:cols_dev]
    for c in range(3):
        f_beside = -vol_low * (piola_lx[c] - piola_ly[c])
        f_across_low = -vol_low * piola_ly[c]
        f_across_up = -vol_up * piola_ux[c]
        f_upward = -vol_up * (piola_uy[c] - piola_ux[c])
        f_anchor = -(f_beside + f_across_low) - (f_across_up + f_upward)
        force = (
            f_anchor
            + from_left(f_beside)
            + from_below(f_upward)
            + from_below(from_left(f_across_low + f_across_up))
        )
        speed_up = force[8 : 8 + rows_dev, 0:cols_dev] / node_mass
        speed[c] = speed_up + GRAVITY if c == 2 else speed_up


def sheet(acc, rims, planes):
    tall, width = planes[2].shape
    rows_dev, cols_dev = tall - 16, width - LANE
    long = rows_dev + 2 * HALO
    tiles, channels, _ = rims[2].shape

    def scratch(*shape):
        return pltpu.VMEM(shape, jnp.float32)

    block = scratch(long, channels, width)
    part_halo = [rims[0].shape, rims[1].shape, rims[2].shape, rims[3].shape]
    part_halo += [(2, channels, LANE)] * 2 + [(1, channels, LANE)] * 2
    part_halo += [(2, channels, LANE), (1, channels, LANE)]
    return pl.pallas_call(
        sheet_kernel,
        out_shape=(
            block,
            scratch(3, rows_dev, cols_dev),
        ),
        in_specs=[VMEM] + [HBM] * 7,
        out_specs=(VMEM, VMEM),
        scratch_shapes=[scratch(*shape) for shape in part_halo]
        + [
            block,
            block,
            scratch(5, tall, width),
            scratch(4, tall, width),
            scratch(tall, width),
            scratch(7, tall, width),
            scratch(tiles, channels, LANE),
            pltpu.SemaphoreType.DMA((6,)),
            pltpu.SemaphoreType.DMA((10,)),
            pltpu.SemaphoreType.DMA((10,)),
            pltpu.SemaphoreType.DMA((2,)),
            pltpu.SemaphoreType.DMA((2,)),
        ],
        compiler_params=pltpu.CompilerParams(
            vmem_limit_bytes=24 * MIB, collective_id=2, has_side_effects=True
        ),
        name="sheet",
    )(acc, *rims, *planes)


def finish_kernel(total, speed_up, velocity, out, vel_out):
    channels, rows, cols = out.shape
    here = pl.ds(HALO + pl.program_id(0) * rows, rows)
    for channel in range(channels):
        out[channel] = total[here, channel, 0:cols]
    vel_out[...] = velocity[...] + TIME_STEP * speed_up[...]


def finish(total, speed_up, velocity):
    channels = total.shape[1]
    rows_dev, cols_dev = velocity.shape[1:]

    def plane(count):
        return pl.BlockSpec((count, 8, cols_dev), lambda i: (0, i, 0))

    return pl.pallas_call(
        finish_kernel,
        grid=(rows_dev // 8,),
        out_shape=(
            jax.ShapeDtypeStruct((channels, rows_dev, cols_dev), jnp.float32),
            jax.ShapeDtypeStruct(velocity.shape, jnp.float32),
        ),
        in_specs=[VMEM, plane(3), plane(3)],
        out_specs=(plane(channels), plane(3)),
        compiler_params=pltpu.CompilerParams(vmem_limit_bytes=40 * MIB),
        name="finish",
    )(total, speed_up, velocity)


def local(
    old_values,
    pair_rows,
    pair_targets,
    pair_weights,
    pair_counts,
    cell_area,
    thickness,
    displacement,
    velocity,
):
    rows_dev, cols_dev = cell_area.shape[1:]
    arrived, ids, planes, acc = send(
        pair_counts,
        pair_rows,
        pair_targets,
        pair_weights,
        old_values,
        cell_area,
        thickness,
        displacement,
    )
    *rims, acc = scatter(ids, arrived, acc, rows_dev, cols_dev)
    acc = pltpu.with_memory_space_constraint(acc, pltpu.VMEM)
    total, speed_up = sheet(acc, rims, planes)
    return finish(total, speed_up, velocity)


def solution(mesh):
    return jax.shard_map(
        local,
        mesh=mesh,
        in_specs=(
            P(None, ("old", "new")),
            P(("old", "new"), None, None),
            P(("old", "new"), None, None),
            P(("old", "new"), None, None),
            P(("old", "new"), None),
            P(None, "new", "old"),
            P(None, "new", "old"),
            P(None, "new", "old"),
            P(None, "new", "old"),
        ),
        out_specs=(P(None, "new", "old"), P(None, "new", "old")),
        check_vma=False,
    )
```
